32 devices in a mesh: rep: 16 (over z, y, x), shard: 2 (over core).
Axes of the slice: x: 2, y: 2, z: 4, core: 2. Of those that a mesh axis runs over, the one named last changes fastest.
Arguments:
- tokens: bfloat16 [32768, 768], P(('rep', 'shard')), may hold values from -6 to 6
- encoder_states: bfloat16 [65536, 768], P(('rep', 'shard')), may hold values from -6 to 6
- cotangent: bfloat16 [32768, 768], P(('rep', 'shard')), may hold values from -6 to 6
- block_mask: int32 [32, 4, 4], P(('rep', 'shard')), may hold values from 0 to 1, as said below
- wide_master: float32 [768, 9216], P('shard')
- narrow_master: float32 [3072, 768], P('shard'), may hold values from -0.15625 to 0.15625
- vec_master: float32 [768, 17], P('shard')
- wide_first: float32 [768, 9216], P('shard'), may hold values from -1.75 to 1.75
- narrow_first: float32 [3072, 768], P('shard'), may hold values from -1.75 to 1.75
- vec_first: float32 [768, 17], P('shard'), may hold values from -1.75 to 1.75
- wide_second: float32 [768, 9216], P('shard'), may hold values from 0.01 to 1
- narrow_second: float32 [3072, 768], P('shard'), may hold values from 0.01 to 1
- vec_second: float32 [768, 17], P('shard'), may hold values from 0.01 to 1
Outputs:
- out: bfloat16 [32768, 768], P(('rep', 'shard'))
- in_grad: bfloat16 [32768, 768], P(('rep', 'shard'))
- enc_grad: bfloat16 [65536, 768], P(('rep', 'shard'))
- wide_grad: float32 [768, 9216], P('shard')
- narrow_grad: float32 [3072, 768], P('shard')
- vec_grad: float32 [768, 17], P('shard')
- wide_new: float32 [768, 9216], P('shard')
- narrow_new: float32 [3072, 768], P('shard')
- vec_new: float32 [768, 17], P('shard')
- wide_first_new: float32 [768, 9216], P('shard')
- narrow_first_new: float32 [3072, 768], P('shard')
- vec_first_new: float32 [768, 17], P('shard')
- wide_second_new: float32 [768, 9216], P('shard')
- narrow_second_new: float32 [3072, 768], P('shard')
- vec_second_new: float32 [768, 17], P('shard')
- wide_copy: bfloat16 [768, 9216], P('shard')
- narrow_copy: bfloat16 [3072, 768], P('shard')
- vec_copy: bfloat16 [768, 17], P('shard')
The draws below stay inside these ranges and needn't reach their ends.
Inputs may be any that keep to these rules, and one draw needn't show every extreme that they name: block_mask[s, a, b] is 1 where a == b and 0 where b > a; below the diagonal each entry is 0 or 1.
All inputs are finite; a program needn't handle non-finite values.
Results may differ from the reference program's by a relative error of at most 0.03.
The reference program's roundings to bfloat16 on the way count: a program that leaves them out, or rounds other values in their place, can miss the bound.
Values may be sent and summed in bfloat16 or wider, within the bound.
A program may use at most 512 MiB of HBM per device.

```python
import math
import jax
import jax.numpy as jnp
from jax import lax

D = 768
H = 12
HD = 64
FF = 3072
VECS = 17
LEN = 1024
ENC = 2048
BLK = 256
STEP = 4
SEQS = 32
TOKENS = 32768
ENC_ALL = 65536
WIDE = 9216
NB = 4


def draw_block_mask(key, part):
    coins = jax.random.randint(key, (SEQS, NB, NB), 0, 5)
    rows_at = jnp.arange(NB, dtype=jnp.int32)[:, None]
    cols_at = jnp.arange(NB, dtype=jnp.int32)[None, :]
    lower = (coins < 3).astype(jnp.int32)
    return jnp.where(rows_at == cols_at, 1, jnp.where(rows_at > cols_at, lower, 0)).astype(jnp.int32)


def draw_wide_master(key, part):
    base = jnp.clip(jax.random.normal(key, (D, WIDE), jnp.float32), -6.0, 6.0)
    column = jnp.arange(WIDE, dtype=jnp.int32)
    factor = jnp.where(column < 2 * D, 1.4, 1.0)
    factor = jnp.where((column >= 3 * D) & (column < 4 * D), 4.0, factor)
    factor = jnp.where((column >= 4 * D) & (column < 6 * D), 1.4, factor)
    factor = jnp.where((column >= 7 * D) & (column < 8 * D), 6.0, factor)
    return base * factor * D ** (-0.5)


def draw_vec_master(key, part):
    key_one = jax.random.fold_in(key, 1)
    key_two = jax.random.fold_in(key, 2)
    base = jnp.clip(jax.random.normal(key_one, (D, VECS), jnp.float32), -6.0, 6.0) * 0.3
    gain_draw = jax.random.uniform(key_two, (D, VECS), jnp.float32, 0.6, 1.4)
    column = jnp.arange(VECS, dtype=jnp.int32)
    return jnp.where((column >= 11) & (column < 14), gain_draw, base)


def block_scale(key, dims, cuts, low, high):
    loudness = 1.0
    for dim, parts in cuts:
        heights = jax.random.uniform(jax.random.fold_in(jax.random.fold_in(key, 6), dim), (parts,), jnp.float32, low / len(cuts), high / len(cuts))
        loudness = loudness * jnp.repeat(jnp.exp(heights), dims[dim] // parts).reshape((-1,) + (1,) * (len(dims) - 1 - dim))
    return loudness


def scatter_about(stream_key, dims, deviation, most, shards=(), kind=jnp.bfloat16):
    drawn = jax.random.normal(stream_key, dims, jnp.float32) * deviation
    if len(shards) > 0:
        drawn = block_scale(stream_key, dims, shards, -0.22, 0.18) * drawn
    return jnp.clip(drawn, min=-most, max=most).astype(kind)


def setup_inputs(seed: int = 0) -> dict:
    splits = jax.random.split(jax.random.key(seed), 14)
    return {
        "tokens": scatter_about(splits[0], (TOKENS, D), 1.0, 6.0, ((0, 32),)),
        "encoder_states": scatter_about(splits[1], (ENC_ALL, D), 1.0, 6.0, ((0, 32),)),
        "cotangent": scatter_about(splits[2], (TOKENS, D), 1.0, 6.0, ((0, 32),)),
        "block_mask": draw_block_mask(jax.random.fold_in(splits[13], 71), 0),
        "wide_master": draw_wide_master(jax.random.fold_in(splits[13], 71), 0),
        "narrow_master": scatter_about(splits[5], (FF, D), (FF // 2) ** -0.5, 0.15625, ((0, 2),), jnp.float32),
        "vec_master": draw_vec_master(jax.random.fold_in(splits[13], 71), 0),
        "wide_first": scatter_about(splits[7], (D, WIDE), 0.3, 1.75, ((0, 2),), jnp.float32),
        "narrow_first": scatter_about(splits[8], (FF, D), 0.3, 1.75, ((0, 2),), jnp.float32),
        "vec_first": scatter_about(splits[9], (D, VECS), 0.3, 1.75, ((0, 2),), jnp.float32),
        "wide_second": jnp.clip(jnp.exp(math.log(1.0) - 4.6051702 * jax.random.uniform(splits[10], (D, WIDE), jnp.float32) ** block_scale(splits[10], (D, WIDE), ((0, 2),), -0.2, 0.2)), 0.01, 1.0),
        "narrow_second": jnp.clip(jnp.exp(math.log(1.0) - 4.6051702 * jax.random.uniform(splits[11], (FF, D), jnp.float32) ** block_scale(splits[11], (FF, D), ((0, 2),), -0.2, 0.2)), 0.01, 1.0),
        "vec_second": jnp.clip(jnp.exp(math.log(1.0) - 4.6051702 * jax.random.uniform(splits[12], (D, VECS), jnp.float32) ** block_scale(splits[12], (D, VECS), ((0, 2),), -0.2, 0.2)), 0.01, 1.0),
    }


@jax.custom_vjp
def low(v):
    return lax.optimization_barrier(v.astype(jnp.bfloat16)).astype(jnp.float32)

@jax.custom_vjp
def low_back(v):
    return v

def low_keep(v):
    return (low(v), None)

def low_pass(kept, grad):
    return (grad,)

def back_keep(v):
    return (v, None)

def back_low(kept, grad):
    return (low(grad),)
low.defvjp(low_keep, low_pass)
low_back.defvjp(back_keep, back_low)
eps_norm = 1e-05
eps_adam = 1e-08
beta_one = 0.5
beta_two = 0.5
learn_rate = 0.03
vec_rate = 0.25
weight_decay = 0.1
masked_score = -1e+30
highest = lax.Precision.HIGHEST

def matmul(left, right):
    return jnp.dot(left, right, precision=highest, preferred_element_type=jnp.float32)

def rounded(value):
    return low_back(low(value))

def layer_norm(resid, gain, shift):
    average = lax.optimization_barrier(jnp.mean(resid, axis=-1, keepdims=True))
    centred = resid - average
    inverse = lax.rsqrt(lax.optimization_barrier(jnp.mean(centred * centred, axis=-1, keepdims=True)) + eps_norm)
    return centred * inverse * gain + shift

def allowed_pairs(block_table):
    expanded = jnp.repeat(jnp.repeat(block_table, BLK, axis=0), BLK, axis=1) > 0
    places = jnp.arange(LEN, dtype=jnp.int32)
    blocks = places // BLK
    causal = (blocks[:, None] > blocks[None, :]) | (places[:, None] >= places[None, :])
    return expanded & causal

def attend(queries, keys_in, values_in, allowed):
    rows_query = queries.shape[0]
    rows_key = keys_in.shape[0]
    head_q = queries.reshape(rows_query, H, HD)
    head_k = keys_in.reshape(rows_key, H, HD)
    head_v = values_in.reshape(rows_key, H, HD)
    scores = low_back(jnp.einsum('qhd,khd->hqk', head_q, head_k, precision=highest) * HD ** (-0.5))
    if allowed is not None:
        scores = jnp.where(allowed[None], scores, masked_score)
    row_max = lax.optimization_barrier(jnp.max(scores, axis=-1, keepdims=True))
    weights = jnp.exp(scores - row_max)
    probs_low = low(weights / lax.optimization_barrier(jnp.sum(weights, axis=-1, keepdims=True)))
    mixed = jnp.einsum('hqk,khd->qhd', probs_low, head_v, precision=highest)
    return mixed.reshape(rows_query, H * HD)

def layer(tokens_in, encoded, wide, narrow, vector, allowed):
    wide = low(wide)
    narrow = low(narrow)
    vector = low(vector)
    ffn_bias = vector[:, 6:10].T.reshape(FF)
    joint_proj = matmul(tokens_in, wide[:, :3 * D])
    queries = rounded(joint_proj[:, :D] + vector[:, 0])
    keys_self = rounded(joint_proj[:, D:2 * D])
    values_self = rounded(joint_proj[:, 2 * D:3 * D] + vector[:, 1])
    mixed_self = rounded(attend(queries, keys_self, values_self, allowed))
    branch_one = low_back(matmul(mixed_self, wide[:, 3 * D:4 * D]) + vector[:, 2])
    normed_one = layer_norm(tokens_in + branch_one, vector[:, 11], vector[:, 14])
    cross_queries = rounded(matmul(low(normed_one), wide[:, 4 * D:5 * D]) + vector[:, 3])
    enc_proj = matmul(encoded, wide[:, 5 * D:7 * D])
    cross_keys = rounded(enc_proj[:, :D])
    cross_values = rounded(enc_proj[:, D:] + vector[:, 4])
    mixed_cross = rounded(attend(cross_queries, cross_keys, cross_values, None))
    branch_two = low_back(matmul(mixed_cross, wide[:, 7 * D:8 * D]) + vector[:, 5])
    normed_two = layer_norm(normed_one + branch_two, vector[:, 12], vector[:, 15])
    hidden = low_back(matmul(low(normed_two), wide[:, 8 * D:]) + ffn_bias)
    active = low(jax.nn.gelu(hidden, approximate=False))
    branch_three = low_back(matmul(active, narrow) + vector[:, 10])
    return layer_norm(normed_two + branch_three, vector[:, 13], vector[:, 16])

def adam_update(master, first, second, gradient, decay_on, rate):
    first_new = beta_one * first + (1.0 - beta_one) * gradient
    second_new = beta_two * second + (1.0 - beta_two) * gradient * gradient
    first_hat = first_new / (1.0 - beta_one ** STEP)
    second_hat = second_new / (1.0 - beta_two ** STEP)
    master_new = master - rate * (first_hat / (jnp.sqrt(second_hat) + eps_adam) + decay_on * master)
    return (master_new, first_new, second_new)

def reference(tokens, encoder_states, cotangent, block_mask, wide_master, narrow_master, vec_master, wide_first, narrow_first, vec_first, wide_second, narrow_second, vec_second):
    seq_tokens = tokens.astype(jnp.float32).reshape(SEQS, LEN, D)
    seq_encoded = encoder_states.astype(jnp.float32).reshape(SEQS, ENC, D)
    seq_cotangent = cotangent.astype(jnp.float32).reshape(SEQS, LEN, D)

    def one_sequence(running, inputs):
        token_seq, encoded_seq, cotangent_seq, block_table = inputs
        allowed = allowed_pairs(block_table)

        def closed(token_arg, encoded_arg, wide_arg, narrow_arg, vector_arg):
            return layer(token_arg, encoded_arg, wide_arg, narrow_arg, vector_arg, allowed)
        result, pullback = jax.vjp(closed, token_seq, encoded_seq, wide_master, narrow_master, vec_master)
        gradients = pullback(cotangent_seq)
        running = (running[0] + gradients[2], running[1] + gradients[3], running[2] + gradients[4])
        return (running, (result.astype(jnp.bfloat16), gradients[0].astype(jnp.bfloat16), gradients[1].astype(jnp.bfloat16)))
    initial = (jnp.zeros(wide_master.shape, jnp.float32), jnp.zeros(narrow_master.shape, jnp.float32), jnp.zeros(vec_master.shape, jnp.float32))
    totals, (outputs, input_grads, encoder_grads) = lax.scan(one_sequence, initial, (seq_tokens, seq_encoded, seq_cotangent, block_mask))
    factor = float(TOKENS) ** (-0.5)
    wide_grad = totals[0] * factor
    narrow_grad = totals[1] * factor
    vec_grad = totals[2] * factor
    wide_new, wide_first_new, wide_second_new = adam_update(wide_master, wide_first, wide_second, wide_grad, weight_decay, learn_rate)
    narrow_new, narrow_first_new, narrow_second_new = adam_update(narrow_master, narrow_first, narrow_second, narrow_grad, weight_decay, learn_rate)
    vec_new, vec_first_new, vec_second_new = adam_update(vec_master, vec_first, vec_second, vec_grad, 0.0, vec_rate)
    return (outputs.reshape(TOKENS, D), input_grads.reshape(TOKENS, D), encoder_grads.reshape(ENC_ALL, D), wide_grad, narrow_grad, vec_grad, wide_new, narrow_new, vec_new, wide_first_new, narrow_first_new, vec_first_new, wide_second_new, narrow_second_new, vec_second_new, wide_new.astype(jnp.bfloat16), narrow_new.astype(jnp.bfloat16), vec_new.astype(jnp.bfloat16))
```

```python
from functools import partial
import math

import jax
import jax.numpy as jnp
from jax import lax
from jax.experimental import pallas as pl
from jax.experimental.pallas import tpu as pltpu
from jax.sharding import PartitionSpec as P

D = 768
H = 12
HD = 64
FF = 3072
LEN = 1024
BLK = 256
STEP = 4


eps_norm = 1e-05
eps_adam = 1e-08
beta_one = 0.5
beta_two = 0.5
learn_rate = 0.03
vec_rate = 0.25
weight_decay = 0.1
masked_score = -1e30
FACTOR = HD ** (-0.5)
SCALE2 = FACTOR / math.log(2.0)


def matmul(left, right):
    return jnp.dot(left, right, preferred_element_type=jnp.float32)


def matmul_left(left, right):
    return lax.dot_general(
        left, right, (((0,), (0,)), ((), ())), preferred_element_type=jnp.float32
    )


def matmul_right(left, right):
    return lax.dot_general(
        left, right, (((1,), (1,)), ((), ())), preferred_element_type=jnp.float32
    )


def norm_forward(resid, gain, shift):
    average = jnp.mean(resid, axis=-1, keepdims=True)
    centred = resid - average
    inverse = lax.rsqrt(jnp.mean(centred * centred, axis=-1, keepdims=True) + eps_norm)
    normed = centred * inverse
    return (normed * gain + shift, normed, inverse)


def norm_backward(upstream, normed, inverse, gain):
    scaled = upstream * gain
    centred = scaled - jnp.mean(scaled, axis=-1, keepdims=True)
    resid_grad = inverse * (centred - normed * jnp.mean(scaled * normed, axis=-1, keepdims=True))
    return (resid_grad, jnp.sum(upstream * normed, axis=0), jnp.sum(upstream, axis=0))


def head_masks(rows):
    first = lax.broadcasted_iota(jnp.int32, (rows, 128), 1) < HD
    return (first, jnp.logical_not(first))


def keep(mask, value):
    return jnp.where(mask, value, jnp.zeros((), value.dtype))


def rows_dot(left, right):
    return jnp.dot(left, right, preferred_element_type=jnp.float32)


def rows_dot_t(left, right):
    return lax.dot_general(
        left, right, (((1,), (1,)), ((), ())), preferred_element_type=jnp.float32
    )


def forward_kernel(causal, mask_ref, q_ref, k_ref, v_ref, o_ref, lse_ref, qm_ref, vt_ref, acc_ref, sum_ref, top_ref):
    rows, keys = q_ref.shape[0], k_ref.shape[0]
    tile = BLK
    seq = pl.program_id(0)
    queries = q_ref[...]
    for head, mask in enumerate(head_masks(rows)):
        qm_ref[head] = keep(mask, queries)
    vt_ref[...] = v_ref[...].T
    if causal:
        below = lax.broadcasted_iota(jnp.int32, (BLK, BLK), 0) <= lax.broadcasted_iota(
            jnp.int32, (BLK, BLK), 1
        )

    def start_of(j):
        return j * tile if causal else 0

    def scores_of(j, head):
        begin = start_of(j)
        scores = rows_dot_t(k_ref[j * tile : (j + 1) * tile, :], qm_ref[head, begin:, :]) * SCALE2
        if causal:
            pieces = [jnp.where(below, scores[:, :BLK], masked_score)]
            for i in range(j + 1, rows // BLK):
                off = jnp.where(mask_ref[seq, i, j] > 0, 0.0, masked_score)
                pieces.append(scores[:, (i - j) * BLK : (i - j + 1) * BLK] + off)
            scores = jnp.concatenate(pieces, axis=1)
        return scores

    def add_tile(j, head, scores, shift):
        begin = start_of(j)
        if shift is not None:
            scores = scores - shift[:, begin:]
        probs = jnp.exp2(scores)
        total = jnp.sum(probs, axis=0, keepdims=True)
        mixed = rows_dot(
            vt_ref[head * HD : (head + 1) * HD, j * tile : (j + 1) * tile], probs.astype(jnp.bfloat16)
        )
        if j == 0:
            sum_ref[head : head + 1, :] = total
            acc_ref[head] = mixed
        else:
            sum_ref[head : head + 1, begin:] += total
            acc_ref[head, :, begin:] += mixed

    def finish(shifts):
        both = []
        for head in range(2):
            total = sum_ref[head : head + 1, :]
            lse = jnp.log2(total)
            if shifts is not None:
                lse = lse + shifts[head]
            lse_ref[0, 0, head : head + 1, :] = lse
            both.append(acc_ref[head] * (1.0 / total))
        o_ref[...] = jnp.concatenate(both, axis=0).T.astype(jnp.bfloat16)

    lse_ref[...] = jnp.zeros_like(lse_ref)
    waiting = []
    for j in range(keys // tile):
        for head in range(2):
            waiting.append((j, head, scores_of(j, head)))
            if len(waiting) > 1:
                add_tile(*waiting.pop(0), None)
    while waiting:
        add_tile(*waiting.pop(0), None)
    finish(None)
    sums = sum_ref[...]
    usable = jnp.min(jnp.where((sums > 1e-25) & (sums < 1e30), 1, 0))

    @pl.when(usable == 0)
    def _():
        for head in range(2):
            for j in range(keys // tile):
                peak = jnp.max(scores_of(j, head), axis=0, keepdims=True)
                begin = start_of(j)
                if j == 0:
                    top_ref[head : head + 1, :] = peak
                else:
                    top_ref[head : head + 1, begin:] = jnp.maximum(
                        top_ref[head : head + 1, begin:], peak
                    )
        shifts = [top_ref[0:1, :], top_ref[1:2, :]]
        for head in range(2):
            for j in range(keys // tile):
                add_tile(j, head, scores_of(j, head), shifts[head])
        finish(shifts)


def attend_forward(queries, keys_in, values_in, block_table, causal):
    seqs = block_table.shape[0]
    rows, keys = queries.shape[0] // seqs, keys_in.shape[0] // seqs
    spec_q = pl.BlockSpec((rows, 128), lambda s, i, m: (s, i))
    spec_k = pl.BlockSpec((keys, 128), lambda s, i, m: (s, i))
    spec_l = pl.BlockSpec((1, 1, 8, rows), lambda s, i, m: (s, i, 0, 0))
    area = rows * keys * H * HD * seqs
    return pl.pallas_call(
        partial(forward_kernel, causal),
        grid_spec=pltpu.PrefetchScalarGridSpec(
            num_scalar_prefetch=1,
            grid=(seqs, D // 128),
            in_specs=[spec_q, spec_k, spec_k],
            out_specs=[spec_q, spec_l],
            scratch_shapes=[
                pltpu.VMEM((2, rows, 128), jnp.bfloat16),
                pltpu.VMEM((128, keys), jnp.bfloat16),
                pltpu.VMEM((2, HD, rows), jnp.float32),
                pltpu.VMEM((2, rows), jnp.float32),
                pltpu.VMEM((2, rows), jnp.float32),
            ],
        ),
        out_shape=[
            jax.ShapeDtypeStruct(queries.shape, jnp.bfloat16),
            jax.ShapeDtypeStruct((seqs, D // 128, 8, rows), jnp.float32),
        ],
        compiler_params=pltpu.CompilerParams(vmem_limit_bytes=48 << 20),
        cost_estimate=pl.CostEstimate(
            flops=(8 if causal else 16) * area, bytes_accessed=4 * queries.size, transcendentals=0
        ),
    )(block_table, queries, keys_in, values_in)


def backward_kernel(
    causal, mask_ref, q_ref, k_ref, v_ref, m_ref, x_ref, lse_ref, dq_ref, dk_ref, dv_ref,
    qm_ref, mm_ref, qt_ref, mt_ref, col_ref, acc_ref, dkt_ref, dvt_ref,
):
    rows, keys = q_ref.shape[0], k_ref.shape[0]
    seq = pl.program_id(0)
    step, tile = (BLK, BLK) if causal else (2 * BLK, 2 * BLK)
    masks = head_masks(rows)
    masks_k = head_masks(tile)
    queries, grads = q_ref[...], m_ref[...]
    qt_ref[...] = queries.T
    mt_ref[...] = grads.T
    product = grads.astype(jnp.float32) * x_ref[...].astype(jnp.float32)
    lse = lse_ref[0, 0].T
    for head in range(2):
        qm_ref[head] = keep(masks[head], queries)
        mm_ref[head] = keep(masks[head], grads)
        centre = jnp.sum(keep(masks[head], product), axis=1, keepdims=True)
        col_ref[head] = jnp.broadcast_to(centre, (rows, 128))
        col_ref[2 + head] = jnp.broadcast_to(lse[:, head : head + 1], (rows, 128))
    if causal:
        below = lax.broadcasted_iota(jnp.int32, (BLK, BLK), 0) >= lax.broadcasted_iota(
            jnp.int32, (BLK, BLK), 1
        )

    def widen(column):
        return jnp.concatenate([column] * (tile // 128), axis=1)

    for j in range(keys // tile):
        key_rows = slice(j * tile, (j + 1) * tile)
        key, value = k_ref[key_rows, :], v_ref[key_rows, :]
        key_masked = [keep(mask, key) for mask in masks_k]
        total_k, total_v = [None, None], [None, None]
        first_step = j if causal else 0
        for i in range(first_step, rows // step):
            here = slice(i * step, (i + 1) * step)
            for head in range(2):
                scores = rows_dot_t(qm_ref[head, here, :], key)
                prob_grad = rows_dot_t(mm_ref[head, here, :], value)
                level = col_ref[2 + head, here]
                if causal and i > j:
                    level = level + jnp.where(mask_ref[seq, i, j] > 0, 0.0, -masked_score)
                probs = jnp.exp2(scores * SCALE2 - widen(level))
                if causal and i == j:
                    probs = jnp.where(below, probs, 0.0)
                score_grad = (probs * (prob_grad - widen(col_ref[head, here]))).astype(jnp.bfloat16)
                probs = probs.astype(jnp.bfloat16)
                part = slice(head * HD, (head + 1) * HD)
                add_v = rows_dot(mt_ref[part, here], probs)
                add_k = rows_dot(qt_ref[part, here], score_grad)
                total_v[head] = add_v if total_v[head] is None else total_v[head] + add_v
                total_k[head] = add_k if total_k[head] is None else total_k[head] + add_k
                add_q = rows_dot(score_grad, key_masked[head])
                if j == 0 and head == 0:
                    acc_ref[here, :] = add_q
                else:
                    acc_ref[here, :] += add_q
        for head in range(2):
            part = slice(head * HD, (head + 1) * HD)
            dkt_ref[part, key_rows] = total_k[head] * FACTOR
            dvt_ref[part, key_rows] = total_v[head]
    dq_ref[...] = (acc_ref[...] * FACTOR).astype(jnp.bfloat16)
    dk_ref[...] = dkt_ref[...].T.astype(jnp.bfloat16)
    dv_ref[...] = dvt_ref[...].T.astype(jnp.bfloat16)


def attend_backward(queries, keys_in, values_in, block_table, causal, mixed, lse, mixed_grad):
    seqs = block_table.shape[0]
    rows, keys = queries.shape[0] // seqs, keys_in.shape[0] // seqs
    spec_q = pl.BlockSpec((rows, 128), lambda s, i, m: (s, i))
    spec_k = pl.BlockSpec((keys, 128), lambda s, i, m: (s, i))
    spec_l = pl.BlockSpec((1, 1, 8, rows), lambda s, i, m: (s, i, 0, 0))
    area = rows * keys * H * HD * seqs
    return pl.pallas_call(
        partial(backward_kernel, causal),
        grid_spec=pltpu.PrefetchScalarGridSpec(
            num_scalar_prefetch=1,
            grid=(seqs, D // 128),
            in_specs=[spec_q, spec_k, spec_k, spec_q, spec_q, spec_l],
            out_specs=[spec_q, spec_k, spec_k],
            scratch_shapes=[
                pltpu.VMEM((2, rows, 128), jnp.bfloat16),
                pltpu.VMEM((2, rows, 128), jnp.bfloat16),
                pltpu.VMEM((128, rows), jnp.bfloat16),
                pltpu.VMEM((128, rows), jnp.bfloat16),
                pltpu.VMEM((4, rows, 128), jnp.float32),
                pltpu.VMEM((rows, 128), jnp.float32),
                pltpu.VMEM((128, keys), jnp.float32),
                pltpu.VMEM((128, keys), jnp.float32),
            ],
        ),
        out_shape=[
            jax.ShapeDtypeStruct(queries.shape, jnp.bfloat16),
            jax.ShapeDtypeStruct(keys_in.shape, jnp.bfloat16),
            jax.ShapeDtypeStruct(keys_in.shape, jnp.bfloat16),
        ],
        compiler_params=pltpu.CompilerParams(vmem_limit_bytes=48 << 20),
        cost_estimate=pl.CostEstimate(
            flops=(20 if causal else 40) * area, bytes_accessed=4 * queries.size, transcendentals=0
        ),
    )(block_table, queries, keys_in, values_in, mixed_grad, mixed, lse)


def adam_update(master, first, second, gradient, decay_on, rate):
    first_new = beta_one * first + (1.0 - beta_one) * gradient
    second_new = beta_two * second + (1.0 - beta_two) * gradient * gradient
    first_hat = first_new / (1.0 - beta_one**STEP)
    second_hat = second_new / (1.0 - beta_two**STEP)
    master_new = master - rate * (first_hat / (jnp.sqrt(second_hat) + eps_adam) + decay_on * master)
    return (master_new, first_new, second_new)


def column_sum(matrix):
    return jnp.sum(matrix.astype(jnp.float32), axis=0)


def on_device(
    tokens,
    encoder_states,
    cotangent,
    block_mask,
    wide_master,
    narrow_master,
    vec_master,
    wide_first,
    narrow_first,
    vec_first,
    wide_second,
    narrow_second,
    vec_second,
):
    replicas = lax.axis_size("rep")
    shards = lax.axis_size("shard")
    tokens_all = tokens.shape[0] * replicas * shards

    copies = (
        wide_master.astype(jnp.bfloat16),
        narrow_master.astype(jnp.bfloat16),
        vec_master.astype(jnp.bfloat16),
    )
    wide_full, narrow_full, vec_full = (
        lax.all_gather(copies[0], "shard", axis=0, tiled=True),
        lax.all_gather(copies[1], "shard", axis=0, tiled=True),
        lax.all_gather(copies[2], "shard", axis=0, tiled=True),
    )
    vector = vec_full.astype(jnp.float32)
    ffn_bias = vector[:, 6:10].T.reshape(FF)
    joint_proj = matmul(tokens, wide_full[:, : 3 * D])
    queries = (joint_proj[:, :D] + vector[:, 0]).astype(jnp.bfloat16)
    keys_self = joint_proj[:, D : 2 * D].astype(jnp.bfloat16)
    values_self = (joint_proj[:, 2 * D :] + vector[:, 1]).astype(jnp.bfloat16)
    mixed_self, totals_self = attend_forward(queries, keys_self, values_self, block_mask, True)
    branch_one = matmul(mixed_self, wide_full[:, 3 * D : 4 * D]) + vector[:, 2]
    normed_one, unit_one, scale_one = norm_forward(
        tokens.astype(jnp.float32) + branch_one, vector[:, 11], vector[:, 14]
    )
    normed_low = normed_one.astype(jnp.bfloat16)
    cross_queries = (matmul(normed_low, wide_full[:, 4 * D : 5 * D]) + vector[:, 3]).astype(
        jnp.bfloat16
    )
    enc_proj = matmul(encoder_states, wide_full[:, 5 * D : 7 * D])
    cross_keys = enc_proj[:, :D].astype(jnp.bfloat16)
    cross_values = (enc_proj[:, D:] + vector[:, 4]).astype(jnp.bfloat16)

    mixed_cross, totals_cross = attend_forward(
        cross_queries, cross_keys, cross_values, block_mask, False
    )
    branch_two = matmul(mixed_cross, wide_full[:, 7 * D : 8 * D]) + vector[:, 5]
    normed_two, unit_two, scale_two = norm_forward(
        normed_one + branch_two, vector[:, 12], vector[:, 15]
    )
    second_low = normed_two.astype(jnp.bfloat16)
    hidden = matmul(second_low, wide_full[:, 8 * D :]) + ffn_bias
    active_full, gelu_pull = jax.vjp(partial(jax.nn.gelu, approximate=False), hidden)
    active = active_full.astype(jnp.bfloat16)
    branch_three = matmul(active, narrow_full) + vector[:, 10]
    final_out, unit_three, scale_three = norm_forward(
        normed_two + branch_three, vector[:, 13], vector[:, 16]
    )
    output = final_out.astype(jnp.bfloat16)
    grad_three, gain_three, shift_three = norm_backward(
        cotangent.astype(jnp.float32), unit_three, scale_three, vector[:, 13]
    )
    grad_ffn = grad_three.astype(jnp.bfloat16)
    grad_narrow = matmul_left(active, grad_ffn)
    grad_hidden = gelu_pull(matmul_right(grad_ffn, narrow_full))[0].astype(jnp.bfloat16)
    grad_ffn_in = matmul_left(second_low, grad_hidden)
    grad_two, gain_two, shift_two = norm_backward(
        grad_three + matmul_right(grad_hidden, wide_full[:, 8 * D :]),
        unit_two,
        scale_two,
        vector[:, 12],
    )
    grad_cross = grad_two.astype(jnp.bfloat16)
    grad_cross_out = matmul_left(mixed_cross, grad_cross)
    grad_cross_mix = matmul_right(grad_cross, wide_full[:, 7 * D : 8 * D]).astype(jnp.bfloat16)

    grad_cross_queries, grad_cross_keys, grad_cross_values = attend_backward(
        cross_queries, cross_keys, cross_values, block_mask, False, mixed_cross, totals_cross, grad_cross_mix
    )
    grad_enc_proj = jnp.concatenate([grad_cross_keys, grad_cross_values], 1)
    grad_cross_query = matmul_left(normed_low, grad_cross_queries)
    grad_cross_pair = matmul_left(encoder_states, grad_enc_proj)
    enc_grad = matmul_right(grad_enc_proj, wide_full[:, 5 * D : 7 * D]).astype(jnp.bfloat16)
    grad_one, gain_one, shift_one = norm_backward(
        grad_two + matmul_right(grad_cross_queries, wide_full[:, 4 * D : 5 * D]),
        unit_one,
        scale_one,
        vector[:, 11],
    )
    grad_self = grad_one.astype(jnp.bfloat16)
    grad_self_out = matmul_left(mixed_self, grad_self)
    grad_self_mix = matmul_right(grad_self, wide_full[:, 3 * D : 4 * D]).astype(jnp.bfloat16)

    grad_queries, grad_keys, grad_values = attend_backward(
        queries, keys_self, values_self, block_mask, True, mixed_self, totals_self, grad_self_mix
    )
    grad_joint_proj = jnp.concatenate([grad_queries, grad_keys, grad_values], 1)
    grad_joint = matmul_left(tokens, grad_joint_proj)
    in_grad = (grad_one + matmul_right(grad_joint_proj, wide_full[:, : 3 * D])).astype(jnp.bfloat16)
    factor = float(tokens_all) ** (-0.5)

    def summed(term):
        owned = lax.psum_scatter(
            (term * factor).astype(jnp.bfloat16), "shard", scatter_dimension=0, tiled=True
        )
        return lax.psum(owned, "rep").astype(jnp.float32)

    ffn_sum = summed(grad_ffn_in)
    narrow_grad = summed(grad_narrow)
    cross_sum = summed(jnp.concatenate([grad_self_out, grad_cross_query, grad_cross_pair, grad_cross_out], 1))
    joint_sum = summed(grad_joint)
    wide_grad = jnp.concatenate([joint_sum, cross_sum, ffn_sum], 1)
    bias_front = jnp.stack(
        [
            column_sum(grad_joint_proj[:, :D]),
            column_sum(grad_joint_proj[:, 2 * D :]),
            column_sum(grad_self),
            column_sum(grad_cross_queries),
            column_sum(grad_enc_proj[:, D:]),
            column_sum(grad_cross),
        ],
        1,
    )
    bias_back = jnp.stack(
        [column_sum(grad_ffn), gain_one, gain_two, gain_three, shift_one, shift_two, shift_three], 1
    )
    vec_grad = summed(jnp.concatenate([bias_front, column_sum(grad_hidden).reshape(4, D).T, bias_back], 1))
    wide_new, wide_first_new, wide_second_new = adam_update(
        wide_master, wide_first, wide_second, wide_grad, weight_decay, learn_rate
    )
    narrow_new, narrow_first_new, narrow_second_new = adam_update(
        narrow_master, narrow_first, narrow_second, narrow_grad, weight_decay, learn_rate
    )
    vec_new, vec_first_new, vec_second_new = adam_update(
        vec_master, vec_first, vec_second, vec_grad, 0.0, vec_rate
    )
    return (
        output,
        in_grad,
        enc_grad,
        wide_grad,
        narrow_grad,
        vec_grad,
        wide_new,
        narrow_new,
        vec_new,
        wide_first_new,
        narrow_first_new,
        vec_first_new,
        wide_second_new,
        narrow_second_new,
        vec_second_new,
        wide_new.astype(jnp.bfloat16),
        narrow_new.astype(jnp.bfloat16),
        vec_new.astype(jnp.bfloat16),
    )


def solution(mesh):
    in_specs = (
        P(("rep", "shard"), None),
        P(("rep", "shard"), None),
        P(("rep", "shard"), None),
        P(("rep", "shard"), None, None),
        P("shard", None),
        P("shard", None),
        P("shard", None),
        P("shard", None),
        P("shard", None),
        P("shard", None),
        P("shard", None),
        P("shard", None),
        P("shard", None),
    )
    out_specs = (
        P(("rep", "shard"), None),
        P(("rep", "shard"), None),
        P(("rep", "shard"), None),
        P("shard", None),
        P("shard", None),
        P("shard", None),
        P("shard", None),
        P("shard", None),
        P("shard", None),
        P("shard", None),
        P("shard", None),
        P("shard", None),
        P("shard", None),
        P("shard", None),
        P("shard", None),
        P("shard", None),
        P("shard", None),
        P("shard", None),
    )
    return jax.shard_map(
        on_device, mesh=mesh, in_specs=in_specs, out_specs=out_specs, check_vma=False
    )
```

```python
from functools import partial
import math

import jax
import jax.numpy as jnp
from jax import lax
from jax.experimental import pallas as pl
from jax.experimental.pallas import tpu as pltpu
from jax.sharding import PartitionSpec as P

D = 768
H = 12
HD = 64
FF = 3072
LEN = 1024
BLK = 256
STEP = 4


eps_norm = 1e-05
eps_adam = 1e-08
beta_one = 0.5
beta_two = 0.5
learn_rate = 0.03
vec_rate = 0.25
weight_decay = 0.1
masked_score = -1e30
FACTOR = HD ** (-0.5)
SCALE2 = FACTOR / math.log(2.0)


def head_masks(rows):
    first = lax.broadcasted_iota(jnp.int32, (rows, 128), 1) < HD
    return (first, jnp.logical_not(first))


def keep(mask, value):
    return jnp.where(mask, value, jnp.zeros((), value.dtype))


def rows_dot(left, right):
    return jnp.dot(left, right, preferred_element_type=jnp.float32)


def rows_dot_t(left, right):
    return lax.dot_general(
        left, right, (((1,), (1,)), ((), ())), preferred_element_type=jnp.float32
    )


def forward_kernel(causal, mask_ref, q_ref, k_ref, v_ref, o_ref, lse_ref, qm_ref, vt_ref, acc_ref, sum_ref, top_ref):
    rows, keys = q_ref.shape[0], k_ref.shape[0]
    tile = BLK
    seq = pl.program_id(0)
    queries = q_ref[...]
    for head, mask in enumerate(head_masks(rows)):
        qm_ref[head] = keep(mask, queries)
    vt_ref[...] = v_ref[...].T
    if causal:
        below = lax.broadcasted_iota(jnp.int32, (BLK, BLK), 0) <= lax.broadcasted_iota(
            jnp.int32, (BLK, BLK), 1
        )

    def start_of(j):
        return j * tile if causal else 0

    def scores_of(j, head):
        begin = start_of(j)
        scores = rows_dot_t(k_ref[j * tile : (j + 1) * tile, :], qm_ref[head, begin:, :]) * SCALE2
        if causal:
            pieces = [jnp.where(below, scores[:, :BLK], masked_score)]
            for i in range(j + 1, rows // BLK):
                off = jnp.where(mask_ref[seq, i, j] > 0, 0.0, masked_score)
                pieces.append(scores[:, (i - j) * BLK : (i - j + 1) * BLK] + off)
            scores = jnp.concatenate(pieces, axis=1)
        return scores

    def add_tile(j, head, scores, shift):
        begin = start_of(j)
        if shift is not None:
            scores = scores - shift[:, begin:]
        probs = jnp.exp2(scores)
        total = jnp.sum(probs, axis=0, keepdims=True)
        mixed = rows_dot(
            vt_ref[head * HD : (head + 1) * HD, j * tile : (j + 1) * tile], probs.astype(jnp.bfloat16)
        )
        if j == 0:
            sum_ref[head : head + 1, :] = total
            acc_ref[head] = mixed
        else:
            sum_ref[head : head + 1, begin:] += total
            acc_ref[head, :, begin:] += mixed

    def finish(shifts):
        both = []
        for head in range(2):
            total = sum_ref[head : head + 1, :]
            lse = jnp.log2(total)
            if shifts is not None:
                lse = lse + shifts[head]
            lse_ref[0, 0, head : head + 1, :] = lse
            both.append(acc_ref[head] * (1.0 / total))
        o_ref[...] = jnp.concatenate(both, axis=0).T.astype(jnp.bfloat16)

    lse_ref[...] = jnp.zeros_like(lse_ref)
    waiting = []
    for j in range(keys // tile):
        for head in range(2):
            waiting.append((j, head, scores_of(j, head)))
            if len(waiting) > 1:
                add_tile(*waiting.pop(0), None)
    while waiting:
        add_tile(*waiting.pop(0), None)
    finish(None)
    sums = sum_ref[...]
    usable = jnp.min(jnp.where((sums > 1e-25) & (sums < 1e30), 1, 0))

    @pl.when(usable == 0)
    def _():
        for head in range(2):
            for j in range(keys // tile):
                peak = jnp.max(scores_of(j, head), axis=0, keepdims=True)
                begin = start_of(j)
                if j == 0:
                    top_ref[head : head + 1, :] = peak
                else:
                    top_ref[head : head + 1, begin:] = jnp.maximum(
                        top_ref[head : head + 1, begin:], peak
                    )
        shifts = [top_ref[0:1, :], top_ref[1:2, :]]
        for head in range(2):
            for j in range(keys // tile):
                add_tile(j, head, scores_of(j, head), shifts[head])
        finish(shifts)


def attend_forward(queries, keys_in, values_in, block_table, causal):
    seqs = block_table.shape[0]
    rows, keys = queries.shape[0] // seqs, keys_in.shape[0] // seqs
    spec_q = pl.BlockSpec((rows, 128), lambda s, i, m: (s, i))
    spec_k = pl.BlockSpec((keys, 128), lambda s, i, m: (s, i))
    spec_l = pl.BlockSpec((1, 1, 8, rows), lambda s, i, m: (s, i, 0, 0))
    area = rows * keys * H * HD * seqs
    return pl.pallas_call(
        partial(forward_kernel, causal),
        grid_spec=pltpu.PrefetchScalarGridSpec(
            num_scalar_prefetch=1,
            grid=(seqs, D // 128),
            in_specs=[spec_q, spec_k, spec_k],
            out_specs=[spec_q, spec_l],
            scratch_shapes=[
                pltpu.VMEM((2, rows, 128), jnp.bfloat16),
                pltpu.VMEM((128, keys), jnp.bfloat16),
                pltpu.VMEM((2, HD, rows), jnp.float32),
                pltpu.VMEM((2, rows), jnp.float32),
                pltpu.VMEM((2, rows), jnp.float32),
            ],
        ),
        out_shape=[
            jax.ShapeDtypeStruct(queries.shape, jnp.bfloat16),
            jax.ShapeDtypeStruct((seqs, D // 128, 8, rows), jnp.float32),
        ],
        compiler_params=pltpu.CompilerParams(vmem_limit_bytes=48 << 20),
        cost_estimate=pl.CostEstimate(
            flops=(8 if causal else 16) * area, bytes_accessed=4 * queries.size, transcendentals=0
        ),
    )(block_table, queries, keys_in, values_in)


def backward_kernel(
    causal, mask_ref, q_ref, k_ref, v_ref, m_ref, x_ref, lse_ref, dq_ref, dk_ref, dv_ref,
    qm_ref, mm_ref, qt_ref, mt_ref, col_ref, acc_ref, dkt_ref, dvt_ref,
):
    rows, keys = q_ref.shape[0], k_ref.shape[0]
    seq = pl.program_id(0)
    step, tile = (BLK, BLK) if causal else (2 * BLK, 2 * BLK)
    masks = head_masks(rows)
    masks_k = head_masks(tile)
    queries, grads = q_ref[...], m_ref[...]
    qt_ref[...] = queries.T
    mt_ref[...] = grads.T
    product = grads.astype(jnp.float32) * x_ref[...].astype(jnp.float32)
    lse = lse_ref[0, 0].T
    for head in range(2):
        qm_ref[head] = keep(masks[head], queries)
        mm_ref[head] = keep(masks[head], grads)
        centre = jnp.sum(keep(masks[head], product), axis=1, keepdims=True)
        col_ref[head] = jnp.broadcast_to(centre, (rows, 128))
        col_ref[2 + head] = jnp.broadcast_to(lse[:, head : head + 1], (rows, 128))
    if causal:
        below = lax.broadcasted_iota(jnp.int32, (BLK, BLK), 0) >= lax.broadcasted_iota(
            jnp.int32, (BLK, BLK), 1
        )

    def widen(column):
        return jnp.concatenate([column] * (tile // 128), axis=1)

    for j in range(keys // tile):
        key_rows = slice(j * tile, (j + 1) * tile)
        key, value = k_ref[key_rows, :], v_ref[key_rows, :]
        key_masked = [keep(mask, key) for mask in masks_k]
        total_k, total_v = [None, None], [None, None]
        first_step = j if causal else 0
        for i in range(first_step, rows // step):
            here = slice(i * step, (i + 1) * step)
            for head in range(2):
                scores = rows_dot_t(qm_ref[head, here, :], key)
                prob_grad = rows_dot_t(mm_ref[head, here, :], value)
                level = col_ref[2 + head, here]
                if causal and i > j:
                    level = level + jnp.where(mask_ref[seq, i, j] > 0, 0.0, -masked_score)
                probs = jnp.exp2(scores * SCALE2 - widen(level))
                if causal and i == j:
                    probs = jnp.where(below, probs, 0.0)
                score_grad = (probs * (prob_grad - widen(col_ref[head, here]))).astype(jnp.bfloat16)
                probs = probs.astype(jnp.bfloat16)
                part = slice(head * HD, (head + 1) * HD)
                add_v = rows_dot(mt_ref[part, here], probs)
                add_k = rows_dot(qt_ref[part, here], score_grad)
                total_v[head] = add_v if total_v[head] is None else total_v[head] + add_v
                total_k[head] = add_k if total_k[head] is None else total_k[head] + add_k
                add_q = rows_dot(score_grad, key_masked[head])
                if j == 0 and head == 0:
                    acc_ref[here, :] = add_q
                else:
                    acc_ref[here, :] += add_q
        for head in range(2):
            part = slice(head * HD, (head + 1) * HD)
            dkt_ref[part, key_rows] = total_k[head] * FACTOR
            dvt_ref[part, key_rows] = total_v[head]
    dq_ref[...] = (acc_ref[...] * FACTOR).astype(jnp.bfloat16)
    dk_ref[...] = dkt_ref[...].T.astype(jnp.bfloat16)
    dv_ref[...] = dvt_ref[...].T.astype(jnp.bfloat16)


def attend_backward(queries, keys_in, values_in, block_table, causal, mixed, lse, mixed_grad):
    seqs = block_table.shape[0]
    rows, keys = queries.shape[0] // seqs, keys_in.shape[0] // seqs
    spec_q = pl.BlockSpec((rows, 128), lambda s, i, m: (s, i))
    spec_k = pl.BlockSpec((keys, 128), lambda s, i, m: (s, i))
    spec_l = pl.BlockSpec((1, 1, 8, rows), lambda s, i, m: (s, i, 0, 0))
    area = rows * keys * H * HD * seqs
    return pl.pallas_call(
        partial(backward_kernel, causal),
        grid_spec=pltpu.PrefetchScalarGridSpec(
            num_scalar_prefetch=1,
            grid=(seqs, D // 128),
            in_specs=[spec_q, spec_k, spec_k, spec_q, spec_q, spec_l],
            out_specs=[spec_q, spec_k, spec_k],
            scratch_shapes=[
                pltpu.VMEM((2, rows, 128), jnp.bfloat16),
                pltpu.VMEM((2, rows, 128), jnp.bfloat16),
                pltpu.VMEM((128, rows), jnp.bfloat16),
                pltpu.VMEM((128, rows), jnp.bfloat16),
                pltpu.VMEM((4, rows, 128), jnp.float32),
                pltpu.VMEM((rows, 128), jnp.float32),
                pltpu.VMEM((128, keys), jnp.float32),
                pltpu.VMEM((128, keys), jnp.float32),
            ],
        ),
        out_shape=[
            jax.ShapeDtypeStruct(queries.shape, jnp.bfloat16),
            jax.ShapeDtypeStruct(keys_in.shape, jnp.bfloat16),
            jax.ShapeDtypeStruct(keys_in.shape, jnp.bfloat16),
        ],
        compiler_params=pltpu.CompilerParams(vmem_limit_bytes=48 << 20),
        cost_estimate=pl.CostEstimate(
            flops=(20 if causal else 40) * area, bytes_accessed=4 * queries.size, transcendentals=0
        ),
    )(block_table, queries, keys_in, values_in, mixed_grad, mixed, lse)


ROWS = 256


def gelu_pair(x):
    magnitude = jnp.abs(x)
    bell = jnp.exp2((x * x) * (-0.5 / math.log(2.0)))
    t = 1.0 / (1.0 + (0.3275911 * math.sqrt(0.5)) * magnitude)
    poly = t * (0.127414796 + t * (-0.142248368 + t * (0.7107068705 + t * (-0.7265760135 + t * 0.5307027145))))
    tail = poly * bell
    phi_sum = jnp.where(x >= 0.0, 1.0 - tail, tail)
    return x * phi_sum, phi_sum + x * (bell * (1.0 / math.sqrt(2.0 * math.pi)))


def unit_rows(resid):
    average = jnp.mean(resid, axis=-1, keepdims=True)
    centred = resid - average
    inverse = lax.rsqrt(jnp.mean(centred * centred, axis=-1, keepdims=True) + eps_norm)
    return centred * inverse, inverse


def back_rows(upstream, unit, inverse, gain):
    scaled = upstream * gain
    centred = scaled - jnp.mean(scaled, axis=-1, keepdims=True)
    return inverse * (centred - unit * jnp.mean(scaled * unit, axis=-1, keepdims=True))


def column_dot(left, right):
    return lax.dot_general(left, right, (((0,), (0,)), ((), ())), preferred_element_type=jnp.float32)


def row_total(value):
    return jnp.sum(value, axis=0, keepdims=True)


def center_kernel(
    factor, mix_ref, one_ref, cot_ref, co_ref, win_ref, wout_ref, vec_ref,
    out_ref, two_ref, gmix_ref, tw_ref, tn_ref, tc_ref, sums_ref,
    low_ref, unit_ref, inv_ref, res_ref, act_ref, slope_ref, acc_ref, gffn_ref, bh_ref, gcross_ref,
):
    step = pl.program_id(0)
    rows = mix_ref.shape[0]
    blocks = rows // ROWS

    def vec(i):
        return vec_ref[i : i + 1, :]

    def each(body):
        def run(r, carry):
            body(pl.ds(pl.multiple_of(r * ROWS, ROWS), ROWS))
            return carry

        lax.fori_loop(0, blocks, run, 0)

    @pl.when(step == 0)
    def _():
        sums_ref[...] = jnp.zeros_like(sums_ref)

        def body(at):
            resid = one_ref[at, :] + rows_dot(mix_ref[at, :], co_ref[...]) + vec(5)
            unit, inverse = unit_rows(resid)
            unit_ref[at, :] = unit
            inv_ref[at, :] = jnp.broadcast_to(inverse, (ROWS, 128))
            normed = unit * vec(12) + vec(15)
            res_ref[at, :] = normed + vec(10)
            low_ref[at, :] = normed.astype(jnp.bfloat16)

        each(body)

    @pl.when(step < 4)
    def _():
        bias = vec_ref[pl.ds(6 + step, 1), :]

        def body(at):
            hidden = rows_dot(low_ref[at, :], win_ref[...]) + bias
            value, slope = gelu_pair(hidden)
            value = value.astype(jnp.bfloat16)
            act_ref[step, at, :] = value
            slope_ref[step, at, :] = slope.astype(jnp.bfloat16)
            res_ref[at, :] += rows_dot(value, wout_ref[...])

        each(body)

    @pl.when(step == 3)
    def _():
        def body(at):
            unit, inverse = unit_rows(res_ref[at, :])
            out_ref[at, :] = (unit * vec(13) + vec(16)).astype(jnp.bfloat16)
            upstream = cot_ref[at, :].astype(jnp.float32)
            grad = back_rows(upstream, unit, inverse, vec(13))
            acc_ref[at, :] = grad
            low = grad.astype(jnp.bfloat16)
            gffn_ref[at, :] = low
            sums_ref[13:14, :] += row_total(upstream * unit)
            sums_ref[16:17, :] += row_total(upstream)
            sums_ref[10:11, :] += row_total(low.astype(jnp.float32))

        each(body)

    @pl.when(step >= 4)
    def _():
        c = step - 4

        def body(at):
            grad = rows_dot_t(gffn_ref[at, :], wout_ref[...]) * slope_ref[c, at, :].astype(jnp.float32)
            low = grad.astype(jnp.bfloat16)
            bh_ref[at, :] = low
            sums_ref[pl.ds(step + 2, 1), :] += row_total(low.astype(jnp.float32))
            acc_ref[at, :] += rows_dot_t(low, win_ref[...])

        each(body)
        tn_ref[...] = (column_dot(act_ref[c], gffn_ref[...]) * factor).astype(jnp.bfloat16)
        rows_each = tw_ref.shape[1]
        for s in range(tw_ref.shape[0]):
            cols = slice(s * rows_each, (s + 1) * rows_each)
            tw_ref[s] = (column_dot(low_ref[:, cols], bh_ref[...]) * factor).astype(jnp.bfloat16)

    @pl.when(step == 7)
    def _():
        def body(at):
            upstream = acc_ref[at, :]
            unit = unit_ref[at, :]
            inverse = inv_ref[at, 0:1]
            grad = back_rows(upstream, unit, inverse, vec(12))
            two_ref[at, :] = grad
            low = grad.astype(jnp.bfloat16)
            gcross_ref[at, :] = low
            gmix_ref[at, :] = rows_dot_t(low, co_ref[...]).astype(jnp.bfloat16)
            sums_ref[12:13, :] += row_total(upstream * unit)
            sums_ref[15:16, :] += row_total(upstream)
            sums_ref[5:6, :] += row_total(low.astype(jnp.float32))

        each(body)
        tc_ref[...] = (column_dot(mix_ref[...], gcross_ref[...]) * factor).astype(jnp.bfloat16)


def center(mixed, one, cotangent, wide_full, narrow_full, vec_rows, factor, shards):
    rows = mixed.shape[0]
    whole = pl.BlockSpec((rows, D), lambda i: (0, 0))
    rows_each = D // shards
    bf16, f32 = jnp.bfloat16, jnp.float32
    return pl.pallas_call(
        partial(center_kernel, factor),
        grid=(8,),
        in_specs=[
            whole,
            whole,
            whole,
            pl.BlockSpec((D, D), lambda i: (0, 7)),
            pl.BlockSpec((D, D), lambda i: (0, 8 + i % 4)),
            pl.BlockSpec((D, D), lambda i: (i % 4, 0)),
            pl.BlockSpec(vec_rows.shape, lambda i: (0, 0)),
        ],
        out_specs=[
            whole,
            whole,
            whole,
            pl.BlockSpec((shards, rows_each, D), lambda i: (0, jnp.maximum(i - 4, 0), 0)),
            pl.BlockSpec((D, D), lambda i: (jnp.maximum(i - 4, 0), 0)),
            pl.BlockSpec((D, D), lambda i: (0, 0)),
            pl.BlockSpec((24, D), lambda i: (0, 0)),
        ],
        out_shape=[
            jax.ShapeDtypeStruct((rows, D), bf16),
            jax.ShapeDtypeStruct((rows, D), f32),
            jax.ShapeDtypeStruct((rows, D), bf16),
            jax.ShapeDtypeStruct((shards, 4 * rows_each, D), bf16),
            jax.ShapeDtypeStruct((FF, D), bf16),
            jax.ShapeDtypeStruct((D, D), bf16),
            jax.ShapeDtypeStruct((24, D), f32),
        ],
        scratch_shapes=[
            pltpu.VMEM((rows, D), bf16),
            pltpu.VMEM((rows, D), f32),
            pltpu.VMEM((rows, 128), f32),
            pltpu.VMEM((rows, D), f32),
            pltpu.VMEM((4, rows, D), bf16),
            pltpu.VMEM((4, rows, D), bf16),
            pltpu.VMEM((rows, D), f32),
            pltpu.VMEM((rows, D), bf16),
            pltpu.VMEM((rows, D), bf16),
            pltpu.VMEM((rows, D), bf16),
        ],
        compiler_params=pltpu.CompilerParams(vmem_limit_bytes=58 << 20),
        cost_estimate=pl.CostEstimate(flops=54 * rows * D * D, bytes_accessed=30 << 20, transcendentals=0),
    )(mixed, one, cotangent, wide_full, wide_full, narrow_full, vec_rows)


MESH_ID = pl.DeviceIdType.MESH


def peers_of(lanes):
    rep, shard = lax.axis_index("rep"), lax.axis_index("shard")
    x, y, z = rep % 2, (rep // 2) % 2, rep // 4
    base = rep - z * 4
    others = [(base + 4 * ((z + k) % lanes), shard) for k in range(1, lanes)]
    first = rep + 1 - 2 * x
    second = rep + 2 - 4 * y
    return rep, shard, x, y, z, (rep, 1 - shard), (first, shard), (second, shard), others


def enter_barrier(lanes):
    _, _, _, _, _, sibling, first, second, others = peers_of(lanes)
    barrier = pltpu.get_barrier_semaphore()
    for peer in [sibling, first, second] + others:
        pl.semaphore_signal(barrier, inc=1, device_id=peer, device_id_type=MESH_ID)
    pl.semaphore_wait(barrier, 2 + lanes)


def aligned(value):
    return pl.multiple_of(value, 16)


def bulk_scratch(rows, lanes):
    block = rows // (4 * lanes)
    bf16 = jnp.bfloat16
    return [
        pltpu.VMEM((rows, D), bf16),
        pltpu.VMEM((rows, D), bf16),
        pltpu.VMEM((rows // 2, D), bf16),
        pltpu.VMEM((rows // 4, D), bf16),
        pltpu.VMEM((lanes, block, D), bf16),
        pltpu.SemaphoreType.DMA((5 + 2 * lanes,)),
        pltpu.SemaphoreType.DMA((5 + 2 * lanes,)),
        pltpu.SemaphoreType.DMA((2,)),
    ]


def bulk_steps(term_ref, sum_ref, scratch, x_first, lanes):
    acc, got_core, got_a, got_b, got_z, send_sem, recv_sem, local_sem = scratch
    full = got_core
    rows = acc.shape[0]
    half, quarter, block = rows // 2, rows // 4, rows // (4 * lanes)
    rep, shard, x, y, z, sibling, peer_x, peer_y, others = peers_of(lanes)
    here_a, here_b = (x, y) if x_first else (y, x)
    peer_a, peer_b = (peer_x, peer_y) if x_first else (peer_y, peer_x)
    mine_a = aligned(here_a * half)
    theirs_a = aligned((1 - here_a) * half)
    mine_b = aligned(here_a * half + here_b * quarter)
    theirs_b = aligned(here_a * half + (1 - here_b) * quarter)
    mine_z = aligned(mine_b + z * block)

    def remote(index, source, target, peer):
        return pltpu.make_async_remote_copy(
            src_ref=source,
            dst_ref=target,
            send_sem=send_sem.at[index],
            recv_sem=recv_sem.at[index],
            device_id=peer,
            device_id_type=MESH_ID,
        )

    core = remote(0, term_ref.at[1 - shard], got_core, sibling)
    load = pltpu.make_async_copy(term_ref.at[shard], acc, local_sem.at[0])
    to_a = remote(1, acc.at[pl.ds(theirs_a, half)], got_a, peer_a)
    to_b = remote(2, acc.at[pl.ds(theirs_b, quarter)], got_b, peer_b)
    to_z, all_z = [], []
    for k, peer in enumerate(others):
        theirs = aligned(mine_b + ((z + k + 1) % lanes) * block)
        to_z.append(remote(5 + k, acc.at[pl.ds(theirs, block)], got_z.at[z], peer))
        all_z.append(
            remote(5 + lanes + k, full.at[pl.ds(mine_z, block)], full.at[pl.ds(mine_z, block)], peer)
        )
    all_b = remote(3, full.at[pl.ds(mine_b, quarter)], full.at[pl.ds(mine_b, quarter)], peer_b)
    all_a = remote(4, full.at[pl.ds(mine_a, half)], full.at[pl.ds(mine_a, half)], peer_a)
    store = pltpu.make_async_copy(full, sum_ref, local_sem.at[1])

    def add(start, count, got):
        def body(i, carry):
            there = pl.ds(aligned(start + i * block), block)
            total = acc[there, :].astype(jnp.float32) + got[pl.ds(aligned(i * block), block), :].astype(
                jnp.float32
            )
            acc[there, :] = total.astype(jnp.bfloat16)
            return carry

        lax.fori_loop(0, count // block, body, 0)

    def step_core():
        core.start()
        load.start()

    def step_a():
        load.wait()
        core.wait()
        add(0, rows, got_core)
        to_a.start()

    def step_b():
        to_a.wait()
        add(mine_a, half, got_a)
        to_b.start()

    def step_z():
        to_b.wait()
        add(mine_b, quarter, got_b)
        for copy in to_z:
            copy.start()

    def step_gather_z():
        for copy in to_z:
            copy.wait()
        there = pl.ds(mine_z, block)
        total = acc[there, :].astype(jnp.float32)
        for k in range(1, lanes):
            total = total + got_z[(z + k) % lanes].astype(jnp.float32)
        full[there, :] = total.astype(jnp.bfloat16)
        for copy in all_z:
            copy.start()

    def step_gather_b():
        for copy in all_z:
            copy.wait()
        all_b.start()

    def step_gather_a():
        all_b.wait()
        all_a.start()

    def step_store():
        all_a.wait()
        store.start()

    return [
        step_core, step_a, step_b, step_z, step_gather_z, step_gather_b, step_gather_a, step_store, store.wait,
    ]


def small_scratch(shape, lanes):
    return [
        pltpu.VMEM((3,) + shape, jnp.float32),
        pltpu.VMEM((3,) + shape, jnp.float32),
        pltpu.VMEM((lanes,) + shape, jnp.float32),
        pltpu.SemaphoreType.DMA((3 + lanes,)),
        pltpu.SemaphoreType.DMA((3 + lanes,)),
    ]


def small_steps(term_ref, sum_ref, scratch, lanes):
    held, got, got_z, send_sem, recv_sem = scratch
    rep, shard, x, y, z, sibling, peer_x, peer_y, others = peers_of(lanes)

    def remote(index, source, target, peer):
        return pltpu.make_async_remote_copy(
            src_ref=source,
            dst_ref=target,
            send_sem=send_sem.at[index],
            recv_sem=recv_sem.at[index],
            device_id=peer,
            device_id_type=MESH_ID,
        )

    core = remote(0, term_ref.at[1 - shard], got.at[0], sibling)
    to_x = remote(1, held.at[0], got.at[1], peer_x)
    to_y = remote(2, held.at[1], got.at[2], peer_y)
    to_z = [remote(3 + k, held.at[2], got_z.at[z], peer) for k, peer in enumerate(others)]

    def step_x():
        core.wait()
        held[0] = term_ref[shard] + got[0]
        to_x.start()

    def step_y():
        to_x.wait()
        held[1] = held[0] + got[1]
        to_y.start()

    def step_z():
        to_y.wait()
        held[2] = held[1] + got[2]
        got_z[z] = held[2]
        for copy in to_z:
            copy.start()

    def step_end():
        for copy in to_z:
            copy.wait()
        total = got_z[0]
        for k in range(1, lanes):
            total = total + got_z[k]
        sum_ref[...] = total

    return [core.start, step_x, step_y, step_z, step_end]


def interleave(plans):
    last = max(begin + len(steps) for begin, steps in plans)
    for tick in range(last):
        for begin, steps in plans:
            if 0 <= tick - begin < len(steps):
                steps[tick - begin]()


def reduce_kernel(lanes, count, *refs):
    terms, small_term = refs[:count], refs[count]
    sums, small_sum = refs[count + 1], refs[count + 2]
    scratch = refs[count + 3 :]
    enter_barrier(lanes)
    plans = []
    at = 0
    for i, term in enumerate(terms):
        rows = term.shape[1]
        plans.append(
            (i // 2, bulk_steps(term, sums.at[pl.ds(at, rows)], scratch[8 * i : 8 * i + 8], i % 2 == 0, lanes))
        )
        at += rows
    plans.append((0, small_steps(small_term, small_sum, scratch[8 * count :], lanes)))
    interleave(plans)


def reduce_all(terms, small, lanes):
    any_spec, vmem_spec = pl.BlockSpec(memory_space=pl.ANY), pl.BlockSpec(memory_space=pltpu.VMEM)
    count = len(terms)
    total = sum(term.shape[1] for term in terms)
    scratch = []
    for term in terms:
        scratch += bulk_scratch(term.shape[1], lanes)
    scratch += small_scratch(small.shape[1:], lanes)
    return pl.pallas_call(
        partial(reduce_kernel, lanes, count),
        in_specs=[any_spec] * count + [vmem_spec],
        out_specs=[any_spec, vmem_spec],
        out_shape=[
            jax.ShapeDtypeStruct((total, D), jnp.bfloat16),
            jax.ShapeDtypeStruct(small.shape[1:], jnp.float32),
        ],
        scratch_shapes=scratch,
        compiler_params=pltpu.CompilerParams(
            collective_id=0, has_side_effects=True, vmem_limit_bytes=56 << 20
        ),
    )(*terms, small)


def adam_update(master, first, second, gradient, decay_on, rate):
    first_new = beta_one * first + (1.0 - beta_one) * gradient
    second_new = beta_two * second + (1.0 - beta_two) * gradient * gradient
    first_hat = first_new / (1.0 - beta_one**STEP)
    second_hat = second_new / (1.0 - beta_two**STEP)
    master_new = master - rate * (first_hat / (jnp.sqrt(second_hat) + eps_adam) + decay_on * master)
    return (master_new, first_new, second_new)


def wide_column(i):
    return jnp.where(i < 4, i + 8, jnp.where(i < 8, 11, jnp.where(i < 12, i - 4, i - 12)))


def narrow_row(i):
    return jnp.clip(i - 4, 0, 3)


def adam_kernel(sum_ref, wm, wf, ws, nm, nf, ns, wg, wn, wfn, wsn, wc, ng, nn, nfn, nsn, nc):
    step = pl.program_id(0)

    def update(master, first, second, grad, new, first_new, second_new, copy):
        def body(r, carry):
            at = pl.ds(pl.multiple_of(r * 32, 32), 32)
            gradient = sum_ref[at, :].astype(jnp.float32)
            grad[at, :] = gradient
            value, one, two = adam_update(
                master[at, :], first[at, :], second[at, :], gradient, weight_decay, learn_rate
            )
            new[at, :] = value
            first_new[at, :] = one
            second_new[at, :] = two
            copy[at, :] = value.astype(jnp.bfloat16)
            return carry

        lax.fori_loop(0, sum_ref.shape[0] // 32, body, 0, unroll=True)

    narrow_step = (step >= 4) & (step < 8)

    @pl.when(jnp.logical_not(narrow_step))
    def _():
        update(wm, wf, ws, wg, wn, wfn, wsn, wc)

    @pl.when(narrow_step)
    def _():
        update(nm, nf, ns, ng, nn, nfn, nsn, nc)


def adam_all(sums, wide, narrow):
    rows = wide[0].shape[0]
    spec_w = pl.BlockSpec((rows, D), lambda i: (0, wide_column(i)))
    spec_n = pl.BlockSpec((rows, D), lambda i: (narrow_row(i), 0))
    f32, bf16 = jnp.float32, jnp.bfloat16

    def shapes(like):
        return [jax.ShapeDtypeStruct(like.shape, f32)] * 4 + [jax.ShapeDtypeStruct(like.shape, bf16)]

    return pl.pallas_call(
        adam_kernel,
        grid=(16,),
        in_specs=[pl.BlockSpec((rows, D), lambda i: (i, 0))] + [spec_w] * 3 + [spec_n] * 3,
        out_specs=[spec_w] * 5 + [spec_n] * 5,
        out_shape=shapes(wide[0]) + shapes(narrow[0]),
        compiler_params=pltpu.CompilerParams(vmem_limit_bytes=58 << 20),
    )(sums, *wide, *narrow)


def matmul(left, right):
    return jnp.dot(left, right, preferred_element_type=jnp.float32)


def matmul_left(left, right):
    return lax.dot_general(
        left, right, (((0,), (0,)), ((), ())), preferred_element_type=jnp.float32
    )


def matmul_right(left, right):
    return lax.dot_general(
        left, right, (((1,), (1,)), ((), ())), preferred_element_type=jnp.float32
    )


def norm_forward(resid, gain, shift):
    average = jnp.mean(resid, axis=-1, keepdims=True)
    centred = resid - average
    inverse = lax.rsqrt(jnp.mean(centred * centred, axis=-1, keepdims=True) + eps_norm)
    normed = centred * inverse
    return (normed * gain + shift, normed, inverse)


def norm_backward(upstream, normed, inverse, gain):
    scaled = upstream * gain
    centred = scaled - jnp.mean(scaled, axis=-1, keepdims=True)
    resid_grad = inverse * (centred - normed * jnp.mean(scaled * normed, axis=-1, keepdims=True))
    return (resid_grad, jnp.sum(upstream * normed, axis=0), jnp.sum(upstream, axis=0))


def column_sum(matrix):
    return jnp.sum(matrix.astype(jnp.float32), axis=0)


def on_device(
    tokens,
    encoder_states,
    cotangent,
    block_mask,
    wide_master,
    narrow_master,
    vec_master,
    wide_first,
    narrow_first,
    vec_first,
    wide_second,
    narrow_second,
    vec_second,
):
    replicas = lax.axis_size("rep")
    shards = lax.axis_size("shard")
    tokens_all = tokens.shape[0] * replicas * shards
    factor = float(tokens_all) ** (-0.5)
    bf16, f32 = jnp.bfloat16, jnp.float32

    def gathered(part):
        return lax.all_gather(part.astype(bf16), "shard", axis=0, tiled=True)

    wide_full = gathered(wide_master)
    narrow_full = gathered(narrow_master)
    vector = gathered(vec_master).astype(f32)
    vec_rows = jnp.pad(vector.T, ((0, 24 - vector.shape[1]), (0, 0)))
    joint_proj = matmul(tokens, wide_full[:, : 3 * D])
    queries = (joint_proj[:, :D] + vector[:, 0]).astype(bf16)
    keys_self = joint_proj[:, D : 2 * D].astype(bf16)
    values_self = (joint_proj[:, 2 * D :] + vector[:, 1]).astype(bf16)
    mixed_self, totals_self = attend_forward(queries, keys_self, values_self, block_mask, True)
    branch_one = matmul(mixed_self, wide_full[:, 3 * D : 4 * D]) + vector[:, 2]
    normed_one, unit_one, scale_one = norm_forward(
        tokens.astype(f32) + branch_one, vector[:, 11], vector[:, 14]
    )
    normed_low = normed_one.astype(bf16)
    cross_queries = (matmul(normed_low, wide_full[:, 4 * D : 5 * D]) + vector[:, 3]).astype(bf16)
    enc_proj = matmul(encoder_states, wide_full[:, 5 * D : 7 * D])
    cross_keys = enc_proj[:, :D].astype(bf16)
    cross_values = (enc_proj[:, D:] + vector[:, 4]).astype(bf16)
    mixed_cross, totals_cross = attend_forward(
        cross_queries, cross_keys, cross_values, block_mask, False
    )
    output, grad_two, grad_cross_mix, term_in, term_narrow, term_co, sums = center(
        mixed_cross, normed_one, cotangent, wide_full, narrow_full, vec_rows, factor, shards
    )
    grad_cq, grad_ck, grad_cv = attend_backward(
        cross_queries, cross_keys, cross_values, block_mask, False, mixed_cross, totals_cross, grad_cross_mix
    )

    def split(term):
        return term.reshape(shards, -1, D)

    def units(*pairs):
        return jnp.concatenate(
            [split((matmul_left(left, right) * factor).astype(bf16)) for left, right in pairs], 1
        )

    terms = [term_in, split(term_narrow)]
    terms.append(units((normed_low, grad_cq), (encoder_states, grad_ck)))
    terms.append(jnp.concatenate([units((encoder_states, grad_cv)), split(term_co)], 1))
    enc_grad = (
        matmul_right(grad_ck, wide_full[:, 5 * D : 6 * D]) + matmul_right(grad_cv, wide_full[:, 6 * D : 7 * D])
    ).astype(bf16)
    grad_one, gain_one, shift_one = norm_backward(
        grad_two + matmul_right(grad_cq, wide_full[:, 4 * D : 5 * D]), unit_one, scale_one, vector[:, 11]
    )
    grad_self = grad_one.astype(bf16)
    grad_self_mix = matmul_right(grad_self, wide_full[:, 3 * D : 4 * D]).astype(bf16)
    grad_q, grad_k, grad_v = attend_backward(
        queries, keys_self, values_self, block_mask, True, mixed_self, totals_self, grad_self_mix
    )
    terms.append(units((tokens, grad_q), (tokens, grad_k)))
    terms.append(units((tokens, grad_v), (mixed_self, grad_self)))
    in_grad = (
        grad_one
        + matmul_right(grad_q, wide_full[:, :D])
        + matmul_right(grad_k, wide_full[:, D : 2 * D])
        + matmul_right(grad_v, wide_full[:, 2 * D : 3 * D])
    ).astype(bf16)
    fresh = jnp.zeros((24, D), f32)
    for row, value in (
        (0, column_sum(grad_q)),
        (1, column_sum(grad_v)),
        (2, column_sum(grad_self)),
        (3, column_sum(grad_cq)),
        (4, column_sum(grad_cv)),
        (11, gain_one),
        (14, shift_one),
    ):
        fresh = fresh.at[row].set(value)
    term_vec = (sums + fresh) * factor
    term_vec = term_vec.reshape(24, shards, -1).transpose(1, 0, 2)
    total, vec_sum = all_summed(terms, term_vec, replicas, shards)
    vec_grad = vec_sum[: vec_master.shape[1]].T
    (
        wide_grad, wide_new, wide_first_new, wide_second_new, wide_copy,
        narrow_grad, narrow_new, narrow_first_new, narrow_second_new, narrow_copy,
    ) = adam_all(
        total, (wide_master, wide_first, wide_second), (narrow_master, narrow_first, narrow_second)
    )
    vec_new, vec_first_new, vec_second_new = adam_update(
        vec_master, vec_first, vec_second, vec_grad, 0.0, vec_rate
    )
    return (
        output,
        in_grad,
        enc_grad,
        wide_grad,
        narrow_grad,
        vec_grad,
        wide_new,
        narrow_new,
        vec_new,
        wide_first_new,
        narrow_first_new,
        vec_first_new,
        wide_second_new,
        narrow_second_new,
        vec_second_new,
        wide_copy,
        narrow_copy,
        vec_new.astype(bf16),
    )


def all_summed(terms, small, replicas, shards):
    lanes = replicas // 4
    if shards == 2 and replicas % 4 == 0 and all(t.shape[1] % (64 * lanes) == 0 for t in terms):
        return reduce_all(terms, small, lanes)

    def summed(term):
        return lax.psum(lax.psum_scatter(term, "shard", scatter_dimension=0), "rep")

    return jnp.concatenate([summed(term) for term in terms], 0), summed(small)


def solution(mesh):
    in_specs = (
        P(("rep", "shard"), None),
        P(("rep", "shard"), None),
        P(("rep", "shard"), None),
        P(("rep", "shard"), None, None),
        P("shard", None),
        P("shard", None),
        P("shard", None),
        P("shard", None),
        P("shard", None),
        P("shard", None),
        P("shard", None),
        P("shard", None),
        P("shard", None),
    )
    out_specs = (
        P(("rep", "shard"), None),
        P(("rep", "shard"), None),
        P(("rep", "shard"), None),
        P("shard", None),
        P("shard", None),
        P("shard", None),
        P("shard", None),
        P("shard", None),
        P("shard", None),
        P("shard", None),
        P("shard", None),
        P("shard", None),
        P("shard", None),
        P("shard", None),
        P("shard", None),
        P("shard", None),
        P("shard", None),
        P("shard", None),
    )
    return jax.shard_map(
        on_device, mesh=mesh, in_specs=in_specs, out_specs=out_specs, check_vma=False
    )
```

```python
from functools import partial
import math

import jax
import jax.numpy as jnp
from jax import lax
from jax.experimental import pallas as pl
from jax.experimental.pallas import tpu as pltpu
from jax.sharding import PartitionSpec as P

D = 768
H = 12
HD = 64
FF = 3072
LEN = 1024
BLK = 256
STEP = 4


eps_norm = 1e-05
eps_adam = 1e-08
beta_one = 0.5
beta_two = 0.5
learn_rate = 0.03
vec_rate = 0.25
weight_decay = 0.1
masked_score = -1e30
FACTOR = HD ** (-0.5)
SCALE2 = FACTOR / math.log(2.0)


CROSS_TABLE = {
    (0, 1): ((0, 0), (1, 0), (2, 0), (3, 0)),
    (0, 7): ((0, 1), (1, 1), (2, 1), (3, 1)),
    (1, 7): ((0, 2), (1, 2), (2, 2), (3, 2)),
    (1, 13): ((4, 0), (5, 0), (6, 0), (7, 0)),
    (2, 7): ((0, 3), (1, 3), (2, 3), (3, 3), (4, 1), (5, 1), (6, 1), (7, 1)),
    (3, 7): ((0, 4), (1, 4), (2, 4), (3, 4), (4, 2), (5, 2), (6, 2), (7, 2)),
    (4, 7): ((0, 5), (1, 5), (2, 5), (3, 5), (4, 3), (5, 3), (6, 3), (7, 3)),
    (5, 7): ((0, 6), (1, 6), (2, 6), (3, 6), (4, 4), (5, 4), (6, 4), (7, 4)),
    (5, 13): ((0, 7), (1, 7), (2, 7), (3, 7), (0, 8), (1, 8), (2, 8), (3, 8)),
}


SELF_TABLE = {
    (0, 1): ((0, 0), (1, 0), (2, 0), (3, 0)),
    (0, 5): ((2, 1), (3, 1)),
    (1, 3): ((0, 1), (1, 1)),
    (2, 3): ((0, 2), (1, 2), (2, 2), (3, 2)),
    (3, 5): ((2, 3), (3, 3)),
    (4, 3): ((0, 3), (1, 3)),
    (4, 8): ((0, 4), (1, 4), (2, 4), (3, 4)),
}


TAIL_ORDER = (
    (10, 0), (0, 0), (1, 0), (2, 0), (3, 0), (4, 0), (5, 0), (4, 1),
    (5, 1), (4, 2), (10, 1), (5, 2), (6, 0), (7, 0), (0, 1), (1, 1),
    (2, 1), (3, 1), (6, 1), (7, 1), (10, 2), (4, 3), (5, 3), (0, 2),
    (1, 2), (2, 2), (3, 2), (8, 0), (9, 0), (4, 4), (10, 3), (5, 4),
    (8, 1), (9, 1), (6, 2), (7, 2), (4, 5), (5, 5), (6, 3), (7, 3),
    (10, 4), (0, 3), (1, 3), (2, 3), (3, 3), (4, 6), (5, 6), (8, 2),
    (9, 2), (0, 4), (1, 4), (2, 4), (3, 4), (6, 4), (7, 4), (8, 3),
    (9, 3), (4, 7), (5, 7), (4, 8), (5, 8), (6, 5), (7, 5), (8, 4),
    (9, 4), (6, 6), (7, 6), (8, 5), (9, 5), (6, 7), (7, 7), (6, 8),
    (7, 8), (8, 6), (9, 6), (8, 7), (9, 7), (8, 8), (9, 8),
)


def head_masks(rows):
    first = lax.broadcasted_iota(jnp.int32, (rows, 128), 1) < HD
    return (first, jnp.logical_not(first))


def keep(mask, value):
    return jnp.where(mask, value, jnp.zeros((), value.dtype))


def rows_dot(left, right):
    return jnp.dot(left, right, preferred_element_type=jnp.float32)


def rows_dot_t(left, right):
    return lax.dot_general(
        left, right, (((1,), (1,)), ((), ())), preferred_element_type=jnp.float32
    )


def forward_kernel(causal, mask_ref, q_ref, k_ref, v_ref, o_ref, lse_ref, qm_ref, vt_ref, acc_ref, sum_ref, top_ref):
    rows, keys = q_ref.shape[0], k_ref.shape[0]
    tile = BLK
    seq = pl.program_id(0)
    queries = q_ref[...]
    for head, mask in enumerate(head_masks(rows)):
        qm_ref[head] = keep(mask, queries)
    vt_ref[...] = v_ref[...].T
    if causal:
        below = lax.broadcasted_iota(jnp.int32, (BLK, BLK), 0) <= lax.broadcasted_iota(
            jnp.int32, (BLK, BLK), 1
        )

    def start_of(j):
        return j * tile if causal else 0

    def scores_of(j, head):
        begin = start_of(j)
        scores = rows_dot_t(k_ref[j * tile : (j + 1) * tile, :], qm_ref[head, begin:, :]) * SCALE2
        if causal:
            pieces = [jnp.where(below, scores[:, :BLK], masked_score)]
            for i in range(j + 1, rows // BLK):
                off = jnp.where(mask_ref[seq, i, j] > 0, 0.0, masked_score)
                pieces.append(scores[:, (i - j) * BLK : (i - j + 1) * BLK] + off)
            scores = jnp.concatenate(pieces, axis=1)
        return scores

    def add_tile(j, head, scores, shift):
        begin = start_of(j)
        if shift is not None:
            scores = scores - shift[:, begin:]
        probs = jnp.exp2(scores)
        total = jnp.sum(probs, axis=0, keepdims=True)
        mixed = rows_dot(
            vt_ref[head * HD : (head + 1) * HD, j * tile : (j + 1) * tile], probs.astype(jnp.bfloat16)
        )
        if j == 0:
            sum_ref[head : head + 1, :] = total
            acc_ref[head] = mixed
        else:
            sum_ref[head : head + 1, begin:] += total
            acc_ref[head, :, begin:] += mixed

    def finish(shifts):
        both = []
        for head in range(2):
            total = sum_ref[head : head + 1, :]
            lse = jnp.log2(total)
            if shifts is not None:
                lse = lse + shifts[head]
            lse_ref[0, 0, head : head + 1, :] = lse
            both.append(acc_ref[head] * (1.0 / total))
        o_ref[...] = jnp.concatenate(both, axis=0).T.astype(jnp.bfloat16)

    lse_ref[...] = jnp.zeros_like(lse_ref)
    waiting = []
    for j in range(keys // tile):
        for head in range(2):
            waiting.append((j, head, scores_of(j, head)))
            if len(waiting) > 1:
                add_tile(*waiting.pop(0), None)
    while waiting:
        add_tile(*waiting.pop(0), None)
    finish(None)
    sums = sum_ref[...]
    usable = jnp.min(jnp.where((sums > 1e-25) & (sums < 1e30), 1, 0))

    @pl.when(usable == 0)
    def _():
        for head in range(2):
            for j in range(keys // tile):
                peak = jnp.max(scores_of(j, head), axis=0, keepdims=True)
                begin = start_of(j)
                if j == 0:
                    top_ref[head : head + 1, :] = peak
                else:
                    top_ref[head : head + 1, begin:] = jnp.maximum(
                        top_ref[head : head + 1, begin:], peak
                    )
        shifts = [top_ref[0:1, :], top_ref[1:2, :]]
        for head in range(2):
            for j in range(keys // tile):
                add_tile(j, head, scores_of(j, head), shifts[head])
        finish(shifts)


def attend_forward(queries, keys_in, values_in, block_table, causal):
    seqs = block_table.shape[0]
    rows, keys = queries.shape[0] // seqs, keys_in.shape[0] // seqs
    spec_q = pl.BlockSpec((rows, 128), lambda s, i: (s, i))
    spec_k = pl.BlockSpec((keys, 128), lambda s, i: (s, i))
    spec_l = pl.BlockSpec((1, 1, 8, rows), lambda s, i: (s, i, 0, 0))
    area = rows * keys * H * HD * seqs
    return pl.pallas_call(
        partial(forward_kernel, causal),
        grid=(seqs, D // 128),
        in_specs=[pl.BlockSpec(memory_space=pltpu.SMEM), spec_q, spec_k, spec_k],
        out_specs=[spec_q, spec_l],
        scratch_shapes=[
            pltpu.VMEM((2, rows, 128), jnp.bfloat16),
            pltpu.VMEM((128, keys), jnp.bfloat16),
            pltpu.VMEM((2, HD, rows), jnp.float32),
            pltpu.VMEM((2, rows), jnp.float32),
            pltpu.VMEM((2, rows), jnp.float32),
        ],
        out_shape=[
            jax.ShapeDtypeStruct(queries.shape, jnp.bfloat16),
            jax.ShapeDtypeStruct((seqs, D // 128, 8, rows), jnp.float32),
        ],
        compiler_params=pltpu.CompilerParams(vmem_limit_bytes=48 << 20),
        cost_estimate=pl.CostEstimate(
            flops=(8 if causal else 16) * area, bytes_accessed=4 * queries.size, transcendentals=0
        ),
    )(block_table, queries, keys_in, values_in)


ROWS = 256


def gelu_pair(x):
    magnitude = jnp.abs(x)
    bell = jnp.exp2((x * x) * (-0.5 / math.log(2.0)))
    t = 1.0 / (1.0 + (0.3275911 * math.sqrt(0.5)) * magnitude)
    poly = t * (0.127414796 + t * (-0.142248368 + t * (0.7107068705 + t * (-0.7265760135 + t * 0.5307027145))))
    tail = poly * bell
    phi_sum = jnp.where(x >= 0.0, 1.0 - tail, tail)
    return x * phi_sum, phi_sum + x * (bell * (1.0 / math.sqrt(2.0 * math.pi)))


def unit_rows(resid):
    average = jnp.mean(resid, axis=-1, keepdims=True)
    centred = resid - average
    inverse = lax.rsqrt(jnp.mean(centred * centred, axis=-1, keepdims=True) + eps_norm)
    return centred * inverse, inverse


def back_rows(upstream, unit, inverse, gain):
    scaled = upstream * gain
    centred = scaled - jnp.mean(scaled, axis=-1, keepdims=True)
    return inverse * (centred - unit * jnp.mean(scaled * unit, axis=-1, keepdims=True))


def column_dot(left, right):
    return lax.dot_general(left, right, (((0,), (0,)), ((), ())), preferred_element_type=jnp.float32)


def row_total(value):
    return jnp.sum(value, axis=0, keepdims=True)


def center_kernel(
    factor, mix_ref, one_ref, cot_ref, co_ref, win_ref, wout_ref, vec_ref,
    out_ref, two_ref, gmix_ref, tw_ref, tn_ref, tc_ref, sums_ref,
    low_ref, unit_ref, inv_ref, res_ref, act_ref, slope_ref, acc_ref, gffn_ref, bh_ref, gcross_ref,
):
    step = pl.program_id(0)
    rows = mix_ref.shape[0]
    blocks = rows // ROWS

    def vec(i):
        return vec_ref[i : i + 1, :]

    def each(body):
        def run(r, carry):
            body(pl.ds(pl.multiple_of(r * ROWS, ROWS), ROWS))
            return carry

        lax.fori_loop(0, blocks, run, 0)

    @pl.when(step == 0)
    def _():
        sums_ref[...] = jnp.zeros_like(sums_ref)

        def body(at):
            resid = one_ref[at, :] + rows_dot(mix_ref[at, :], co_ref[...]) + vec(5)
            unit, inverse = unit_rows(resid)
            unit_ref[at, :] = unit
            inv_ref[at, :] = jnp.broadcast_to(inverse, (ROWS, 128))
            normed = unit * vec(12) + vec(15)
            res_ref[at, :] = normed + vec(10)
            low_ref[at, :] = normed.astype(jnp.bfloat16)

        each(body)

    @pl.when(step < 4)
    def _():
        bias = vec_ref[pl.ds(6 + step, 1), :]

        def body(at):
            hidden = rows_dot(low_ref[at, :], win_ref[...]) + bias
            value, slope = gelu_pair(hidden)
            value = value.astype(jnp.bfloat16)
            act_ref[step, at, :] = value
            slope_ref[step, at, :] = slope.astype(jnp.bfloat16)
            res_ref[at, :] += rows_dot(value, wout_ref[...])

        each(body)

    @pl.when(step == 3)
    def _():
        def body(at):
            unit, inverse = unit_rows(res_ref[at, :])
            out_ref[at, :] = (unit * vec(13) + vec(16)).astype(jnp.bfloat16)
            upstream = cot_ref[at, :].astype(jnp.float32)
            grad = back_rows(upstream, unit, inverse, vec(13))
            acc_ref[at, :] = grad
            low = grad.astype(jnp.bfloat16)
            gffn_ref[at, :] = low
            sums_ref[13:14, :] += row_total(upstream * unit)
            sums_ref[16:17, :] += row_total(upstream)
            sums_ref[10:11, :] += row_total(low.astype(jnp.float32))

        each(body)

    @pl.when(step >= 4)
    def _():
        c = step - 4

        def body(at):
            grad = rows_dot_t(gffn_ref[at, :], wout_ref[...]) * slope_ref[c, at, :].astype(jnp.float32)
            low = grad.astype(jnp.bfloat16)
            bh_ref[at, :] = low
            sums_ref[pl.ds(step + 2, 1), :] += row_total(low.astype(jnp.float32))
            acc_ref[at, :] += rows_dot_t(low, win_ref[...])

        each(body)
        tn_ref[...] = (column_dot(act_ref[c], gffn_ref[...]) * factor).astype(jnp.bfloat16)
        rows_each = tw_ref.shape[1]
        for s in range(tw_ref.shape[0]):
            cols = slice(s * rows_each, (s + 1) * rows_each)
            tw_ref[s] = (column_dot(low_ref[:, cols], bh_ref[...]) * factor).astype(jnp.bfloat16)

    @pl.when(step == 7)
    def _():
        def body(at):
            upstream = acc_ref[at, :]
            unit = unit_ref[at, :]
            inverse = inv_ref[at, 0:1]
            grad = back_rows(upstream, unit, inverse, vec(12))
            two_ref[at, :] = grad
            low = grad.astype(jnp.bfloat16)
            gcross_ref[at, :] = low
            gmix_ref[at, :] = rows_dot_t(low, co_ref[...]).astype(jnp.bfloat16)
            sums_ref[12:13, :] += row_total(upstream * unit)
            sums_ref[15:16, :] += row_total(upstream)
            sums_ref[5:6, :] += row_total(low.astype(jnp.float32))

        each(body)
        tc_ref[...] = (column_dot(mix_ref[...], gcross_ref[...]) * factor).astype(jnp.bfloat16)


def center(mixed, one, cotangent, wide_full, narrow_full, vec_rows, factor, shards):
    rows = mixed.shape[0]
    whole = pl.BlockSpec((rows, D), lambda i: (0, 0))
    rows_each = D // shards
    bf16, f32 = jnp.bfloat16, jnp.float32
    return pl.pallas_call(
        partial(center_kernel, factor),
        grid=(8,),
        in_specs=[
            whole,
            whole,
            whole,
            pl.BlockSpec((D, D), lambda i: (0, 7)),
            pl.BlockSpec((D, D), lambda i: (0, 8 + i % 4)),
            pl.BlockSpec((D, D), lambda i: (i % 4, 0)),
            pl.BlockSpec(vec_rows.shape, lambda i: (0, 0)),
        ],
        out_specs=[
            whole,
            whole,
            whole,
            pl.BlockSpec((shards, rows_each, D), lambda i: (0, jnp.maximum(i - 4, 0), 0)),
            pl.BlockSpec((D, D), lambda i: (jnp.maximum(i - 4, 0), 0)),
            pl.BlockSpec((D, D), lambda i: (0, 0)),
            pl.BlockSpec((24, D), lambda i: (0, 0)),
        ],
        out_shape=[
            jax.ShapeDtypeStruct((rows, D), bf16),
            jax.ShapeDtypeStruct((rows, D), f32),
            jax.ShapeDtypeStruct((rows, D), bf16),
            jax.ShapeDtypeStruct((shards, 4 * rows_each, D), bf16),
            jax.ShapeDtypeStruct((FF, D), bf16),
            jax.ShapeDtypeStruct((D, D), bf16),
            jax.ShapeDtypeStruct((24, D), f32),
        ],
        scratch_shapes=[
            pltpu.VMEM((rows, D), bf16),
            pltpu.VMEM((rows, D), f32),
            pltpu.VMEM((rows, 128), f32),
            pltpu.VMEM((rows, D), f32),
            pltpu.VMEM((4, rows, D), bf16),
            pltpu.VMEM((4, rows, D), bf16),
            pltpu.VMEM((rows, D), f32),
            pltpu.VMEM((rows, D), bf16),
            pltpu.VMEM((rows, D), bf16),
            pltpu.VMEM((rows, D), bf16),
        ],
        compiler_params=pltpu.CompilerParams(vmem_limit_bytes=58 << 20),
        cost_estimate=pl.CostEstimate(flops=54 * rows * D * D, bytes_accessed=30 << 20, transcendentals=0),
    )(mixed, one, cotangent, wide_full, wide_full, narrow_full, vec_rows)


MESH_ID = pl.DeviceIdType.MESH
UNIT = 384
HALF = 384


def peers_of(lanes):
    rep, shard = lax.axis_index("rep"), lax.axis_index("shard")
    x, y, z = rep % 2, (rep // 2) % 2, rep // 4
    base = rep - z * 4
    others = [(base + 4 * ((z + k) % lanes), shard) for k in range(1, lanes)]
    first = rep + 1 - 2 * x
    second = rep + 2 - 4 * y
    return rep, shard, x, y, z, (rep, 1 - shard), (first, shard), (second, shard), others


def enter_barrier(lanes):
    _, _, _, _, _, sibling, first, second, others = peers_of(lanes)
    barrier = pltpu.get_barrier_semaphore()
    for peer in [sibling, first, second] + others:
        pl.semaphore_signal(barrier, inc=1, device_id=peer, device_id_type=MESH_ID)
    pl.semaphore_wait(barrier, 2 + lanes)


def aligned(value, by=16):
    return pl.multiple_of(value, by)


def remote_copy(sems, index, source, target, peer):
    return pltpu.make_async_remote_copy(
        src_ref=source,
        dst_ref=target,
        send_sem=sems[0].at[index],
        recv_sem=sems[1].at[index],
        device_id=peer,
        device_id_type=MESH_ID,
    )


def unit_scratch(mode, lanes):
    bf16 = jnp.bfloat16
    block = UNIT // (2 * lanes)
    shapes = [pltpu.VMEM((UNIT, D), bf16), pltpu.VMEM((block, HALF), bf16)]
    if mode != "gather":
        shapes += [
            pltpu.VMEM((UNIT, D), bf16),
            pltpu.VMEM((UNIT, HALF), bf16),
            pltpu.VMEM((UNIT // 2, HALF), bf16),
            pltpu.VMEM((lanes, block, HALF), bf16),
        ]
    return shapes + [
        pltpu.SemaphoreType.DMA((5 + 2 * lanes,)),
        pltpu.SemaphoreType.DMA((5 + 2 * lanes,)),
        pltpu.SemaphoreType.DMA((3,)),
    ]


def unit_places(x_first, lanes):
    rep, shard, x, y, z, sibling, peer_x, peer_y, others = peers_of(lanes)
    here_a, here_b = (x, y) if x_first else (y, x)
    peer_a, peer_b = (peer_x, peer_y) if x_first else (peer_y, peer_x)
    return shard, z, here_a, here_b, sibling, peer_a, peer_b, others


def scatter_steps(term, row, scratch, x_first, lanes, block_out):
    got, block_ref, acc, got_a, got_b, got_z = scratch[:6]
    sems, local_sem = scratch[-3:-1], scratch[-1]
    shard, z, here_a, here_b, sibling, peer_a, peer_b, others = unit_places(x_first, lanes)
    half_rows, block = UNIT // 2, UNIT // (2 * lanes)
    mine_cols = pl.ds(aligned(here_a * HALF, 128), HALF)
    their_cols = pl.ds(aligned((1 - here_a) * HALF, 128), HALF)
    mine_b = aligned(here_b * half_rows)
    core = remote_copy(sems, 0, term.at[1 - shard, pl.ds(row, UNIT)], got, sibling)
    load = pltpu.make_async_copy(term.at[shard, pl.ds(row, UNIT)], acc, local_sem.at[0])
    to_a = remote_copy(sems, 1, acc.at[:, their_cols], got_a, peer_a)
    to_b = remote_copy(
        sems, 2, acc.at[pl.ds(aligned((1 - here_b) * half_rows), half_rows), mine_cols], got_b, peer_b
    )
    to_z = [
        remote_copy(
            sems, 5 + k, acc.at[pl.ds(aligned(mine_b + ((z + k + 1) % lanes) * block), block), mine_cols],
            got_z.at[z], peer,
        )
        for k, peer in enumerate(others)
    ]
    f32, bf16 = jnp.float32, jnp.bfloat16

    def start():
        core.start()
        load.start()

    def step_a():
        load.wait()
        core.wait()

        def body(i, carry):
            at = pl.ds(aligned(i * block), block)
            acc[at, :] = (acc[at, :].astype(f32) + got[at, :].astype(f32)).astype(bf16)
            return carry

        lax.fori_loop(0, UNIT // block, body, 0)
        to_a.start()

    def step_b():
        to_a.wait()

        def body(i, carry):
            at = pl.ds(aligned(i * block), block)
            acc[at, mine_cols] = (acc[at, mine_cols].astype(f32) + got_a[at, :].astype(f32)).astype(bf16)
            return carry

        lax.fori_loop(0, UNIT // block, body, 0)
        to_b.start()

    def step_z():
        to_b.wait()

        def body(i, carry):
            at = pl.ds(aligned(mine_b + i * block), block)
            other = got_b[pl.ds(aligned(i * block), block), :].astype(f32)
            acc[at, mine_cols] = (acc[at, mine_cols].astype(f32) + other).astype(bf16)
            return carry

        lax.fori_loop(0, half_rows // block, body, 0)
        for copy in to_z:
            copy.start()

    def step_own():
        for copy in to_z:
            copy.wait()
        total = acc[pl.ds(aligned(mine_b + z * block), block), mine_cols].astype(f32)
        for k in range(1, lanes):
            total = total + got_z[(z + k) % lanes].astype(f32)
        block_ref[...] = total.astype(bf16)
        if block_out is not None:
            block_out[...] = total.astype(bf16)

    return [start, step_a, step_b, step_z, step_own]


def gather_steps(block_in, sum_out, scratch, x_first, lanes):
    full, block_ref = scratch[:2]
    sems, local_sem = scratch[-3:-1], scratch[-1]
    shard, z, here_a, here_b, sibling, peer_a, peer_b, others = unit_places(x_first, lanes)
    half_rows, block = UNIT // 2, UNIT // (2 * lanes)
    mine_cols = pl.ds(aligned(here_a * HALF, 128), HALF)
    mine_b = aligned(here_b * half_rows)
    mine_z = full.at[pl.ds(aligned(mine_b + z * block), block), mine_cols]
    mine_half = full.at[pl.ds(mine_b, half_rows), mine_cols]
    mine_all = full.at[:, mine_cols]
    all_z = [remote_copy(sems, 5 + lanes + k, mine_z, mine_z, peer) for k, peer in enumerate(others)]
    all_b = remote_copy(sems, 3, mine_half, mine_half, peer_b)
    all_a = remote_copy(sems, 4, mine_all, mine_all, peer_a)
    store = pltpu.make_async_copy(full, sum_out, local_sem.at[1])

    def start():
        source = block_ref if block_in is None else block_in
        full[pl.ds(aligned(mine_b + z * block), block), mine_cols] = source[...]
        for copy in all_z:
            copy.start()

    def step_b():
        for copy in all_z:
            copy.wait()
        all_b.start()

    def step_a():
        all_b.wait()
        all_a.start()

    def step_store():
        all_a.wait()
        store.start()

    return [start, step_b, step_a, step_store, store.wait]


def joined_steps(scatter, gather):
    own, begin = scatter[-1], gather[0]

    def both():
        own()
        begin()

    return scatter[:-1] + [both] + gather[1:]


def small_scratch(shape, lanes):
    return [
        pltpu.VMEM((3,) + shape, jnp.float32),
        pltpu.VMEM((3,) + shape, jnp.float32),
        pltpu.VMEM((lanes,) + shape, jnp.float32),
        pltpu.SemaphoreType.DMA((3 + lanes,)),
        pltpu.SemaphoreType.DMA((3 + lanes,)),
    ]


def small_steps(term_ref, sum_ref, scratch, lanes):
    held, got, got_z = scratch[:3]
    sems = scratch[3:]
    rep, shard, x, y, z, sibling, peer_x, peer_y, others = peers_of(lanes)
    core = remote_copy(sems, 0, term_ref.at[1 - shard], got.at[0], sibling)
    to_x = remote_copy(sems, 1, held.at[0], got.at[1], peer_x)
    to_y = remote_copy(sems, 2, held.at[1], got.at[2], peer_y)
    to_z = [remote_copy(sems, 3 + k, held.at[2], got_z.at[z], peer) for k, peer in enumerate(others)]

    def step_x():
        core.wait()
        held[0] = term_ref[shard] + got[0]
        to_x.start()

    def step_y():
        to_x.wait()
        held[1] = held[0] + got[1]
        to_y.start()

    def step_z():
        to_y.wait()
        held[2] = held[1] + got[2]
        got_z[z] = held[2]
        for copy in to_z:
            copy.start()

    def step_end():
        for copy in to_z:
            copy.wait()
        total = got_z[0]
        for k in range(1, lanes):
            total = total + got_z[k]
        sum_ref[...] = total

    return [core.start, step_x, step_y, step_z, step_end]


class Traffic:
    def __init__(self, modes, lanes, terms=(), places=(), blocks=None, small=None):
        self.modes, self.lanes, self.terms, self.places = modes, lanes, list(terms), list(places)
        self.blocks, self.small = blocks, small
        self.n_scatter = sum(mode == "scatter" for mode in modes)
        self.n_sum = len(modes) - self.n_scatter

    def operands(self):
        return self.terms + ([self.blocks] if self.blocks is not None else []) + (
            [self.small] if self.small is not None else []
        )

    def in_specs(self):
        vmem = pl.BlockSpec(memory_space=pltpu.VMEM)
        return [pl.BlockSpec(memory_space=pl.ANY)] * len(self.terms) + [vmem] * (
            (self.blocks is not None) + (self.small is not None)
        )

    def out_specs(self):
        specs = []
        if self.n_scatter:
            specs.append(pl.BlockSpec(memory_space=pltpu.VMEM))
        if self.n_sum:
            specs.append(pl.BlockSpec(memory_space=pl.ANY))
        if self.small is not None:
            specs.append(pl.BlockSpec(memory_space=pltpu.VMEM))
        return specs

    def out_shape(self):
        shapes = []
        if self.n_scatter:
            shapes.append(
                jax.ShapeDtypeStruct((self.n_scatter, UNIT // (2 * self.lanes), HALF), jnp.bfloat16)
            )
        if self.n_sum:
            shapes.append(jax.ShapeDtypeStruct((self.n_sum * UNIT, D), jnp.bfloat16))
        if self.small is not None:
            shapes.append(jax.ShapeDtypeStruct(self.small.shape[1:], jnp.float32))
        return shapes

    def scratch(self):
        shapes = []
        for mode in self.modes:
            shapes += unit_scratch(mode, self.lanes)
        if self.small is not None:
            shapes += small_scratch(self.small.shape[1:], self.lanes)
        return shapes

    def steps(self, ins, outs, scratch):
        ins, outs, scratch = list(ins), list(outs), list(scratch)
        terms = [ins.pop(0) for _ in self.terms]
        blocks = ins.pop(0) if self.blocks is not None else None
        small = ins.pop(0) if self.small is not None else None
        block_out = outs.pop(0) if self.n_scatter else None
        sum_out = outs.pop(0) if self.n_sum else None
        small_out = outs.pop(0) if small is not None else None
        found = []
        n_block = n_sum = n_in = n_place = 0
        for i, mode in enumerate(self.modes):
            count = len(unit_scratch(mode, self.lanes))
            mine, scratch = scratch[:count], scratch[count:]
            x_first = None
            if mode != "gather":
                which, row, x_first = self.places[n_place]
                target = block_out.at[n_block] if mode == "scatter" else None
                scatter = scatter_steps(terms[which], row, mine, x_first, self.lanes, target)
                n_block += mode == "scatter"
            else:
                x_first = self.places[n_place]
            n_place += 1
            if mode != "scatter":
                source = None
                if mode == "gather":
                    source = blocks.at[n_in]
                    n_in += 1
                gather = gather_steps(
                    source, sum_out.at[pl.ds(n_sum * UNIT, UNIT)], mine, x_first, self.lanes
                )
                n_sum += 1
            found.append(
                scatter if mode == "scatter" else gather if mode == "gather" else joined_steps(scatter, gather)
            )
        if small is not None:
            found.append(small_steps(small, small_out, scratch, self.lanes))
        return found


def traffic_kernel(traffic, order, *refs):
    n_in, n_out = len(traffic.in_specs()), len(traffic.out_specs())
    steps = traffic.steps(refs[:n_in], refs[n_in : n_in + n_out], refs[n_in + n_out :])
    enter_barrier(traffic.lanes)
    for which, step in order:
        steps[which][step]()


def run_traffic(traffic, order, collective_id):
    return pl.pallas_call(
        partial(traffic_kernel, traffic, order),
        in_specs=traffic.in_specs(),
        out_specs=traffic.out_specs(),
        out_shape=traffic.out_shape(),
        scratch_shapes=traffic.scratch(),
        compiler_params=pltpu.CompilerParams(
            collective_id=collective_id, has_side_effects=True, vmem_limit_bytes=58 << 20
        ),
    )(*traffic.operands())


def backward_kernel(causal, traffic, table, factor, *refs):
    refs = list(refs)
    take = lambda count: [refs.pop(0) for _ in range(count)]
    mask_ref, q_ref, k_ref, v_ref, m_ref, x_ref, lse_ref, left_q_ref, up_ref, wq_ref, wk_ref, wv_ref = take(12)
    if not causal:
        left_k_ref, wo_ref, res_ref, mixo_ref, vec_ref = take(5)
    traffic_in = take(len(traffic.in_specs()) if traffic else 0)
    tq_ref, tk_ref, tv_ref, pair_sums_ref, grad_ref = take(5)
    if not causal:
        encg_ref, gmix_ref, to_ref, norm_sums_ref = take(4)
    traffic_out = take(len(traffic.out_specs()) if traffic else 0)
    qm_ref, mm_ref, qt_ref, mt_ref, col_ref, acc_ref, dkt_ref, dvt_ref, total_ref, up_sem = take(10)
    if not causal:
        total_k_ref, low_ref = take(2)
    bf16, f32 = jnp.bfloat16, jnp.float32
    rows, keys = q_ref.shape[0], k_ref.shape[0]
    pair = pl.program_id(0)
    step, tile = (BLK, BLK) if causal else (2 * BLK, 2 * BLK)
    slot = [0]
    if traffic:
        steps = traffic.steps(traffic_in, traffic_out, refs)

        @pl.when(pair == 0)
        def _():
            enter_barrier(traffic.lanes)

    def hook():
        if traffic:
            for at_pair in range(D // 128):
                todo = table.get((at_pair, slot[0]), ())
                if todo:

                    @pl.when(pair == at_pair)
                    def _():
                        for which, index in todo:
                            steps[which][index]()

        slot[0] += 1

    def each(count, size, body):
        def run(r, carry):
            body(pl.ds(pl.multiple_of(r * size, size), size))
            return carry

        lax.fori_loop(0, count // size, run, 0)

    hook()

    @pl.when(pair == 0)
    def _():
        load = pltpu.make_async_copy(up_ref, total_ref, up_sem)
        load.start()
        load.wait()
        if not causal:
            total_k_ref[...] = jnp.zeros_like(total_k_ref)

    masks = head_masks(rows)
    masks_k = head_masks(tile)
    queries, grads = q_ref[...], m_ref[...]
    qt_ref[...] = queries.T
    mt_ref[...] = grads.T
    product = grads.astype(f32) * x_ref[...].astype(f32)
    lse = lse_ref[0].T
    for head in range(2):
        qm_ref[head] = keep(masks[head], queries)
        mm_ref[head] = keep(masks[head], grads)
        centre = jnp.sum(keep(masks[head], product), axis=1, keepdims=True)
        col_ref[head] = jnp.broadcast_to(centre, (rows, 128))
        col_ref[2 + head] = jnp.broadcast_to(lse[:, head : head + 1], (rows, 128))
    if causal:
        below = lax.broadcasted_iota(jnp.int32, (BLK, BLK), 0) >= lax.broadcasted_iota(
            jnp.int32, (BLK, BLK), 1
        )

    def widen(column):
        return jnp.concatenate([column] * (tile // 128), axis=1)

    def level_of(head, j, begin, end):
        level = col_ref[2 + head, begin:end]
        if not causal:
            return level
        pieces = [level[:BLK]] if begin == j * BLK else []
        for i in range(begin // BLK + len(pieces), end // BLK):
            off = jnp.where(mask_ref[0, i, j] > 0, 0.0, -masked_score)
            pieces.append(level[i * BLK - begin : (i + 1) * BLK - begin] + off)
        return jnp.concatenate(pieces, axis=0) if len(pieces) > 1 else pieces[0]

    for j in range(keys // tile):
        key_rows = slice(j * tile, (j + 1) * tile)
        key, value = k_ref[key_rows, :], v_ref[key_rows, :]
        key_masked = [keep(mask, key) for mask in masks_k]
        total_k, total_v = [None, None], [None, None]
        cuts = (j * tile, rows) if causal else tuple(range(0, rows + 1, step))
        for begin, end in zip(cuts[:-1], cuts[1:]):
            here = slice(begin, end)
            hook()
            for head in range(2):
                scores = rows_dot_t(qm_ref[head, here, :], key)
                prob_grad = rows_dot_t(mm_ref[head, here, :], value)
                scores = scores * SCALE2 - widen(level_of(head, j, begin, end))
                if causal:
                    top = jnp.where(below, scores[:BLK], masked_score)
                    scores = top if end == begin + BLK else jnp.concatenate([top, scores[BLK:]], axis=0)
                probs = jnp.exp2(scores)
                score_grad = (probs * (prob_grad - widen(col_ref[head, here]))).astype(bf16)
                probs = probs.astype(bf16)
                part = slice(head * HD, (head + 1) * HD)
                add_v = rows_dot(mt_ref[part, here], probs)
                add_k = rows_dot(qt_ref[part, here], score_grad)
                total_v[head] = add_v if total_v[head] is None else total_v[head] + add_v
                total_k[head] = add_k if total_k[head] is None else total_k[head] + add_k
                add_q = rows_dot(score_grad, key_masked[head])
                if j == 0 and head == 0:
                    acc_ref[here, :] = add_q
                else:
                    acc_ref[here, :] += add_q
        for head in range(2):
            part = slice(head * HD, (head + 1) * HD)
            dkt_ref[part, key_rows] = (total_k[head] * FACTOR).astype(bf16)
            dvt_ref[part, key_rows] = total_v[head].astype(bf16)
    hook()
    grad_q = (acc_ref[...] * FACTOR).astype(bf16)
    grad_qt = grad_q.T
    pair_sums_ref[0:1, :] = row_total(grad_q.astype(f32))
    pair_sums_ref[1:2, :] = jnp.sum(dvt_ref[...].astype(f32), axis=1, keepdims=True).T

    def put(target, transposed):
        target[...] = (transposed * factor).T.astype(bf16)

    grad_k, grad_v = dkt_ref[...].T, dvt_ref[...].T
    if causal:
        joined = jnp.concatenate([grad_qt, dkt_ref[...], dvt_ref[...]], axis=0)
        found = rows_dot(joined, left_q_ref[...])
        put(tq_ref, found[:128])
        put(tk_ref, found[128:256])
        put(tv_ref, found[256:])
        hook()
        weights = jnp.concatenate([wq_ref[...], wk_ref[...], wv_ref[...]], axis=1)
        total_ref[...] += rows_dot_t(jnp.concatenate([grad_q, grad_k, grad_v], axis=1), weights)
        hook()

        @pl.when(pair == D // 128 - 1)
        def _():
            grad_ref[...] = total_ref[...].astype(bf16)
    else:
        put(tq_ref, rows_dot(grad_qt, left_q_ref[...]))
        total_ref[...] += rows_dot_t(grad_q, wq_ref[...])
        hook()
        found = rows_dot(jnp.concatenate([dkt_ref[...], dvt_ref[...]], axis=0), left_k_ref[...])
        put(tk_ref, found[:128])
        put(tv_ref, found[128:])
        hook()
        weights = jnp.concatenate([wk_ref[...], wv_ref[...]], axis=1)
        total_k_ref[...] += rows_dot_t(jnp.concatenate([grad_k, grad_v], axis=1), weights)
        hook()

        @pl.when(pair == D // 128 - 1)
        def _():
            encg_ref[...] = total_k_ref[...].astype(bf16)
            norm_sums_ref[...] = jnp.zeros_like(norm_sums_ref)

            def body(at):
                unit, inverse = unit_rows(res_ref[at, :])
                upstream = total_ref[at, :]
                grad = back_rows(upstream, unit, inverse, vec_ref[11:12, :])
                grad_ref[at, :] = grad
                low = grad.astype(bf16)
                low_ref[at, :] = low
                gmix_ref[at, :] = rows_dot_t(low, wo_ref[...]).astype(bf16)
                norm_sums_ref[0:1, :] += row_total(upstream * unit)
                norm_sums_ref[1:2, :] += row_total(upstream)
                norm_sums_ref[2:3, :] += row_total(low.astype(f32))

            each(rows, ROWS, body)
            to_ref[...] = (column_dot(mixo_ref[...], low_ref[...]) * factor).astype(bf16)

    hook()


def attend_backward(
    queries, keys_in, values_in, block_table, causal, mixed, lse, mixed_grad, left_q, upstream, wide_full,
    factor, extra, traffic, table, collective_id,
):
    rows, keys = queries.shape[0], keys_in.shape[0]
    bf16, f32 = jnp.bfloat16, jnp.float32
    first = 0 if causal else 4

    def columns(count):
        return pl.BlockSpec((count, 128), lambda i: (0, i))

    def whole(shape):
        return pl.BlockSpec(shape, lambda i: (0,) * len(shape), pipeline_mode=pl.Buffered(1))

    def weight(unit):
        return pl.BlockSpec((D, 128), lambda i: (0, unit * (D // 128) + i))

    spec_q, spec_k = columns(rows), columns(keys)
    in_specs = [pl.BlockSpec(memory_space=pltpu.SMEM), spec_q, spec_k, spec_k, spec_q, spec_q]
    in_specs += [pl.BlockSpec((1, 8, rows), lambda i: (i, 0, 0)), whole((rows, D)), pl.BlockSpec(memory_space=pl.ANY)]
    in_specs += [weight(first), weight(first + 1), weight(first + 2)]
    operands = [block_table, queries, keys_in, values_in, mixed_grad, mixed, lse, left_q, upstream]
    operands += [wide_full] * 3
    shape = jax.ShapeDtypeStruct
    out_specs = [columns(D)] * 3 + [columns(8), whole((rows, D))]
    out_shape = [shape((D, D), bf16)] * 3 + [shape((8, D), f32), shape((rows, D), bf16 if causal else f32)]
    scratch = [
        pltpu.VMEM((2, rows, 128), bf16),
        pltpu.VMEM((2, rows, 128), bf16),
        pltpu.VMEM((128, rows), bf16),
        pltpu.VMEM((128, rows), bf16),
        pltpu.VMEM((4, rows, 128), f32),
        pltpu.VMEM((rows, 128), f32),
        pltpu.VMEM((128, keys), bf16),
        pltpu.VMEM((128, keys), bf16),
        pltpu.VMEM((rows, D), f32),
        pltpu.SemaphoreType.DMA,
    ]
    if not causal:
        states, resid, mixed_self, vec_rows = extra
        in_specs += [whole((keys, D)), pl.BlockSpec((D, D), lambda i: (0, 3), pipeline_mode=pl.Buffered(1)), whole((rows, D)), whole((rows, D))]
        in_specs += [whole(vec_rows.shape)]
        operands += [states, wide_full, resid, mixed_self, vec_rows]
        out_specs += [whole((keys, D)), whole((rows, D)), whole((D, D)), whole((8, D))]
        out_shape += [shape((keys, D), bf16), shape((rows, D), bf16), shape((D, D), bf16), shape((8, D), f32)]
        scratch += [pltpu.VMEM((keys, D), f32), pltpu.VMEM((rows, D), bf16)]
    params = dict(vmem_limit_bytes=62 << 20)
    if traffic:
        in_specs += traffic.in_specs()
        operands += traffic.operands()
        out_specs += traffic.out_specs()
        out_shape += traffic.out_shape()
        scratch += traffic.scratch()
        params.update(collective_id=collective_id, has_side_effects=True)
    return pl.pallas_call(
        partial(backward_kernel, causal, traffic, table, factor),
        grid=(D // 128,),
        in_specs=in_specs,
        out_specs=out_specs,
        out_shape=out_shape,
        scratch_shapes=scratch,
        compiler_params=pltpu.CompilerParams(**params),
        cost_estimate=pl.CostEstimate(
            flops=(20 if causal else 40) * rows * keys * D, bytes_accessed=4 * queries.size, transcendentals=0
        ),
    )(*operands)


def adam_update(master, first, second, gradient, decay_on, rate):
    first_new = beta_one * first + (1.0 - beta_one) * gradient
    second_new = beta_two * second + (1.0 - beta_two) * gradient * gradient
    first_hat = first_new / (1.0 - beta_one**STEP)
    second_hat = second_new / (1.0 - beta_two**STEP)
    master_new = master - rate * (first_hat / (jnp.sqrt(second_hat) + eps_adam) + decay_on * master)
    return (master_new, first_new, second_new)


def wide_column(i):
    late = jnp.where(i < 10, i - 4, jnp.where(i == 10, 7, jnp.where(i == 11, 6, jnp.where(i == 12, 3, i - 13))))
    return jnp.where(i < 4, i + 8, jnp.where(i < 8, 11, late))


def narrow_row(i):
    return jnp.clip(i - 4, 0, 3)


def adam_kernel(in_ref, mid_ref, late_ref, wm, wf, ws, nm, nf, ns, wg, wn, wfn, wsn, wc, ng, nn, nfn, nsn, nc):
    step = pl.program_id(0)
    rows = in_ref.shape[0]

    def update(sum_ref, master, first, second, grad, new, first_new, second_new, copy):
        def body(r, carry):
            at = pl.ds(pl.multiple_of(r * 32, 32), 32)
            gradient = sum_ref[at, :].astype(jnp.float32)
            grad[at, :] = gradient
            value, one, two = adam_update(
                master[at, :], first[at, :], second[at, :], gradient, weight_decay, learn_rate
            )
            new[at, :] = value
            first_new[at, :] = one
            second_new[at, :] = two
            copy[at, :] = value.astype(jnp.bfloat16)
            return carry

        lax.fori_loop(0, rows // 32, body, 0, unroll=True)

    wide_refs = (wm, wf, ws, wg, wn, wfn, wsn, wc)
    narrow_refs = (nm, nf, ns, ng, nn, nfn, nsn, nc)

    @pl.when(step < 4)
    def _():
        update(in_ref, *wide_refs)

    @pl.when((step == 4) | (step == 5))
    def _():
        update(mid_ref, *narrow_refs)

    @pl.when((step == 6) | (step == 7))
    def _():
        update(late_ref, *narrow_refs)

    @pl.when(step >= 8)
    def _():
        update(late_ref, *wide_refs)


def adam_all(sums, wide, narrow):
    rows = wide[0].shape[0]
    spec_w = pl.BlockSpec((rows, D), lambda i: (0, wide_column(i)))
    spec_n = pl.BlockSpec((rows, D), lambda i: (narrow_row(i), 0))
    f32, bf16 = jnp.float32, jnp.bfloat16

    def shapes(like):
        return [jax.ShapeDtypeStruct(like.shape, f32)] * 4 + [jax.ShapeDtypeStruct(like.shape, bf16)]

    return pl.pallas_call(
        adam_kernel,
        grid=(16,),
        in_specs=[
            pl.BlockSpec((rows, D), lambda i: (jnp.minimum(i, 3), 0)),
            pl.BlockSpec((rows, D), lambda i: (jnp.clip(i - 4, 0, 1), 0)),
            pl.BlockSpec((rows, D), lambda i: (jnp.maximum(i - 6, 0), 0)),
        ] + [spec_w] * 3 + [spec_n] * 3,
        out_specs=[spec_w] * 5 + [spec_n] * 5,
        out_shape=shapes(wide[0]) + shapes(narrow[0]),
        compiler_params=pltpu.CompilerParams(vmem_limit_bytes=58 << 20),
    )(*sums, *wide, *narrow)


def matmul(left, right):
    return jnp.dot(left, right, preferred_element_type=jnp.float32)


def matmul_left(left, right):
    return lax.dot_general(
        left, right, (((0,), (0,)), ((), ())), preferred_element_type=jnp.float32
    )


def matmul_right(left, right):
    return lax.dot_general(
        left, right, (((1,), (1,)), ((), ())), preferred_element_type=jnp.float32
    )


def norm_forward(resid, gain, shift):
    average = jnp.mean(resid, axis=-1, keepdims=True)
    centred = resid - average
    inverse = lax.rsqrt(jnp.mean(centred * centred, axis=-1, keepdims=True) + eps_norm)
    normed = centred * inverse
    return normed * gain + shift


def on_device(
    tokens,
    encoder_states,
    cotangent,
    block_mask,
    wide_master,
    narrow_master,
    vec_master,
    wide_first,
    narrow_first,
    vec_first,
    wide_second,
    narrow_second,
    vec_second,
):
    replicas = lax.axis_size("rep")
    shards = lax.axis_size("shard")
    tokens_all = tokens.shape[0] * replicas * shards
    factor = float(tokens_all) ** (-0.5)
    bf16, f32 = jnp.bfloat16, jnp.float32

    def gathered(part):
        return lax.all_gather(part.astype(bf16), "shard", axis=0, tiled=True)

    wide_full = gathered(wide_master)
    narrow_full = gathered(narrow_master)
    vector = gathered(vec_master).astype(f32)
    vec_rows = jnp.pad(vector.T, ((0, 24 - vector.shape[1]), (0, 0)))
    joint_proj = matmul(tokens, wide_full[:, : 3 * D])
    queries = (joint_proj[:, :D] + vector[:, 0]).astype(bf16)
    keys_self = joint_proj[:, D : 2 * D].astype(bf16)
    values_self = (joint_proj[:, 2 * D :] + vector[:, 1]).astype(bf16)
    mixed_self, totals_self = attend_forward(queries, keys_self, values_self, block_mask, True)
    resid_one = tokens.astype(f32) + matmul(mixed_self, wide_full[:, 3 * D : 4 * D]) + vector[:, 2]
    normed_one = norm_forward(resid_one, vector[:, 11], vector[:, 14])
    normed_low = normed_one.astype(bf16)
    cross_queries = (matmul(normed_low, wide_full[:, 4 * D : 5 * D]) + vector[:, 3]).astype(bf16)
    enc_proj = matmul(encoder_states, wide_full[:, 5 * D : 7 * D])
    cross_keys = enc_proj[:, :D].astype(bf16)
    cross_values = (enc_proj[:, D:] + vector[:, 4]).astype(bf16)
    mixed_cross, totals_cross = attend_forward(
        cross_queries, cross_keys, cross_values, block_mask, False
    )
    output, grad_two, grad_cross_mix, term_in, term_narrow, term_co, sums = center(
        mixed_cross, normed_one, cotangent, wide_full, narrow_full, vec_rows, factor, shards
    )

    def split(term):
        return term.reshape(shards, -1, D)

    carried = shards == 2 and replicas % 4 == 0 and UNIT % (32 * (replicas // 4)) == 0
    lanes = replicas // 4
    early = [term_in, split(term_narrow), split(term_co)]
    traffic = None
    if carried:
        places = [(0, UNIT * i, i % 2 == 0) for i in range(4)] + [(1, UNIT * i, i % 2 == 0) for i in range(4)]
        traffic = Traffic(["both"] * 4 + ["scatter"] * 4, lanes, early[:2], places)
    found = attend_backward(
        cross_queries, cross_keys, cross_values, block_mask, False, mixed_cross, totals_cross[0],
        grad_cross_mix, normed_low, grad_two, wide_full, factor,
        (encoder_states, resid_one, mixed_self, vec_rows), traffic, CROSS_TABLE, 1,
    )
    term_cq, term_ck, term_cv, cross_sums, grad_one, enc_grad, grad_self_mix, term_wo, norm_sums = found[:9]
    middle = [split(term) for term in (term_cq, term_ck, term_cv, term_wo)]
    if carried:
        blocks, sum_in = found[9:]
        places = [True, False, (0, 0, True), (1, 0, False)]
        traffic = Traffic(["gather"] * 2 + ["scatter"] * 2, lanes, middle[:2], places, blocks[:2])
    found = attend_backward(
        queries, keys_self, values_self, block_mask, True, mixed_self, totals_self[0],
        grad_self_mix, tokens, grad_one, wide_full, factor, None, traffic, SELF_TABLE, 2,
    )
    late = [split(term) for term in found[:3]]
    self_sums, in_grad = found[3:5]
    term_vec = jnp.concatenate(
        [
            self_sums[0:2],
            norm_sums[2:3],
            cross_sums[0:2],
            sums[5:11],
            norm_sums[0:1],
            sums[12:14],
            norm_sums[1:2],
            sums[15:],
        ],
        0,
    )
    term_vec = (term_vec * factor).reshape(24, shards, -1).transpose(1, 0, 2)
    last = [early[2], middle[2], middle[3]] + late
    if carried:
        blocks_self, sum_mid = found[5:]
        modes = ["gather"] * 4 + ["both"] * 6
        places = [i % 2 == 0 for i in range(4)] + [(i, 0, i % 2 == 0) for i in range(6)]
        traffic = Traffic(modes, lanes, last, places, jnp.concatenate([blocks[2:], blocks_self], 0), term_vec)
        sum_late, vec_sum = run_traffic(traffic, TAIL_ORDER, 0)
        totals = [sum_in, sum_mid, sum_late]
    else:
        narrow_sum = whole_sum(early[1])
        cut = narrow_sum.shape[0] // 2
        rest = [narrow_sum[cut:]] + [whole_sum(term) for term in middle[:2] + last]
        totals = [whole_sum(early[0]), narrow_sum[:cut], jnp.concatenate(rest, 0)]
        vec_sum = lax.psum(lax.psum_scatter(term_vec, "shard", scatter_dimension=0), "rep")
    vec_grad = vec_sum[: vec_master.shape[1]].T
    (
        wide_grad, wide_new, wide_first_new, wide_second_new, wide_copy,
        narrow_grad, narrow_new, narrow_first_new, narrow_second_new, narrow_copy,
    ) = adam_all(
        totals, (wide_master, wide_first, wide_second), (narrow_master, narrow_first, narrow_second)
    )
    vec_new, vec_first_new, vec_second_new = adam_update(
        vec_master, vec_first, vec_second, vec_grad, 0.0, vec_rate
    )
    return (
        output,
        in_grad,
        enc_grad,
        wide_grad,
        narrow_grad,
        vec_grad,
        wide_new,
        narrow_new,
        vec_new,
        wide_first_new,
        narrow_first_new,
        vec_first_new,
        wide_second_new,
        narrow_second_new,
        vec_second_new,
        wide_copy,
        narrow_copy,
        vec_new.astype(bf16),
    )


def whole_sum(term):
    return lax.psum(lax.psum_scatter(term, "shard", scatter_dimension=0), "rep")


def solution(mesh):
    in_specs = (
        P(("rep", "shard"), None),
        P(("rep", "shard"), None),
        P(("rep", "shard"), None),
        P(("rep", "shard"), None, None),
        P("shard", None),
        P("shard", None),
        P("shard", None),
        P("shard", None),
        P("shard", None),
        P("shard", None),
        P("shard", None),
        P("shard", None),
        P("shard", None),
    )
    out_specs = (
        P(("rep", "shard"), None),
        P(("rep", "shard"), None),
        P(("rep", "shard"), None),
        P("shard", None),
        P("shard", None),
        P("shard", None),
        P("shard", None),
        P("shard", None),
        P("shard", None),
        P("shard", None),
        P("shard", None),
        P("shard", None),
        P("shard", None),
        P("shard", None),
        P("shard", None),
        P("shard", None),
        P("shard", None),
        P("shard", None),
    )
    return jax.shard_map(
        on_device, mesh=mesh, in_specs=in_specs, out_specs=out_specs, check_vma=False
    )
```

```python
from functools import partial
import math

import jax
import jax.numpy as jnp
from jax import lax
from jax.experimental import pallas as pl
from jax.experimental.pallas import tpu as pltpu
from jax.sharding import PartitionSpec as P

D = 768
H = 12
HD = 64
FF = 3072
LEN = 1024
BLK = 256
STEP = 4


eps_norm = 1e-05
eps_adam = 1e-08
beta_one = 0.5
beta_two = 0.5
learn_rate = 0.03
vec_rate = 0.25
weight_decay = 0.1
masked_score = -1e30
FACTOR = HD ** (-0.5)
SCALE2 = FACTOR / math.log(2.0)
WIDE_UNITS = 12
ALL_UNITS = 16
N_BOTH = 4
N_SCATTER = 4
N_GATHER = 2
N_MIDDLE = 2


CROSS_TABLE = {
    (0, 0): ((0, 0), (1, 0), (2, 0), (3, 0)),
    (0, 9): ((0, 1), (1, 1), (2, 1), (3, 1)),
    (1, 9): ((0, 2), (1, 2), (2, 2), (3, 2)),
    (2, 0): ((4, 0), (5, 0), (6, 0), (7, 0)),
    (2, 5): ((0, 3), (1, 3), (2, 3), (3, 3)),
    (2, 9): ((4, 1), (5, 1), (6, 1), (7, 1)),
    (3, 5): ((0, 4), (1, 4), (2, 4), (3, 4)),
    (3, 9): ((4, 2), (5, 2), (6, 2), (7, 2)),
    (4, 5): ((0, 5), (1, 5), (2, 5), (3, 5), (4, 3), (5, 3), (6, 3), (7, 3)),
    (5, 0): ((0, 6), (1, 6), (2, 6), (3, 6)),
    (5, 5): ((4, 4), (5, 4), (6, 4), (7, 4)),
    (5, 9): ((0, 7), (1, 7), (2, 7), (3, 7), (0, 8), (1, 8), (2, 8), (3, 8)),
}


SELF_TABLE = {
    (0, 0): ((0, 0), (1, 0), (2, 0), (3, 0)),
    (0, 8): ((2, 1), (3, 1)),
    (1, 3): ((0, 1), (1, 1)),
    (2, 8): ((0, 2), (1, 2), (2, 2), (3, 2)),
    (4, 3): ((2, 3), (3, 3)),
    (4, 8): ((0, 3), (1, 3)),
    (5, 3): ((0, 4), (1, 4)),
    (5, 8): ((2, 4), (3, 4)),
}


TAIL_ORDER = (
    (10, 0), (0, 0), (1, 0), (2, 0), (3, 0), (4, 0), (5, 0), (4, 1),
    (5, 1), (4, 2), (10, 1), (5, 2), (6, 0), (7, 0), (0, 1), (1, 1),
    (2, 1), (3, 1), (6, 1), (7, 1), (10, 2), (4, 3), (5, 3), (0, 2),
    (1, 2), (2, 2), (3, 2), (8, 0), (9, 0), (4, 4), (10, 3), (5, 4),
    (0, 3), (1, 3), (2, 3), (3, 3), (6, 2), (7, 2), (8, 1), (9, 1),
    (10, 4), (4, 5), (5, 5), (6, 3), (7, 3), (8, 2), (9, 2), (4, 6),
    (5, 6), (6, 4), (7, 4), (4, 7), (5, 7), (8, 3), (9, 3), (6, 5),
    (7, 5), (8, 4), (9, 4), (6, 6), (7, 6), (6, 7), (7, 7), (8, 5),
    (9, 5), (8, 6), (9, 6), (8, 7), (9, 7),
)


def head_masks(rows):
    first = lax.broadcasted_iota(jnp.int32, (rows, 128), 1) < HD
    return (first, jnp.logical_not(first))


def keep(mask, value):
    return jnp.where(mask, value, jnp.zeros((), value.dtype))


def rows_dot(left, right):
    return jnp.dot(left, right, preferred_element_type=jnp.float32)


def rows_dot_t(left, right):
    return lax.dot_general(
        left, right, (((1,), (1,)), ((), ())), preferred_element_type=jnp.float32
    )


def forward_kernel(
    causal, mask_ref, left_q_ref, left_k_ref, wq_ref, wk_ref, wv_ref, vec_ref,
    o_ref, lse_ref, q_ref, k_ref, v_ref, qm_ref, vt_ref, acc_ref, sum_ref, top_ref,
):
    rows, keys = q_ref.shape[0], k_ref.shape[0]
    tile = BLK
    bias_q, bias_v = (vec_ref[0:1, :], vec_ref[1:2, :]) if causal else (vec_ref[3:4, :], vec_ref[4:5, :])
    weights = jnp.concatenate([wk_ref[...], wv_ref[...]], axis=1)
    for at in range(0, rows, 2 * BLK):
        here = slice(at, at + 2 * BLK)
        q_ref[here, :] = (rows_dot(left_q_ref[here, :], wq_ref[...]) + bias_q).astype(jnp.bfloat16)
    for at in range(0, keys, 2 * BLK):
        here = slice(at, at + 2 * BLK)
        both = rows_dot(left_k_ref[here, :], weights)
        k_ref[here, :] = both[:, :128].astype(jnp.bfloat16)
        v_ref[here, :] = (both[:, 128:] + bias_v).astype(jnp.bfloat16)
    queries = q_ref[...]
    for head, mask in enumerate(head_masks(rows)):
        qm_ref[head] = keep(mask, queries)
    vt_ref[...] = v_ref[...].T
    if causal:
        below = lax.broadcasted_iota(jnp.int32, (BLK, BLK), 0) <= lax.broadcasted_iota(
            jnp.int32, (BLK, BLK), 1
        )

    def start_of(j):
        return j * tile if causal else 0

    def scores_of(j, head):
        begin = start_of(j)
        scores = rows_dot_t(k_ref[j * tile : (j + 1) * tile, :], qm_ref[head, begin:, :]) * SCALE2
        if causal:
            pieces = [jnp.where(below, scores[:, :BLK], masked_score)]
            for i in range(j + 1, rows // BLK):
                off = jnp.where(mask_ref[0, i, j] > 0, 0.0, masked_score)
                pieces.append(scores[:, (i - j) * BLK : (i - j + 1) * BLK] + off)
            scores = jnp.concatenate(pieces, axis=1)
        return scores

    def add_tile(j, head, scores, shift):
        begin = start_of(j)
        if shift is not None:
            scores = scores - shift[:, begin:]
        probs = jnp.exp2(scores)
        total = jnp.sum(probs, axis=0, keepdims=True)
        mixed = rows_dot(
            vt_ref[head * HD : (head + 1) * HD, j * tile : (j + 1) * tile], probs.astype(jnp.bfloat16)
        )
        if j == 0:
            sum_ref[head : head + 1, :] = total
            acc_ref[head] = mixed
        else:
            sum_ref[head : head + 1, begin:] += total
            acc_ref[head, :, begin:] += mixed

    def finish(shifts):
        both = []
        for head in range(2):
            total = sum_ref[head : head + 1, :]
            lse = jnp.log2(total)
            if shifts is not None:
                lse = lse + shifts[head]
            lse_ref[0, head : head + 1, :] = lse
            both.append(acc_ref[head] * (1.0 / total))
        o_ref[...] = jnp.concatenate(both, axis=0).T.astype(jnp.bfloat16)

    lse_ref[...] = jnp.zeros_like(lse_ref)
    waiting = []
    for j in range(keys // tile):
        for head in range(2):
            waiting.append((j, head, scores_of(j, head)))
            if len(waiting) > 1:
                add_tile(*waiting.pop(0), None)
    while waiting:
        add_tile(*waiting.pop(0), None)
    finish(None)
    sums = sum_ref[...]
    usable = jnp.min(jnp.where((sums > 1e-25) & (sums < 1e30), 1, 0))

    @pl.when(usable == 0)
    def _():
        for head in range(2):
            for j in range(keys // tile):
                peak = jnp.max(scores_of(j, head), axis=0, keepdims=True)
                begin = start_of(j)
                if j == 0:
                    top_ref[head : head + 1, :] = peak
                else:
                    top_ref[head : head + 1, begin:] = jnp.maximum(
                        top_ref[head : head + 1, begin:], peak
                    )
        shifts = [top_ref[0:1, :], top_ref[1:2, :]]
        for head in range(2):
            for j in range(keys // tile):
                add_tile(j, head, scores_of(j, head), shifts[head])
        finish(shifts)


def attend_forward(left_q, left_k, block_table, wide_full, vec_rows, causal):
    rows, keys = left_q.shape[0], left_k.shape[0]
    first = 0 if causal else 4
    bf16, f32 = jnp.bfloat16, jnp.float32

    def columns(count):
        return pl.BlockSpec((count, 128), lambda i: (0, i))

    def whole(count):
        return pl.BlockSpec((count, D), lambda i: (0, 0), pipeline_mode=pl.Buffered(1))

    def weight(unit):
        return pl.BlockSpec((D, 128), lambda i: (0, unit * (D // 128) + i))

    return pl.pallas_call(
        partial(forward_kernel, causal),
        grid=(D // 128,),
        in_specs=[pl.BlockSpec(memory_space=pltpu.SMEM), whole(rows), whole(keys)]
        + [weight(first), weight(first + 1), weight(first + 2), columns(vec_rows.shape[0])],
        out_specs=[columns(rows), pl.BlockSpec((1, 8, rows), lambda i: (i, 0, 0)), columns(rows)]
        + [columns(keys)] * 2,
        out_shape=[
            jax.ShapeDtypeStruct((rows, D), bf16),
            jax.ShapeDtypeStruct((D // 128, 8, rows), f32),
            jax.ShapeDtypeStruct((rows, D), bf16),
            jax.ShapeDtypeStruct((keys, D), bf16),
            jax.ShapeDtypeStruct((keys, D), bf16),
        ],
        scratch_shapes=[
            pltpu.VMEM((2, rows, 128), bf16),
            pltpu.VMEM((128, keys), bf16),
            pltpu.VMEM((2, HD, rows), f32),
            pltpu.VMEM((2, rows), f32),
            pltpu.VMEM((2, rows), f32),
        ],
        compiler_params=pltpu.CompilerParams(vmem_limit_bytes=48 << 20),
        cost_estimate=pl.CostEstimate(
            flops=(8 if causal else 16) * rows * keys * D, bytes_accessed=4 * left_q.size, transcendentals=0
        ),
    )(block_table, left_q, left_k, wide_full, wide_full, wide_full, vec_rows)


ROWS = 256
UNROLL = 4


def gelu_pair(x):
    magnitude = jnp.abs(x)
    bell = jnp.exp2((x * x) * (-0.5 / math.log(2.0)))
    t = 1.0 / (1.0 + (0.3275911 * math.sqrt(0.5)) * magnitude)
    poly = t * (0.127414796 + t * (-0.142248368 + t * (0.7107068705 + t * (-0.7265760135 + t * 0.5307027145))))
    tail = poly * bell
    phi_sum = jnp.where(x >= 0.0, 1.0 - tail, tail)
    return x * phi_sum, phi_sum + x * (bell * (1.0 / math.sqrt(2.0 * math.pi)))


def unit_rows(resid):
    average = jnp.mean(resid, axis=-1, keepdims=True)
    centred = resid - average
    inverse = lax.rsqrt(jnp.mean(centred * centred, axis=-1, keepdims=True) + eps_norm)
    return centred * inverse, inverse


def back_rows(upstream, unit, inverse, gain):
    scaled = upstream * gain
    centred = scaled - jnp.mean(scaled, axis=-1, keepdims=True)
    return inverse * (centred - unit * jnp.mean(scaled * unit, axis=-1, keepdims=True))


def column_dot(left, right):
    return lax.dot_general(left, right, (((0,), (0,)), ((), ())), preferred_element_type=jnp.float32)


def row_total(value):
    return jnp.sum(value, axis=0, keepdims=True)


def center_kernel(
    factor, mix_ref, one_ref, cot_ref, co_ref, win_ref, wout_ref, vec_ref,
    out_ref, two_ref, gmix_ref, tw_ref, tn_ref, tc_ref, sums_ref,
    low_ref, unit_ref, inv_ref, res_ref, act_ref, slope_ref, acc_ref, gffn_ref, bh_ref, gcross_ref,
):
    step = pl.program_id(0)
    rows = mix_ref.shape[0]
    blocks = rows // ROWS

    def vec(i):
        return vec_ref[i : i + 1, :]

    def each(body):
        def run(r, carry):
            body(pl.ds(pl.multiple_of(r * ROWS, ROWS), ROWS))
            return carry

        lax.fori_loop(0, blocks, run, 0, unroll=UNROLL)

    @pl.when(step == 0)
    def _():
        sums_ref[...] = jnp.zeros_like(sums_ref)

        def body(at):
            resid = one_ref[at, :] + rows_dot(mix_ref[at, :], co_ref[...]) + vec(5)
            unit, inverse = unit_rows(resid)
            unit_ref[at, :] = unit
            inv_ref[at, :] = jnp.broadcast_to(inverse, (ROWS, 128))
            normed = unit * vec(12) + vec(15)
            res_ref[at, :] = normed + vec(10)
            low_ref[at, :] = normed.astype(jnp.bfloat16)

        each(body)

    @pl.when(step < 4)
    def _():
        bias = vec_ref[pl.ds(6 + step, 1), :]

        def body(at):
            hidden = rows_dot(low_ref[at, :], win_ref[...]) + bias
            value, slope = gelu_pair(hidden)
            value = value.astype(jnp.bfloat16)
            act_ref[step, at, :] = value
            slope_ref[step, at, :] = slope.astype(jnp.bfloat16)
            res_ref[at, :] += rows_dot(value, wout_ref[...])

        each(body)

    @pl.when(step == 3)
    def _():
        def body(at):
            unit, inverse = unit_rows(res_ref[at, :])
            out_ref[at, :] = (unit * vec(13) + vec(16)).astype(jnp.bfloat16)
            upstream = cot_ref[at, :].astype(jnp.float32)
            grad = back_rows(upstream, unit, inverse, vec(13))
            acc_ref[at, :] = grad
            low = grad.astype(jnp.bfloat16)
            gffn_ref[at, :] = low
            sums_ref[13:14, :] += row_total(upstream * unit)
            sums_ref[16:17, :] += row_total(upstream)
            sums_ref[10:11, :] += row_total(low.astype(jnp.float32))

        each(body)

    @pl.when(step >= 4)
    def _():
        c = step - 4

        def body(at):
            grad = rows_dot_t(gffn_ref[at, :], wout_ref[...]) * slope_ref[c, at, :].astype(jnp.float32)
            low = grad.astype(jnp.bfloat16)
            bh_ref[at, :] = low
            sums_ref[pl.ds(step + 2, 1), :] += row_total(low.astype(jnp.float32))
            acc_ref[at, :] += rows_dot_t(low, win_ref[...])

        each(body)
        tn_ref[...] = (column_dot(act_ref[c], gffn_ref[...]) * factor).astype(jnp.bfloat16)
        rows_each = tw_ref.shape[1]
        for s in range(tw_ref.shape[0]):
            cols = slice(s * rows_each, (s + 1) * rows_each)
            tw_ref[s] = (column_dot(low_ref[:, cols], bh_ref[...]) * factor).astype(jnp.bfloat16)

    @pl.when(step == 7)
    def _():
        def body(at):
            upstream = acc_ref[at, :]
            unit = unit_ref[at, :]
            inverse = inv_ref[at, 0:1]
            grad = back_rows(upstream, unit, inverse, vec(12))
            two_ref[at, :] = grad
            low = grad.astype(jnp.bfloat16)
            gcross_ref[at, :] = low
            gmix_ref[at, :] = rows_dot_t(low, co_ref[...]).astype(jnp.bfloat16)
            sums_ref[12:13, :] += row_total(upstream * unit)
            sums_ref[15:16, :] += row_total(upstream)
            sums_ref[5:6, :] += row_total(low.astype(jnp.float32))

        each(body)
        tc_ref[...] = (column_dot(mix_ref[...], gcross_ref[...]) * factor).astype(jnp.bfloat16)


def center(mixed, one, cotangent, wide_full, narrow_full, vec_rows, factor, shards):
    rows = mixed.shape[0]
    whole = pl.BlockSpec((rows, D), lambda i: (0, 0))
    rows_each = D // shards
    bf16, f32 = jnp.bfloat16, jnp.float32
    return pl.pallas_call(
        partial(center_kernel, factor),
        grid=(8,),
        in_specs=[
            whole,
            whole,
            whole,
            pl.BlockSpec((D, D), lambda i: (0, 7)),
            pl.BlockSpec((D, D), lambda i: (0, 8 + i % 4)),
            pl.BlockSpec((D, D), lambda i: (i % 4, 0)),
            pl.BlockSpec(vec_rows.shape, lambda i: (0, 0)),
        ],
        out_specs=[
            whole,
            whole,
            whole,
            pl.BlockSpec((shards, rows_each, D), lambda i: (0, jnp.maximum(i - 4, 0), 0)),
            pl.BlockSpec((D, D), lambda i: (jnp.maximum(i - 4, 0), 0)),
            pl.BlockSpec((D, D), lambda i: (0, 0)),
            pl.BlockSpec((24, D), lambda i: (0, 0)),
        ],
        out_shape=[
            jax.ShapeDtypeStruct((rows, D), bf16),
            jax.ShapeDtypeStruct((rows, D), f32),
            jax.ShapeDtypeStruct((rows, D), bf16),
            jax.ShapeDtypeStruct((shards, 4 * rows_each, D), bf16),
            jax.ShapeDtypeStruct((FF, D), bf16),
            jax.ShapeDtypeStruct((D, D), bf16),
            jax.ShapeDtypeStruct((24, D), f32),
        ],
        scratch_shapes=[
            pltpu.VMEM((rows, D), bf16),
            pltpu.VMEM((rows, D), f32),
            pltpu.VMEM((rows, 128), f32),
            pltpu.VMEM((rows, D), f32),
            pltpu.VMEM((4, rows, D), bf16),
            pltpu.VMEM((4, rows, D), bf16),
            pltpu.VMEM((rows, D), f32),
            pltpu.VMEM((rows, D), bf16),
            pltpu.VMEM((rows, D), bf16),
            pltpu.VMEM((rows, D), bf16),
        ],
        compiler_params=pltpu.CompilerParams(vmem_limit_bytes=58 << 20),
        cost_estimate=pl.CostEstimate(flops=54 * rows * D * D, bytes_accessed=30 << 20, transcendentals=0),
    )(mixed, one, cotangent, wide_full, wide_full, narrow_full, vec_rows)


MESH_ID = pl.DeviceIdType.MESH
UNIT = 384
HALF = 384


def peers_of(lanes):
    rep, shard = lax.axis_index("rep"), lax.axis_index("shard")
    x, y, z = rep % 2, (rep // 2) % 2, rep // 4
    base = rep - z * 4
    others = [(base + 4 * ((z + k) % lanes), shard) for k in range(1, lanes)]
    first = rep + 1 - 2 * x
    second = rep + 2 - 4 * y
    return rep, shard, x, y, z, (rep, 1 - shard), (first, shard), (second, shard), others


def enter_barrier(lanes):
    _, _, _, _, _, sibling, first, second, others = peers_of(lanes)
    barrier = pltpu.get_barrier_semaphore()
    for peer in [sibling, first, second] + others:
        pl.semaphore_signal(barrier, inc=1, device_id=peer, device_id_type=MESH_ID)
    pl.semaphore_wait(barrier, 2 + lanes)


def aligned(value, by=16):
    return pl.multiple_of(value, by)


def remote_copy(sems, index, source, target, peer):
    return pltpu.make_async_remote_copy(
        src_ref=source,
        dst_ref=target,
        send_sem=sems[0].at[index],
        recv_sem=sems[1].at[index],
        device_id=peer,
        device_id_type=MESH_ID,
    )


def unit_scratch(mode, lanes):
    bf16 = jnp.bfloat16
    block = UNIT // (2 * lanes)
    shapes = [pltpu.VMEM((UNIT, D), bf16), pltpu.VMEM((block, HALF), bf16)]
    if mode != "gather":
        shapes += [
            pltpu.VMEM((UNIT, D), bf16),
            pltpu.VMEM((UNIT, HALF), bf16),
            pltpu.VMEM((UNIT // 2, HALF), bf16),
            pltpu.VMEM((lanes, block, HALF), bf16),
        ]
    return shapes + [
        pltpu.SemaphoreType.DMA((5 + 2 * lanes,)),
        pltpu.SemaphoreType.DMA((5 + 2 * lanes,)),
        pltpu.SemaphoreType.DMA((3,)),
    ]


def unit_places(x_first, lanes):
    rep, shard, x, y, z, sibling, peer_x, peer_y, others = peers_of(lanes)
    here_a, here_b = (x, y) if x_first else (y, x)
    peer_a, peer_b = (peer_x, peer_y) if x_first else (peer_y, peer_x)
    return shard, z, here_a, here_b, sibling, peer_a, peer_b, others


def scatter_steps(term, row, scratch, x_first, lanes, block_out):
    got, block_ref, acc, got_a, got_b, got_z = scratch[:6]
    sems, local_sem = scratch[-3:-1], scratch[-1]
    shard, z, here_a, here_b, sibling, peer_a, peer_b, others = unit_places(x_first, lanes)
    half_rows, block = UNIT // 2, UNIT // (2 * lanes)
    mine_cols = pl.ds(aligned(here_a * HALF, 128), HALF)
    their_cols = pl.ds(aligned((1 - here_a) * HALF, 128), HALF)
    mine_b = aligned(here_b * half_rows)
    core = remote_copy(sems, 0, term.at[1 - shard, pl.ds(row, UNIT)], got, sibling)
    load = pltpu.make_async_copy(term.at[shard, pl.ds(row, UNIT)], acc, local_sem.at[0])
    to_a = remote_copy(sems, 1, acc.at[:, their_cols], got_a, peer_a)
    to_b = remote_copy(
        sems, 2, acc.at[pl.ds(aligned((1 - here_b) * half_rows), half_rows), mine_cols], got_b, peer_b
    )
    to_z = [
        remote_copy(
            sems, 5 + k, acc.at[pl.ds(aligned(mine_b + ((z + k + 1) % lanes) * block), block), mine_cols],
            got_z.at[z], peer,
        )
        for k, peer in enumerate(others)
    ]
    f32, bf16 = jnp.float32, jnp.bfloat16

    def start():
        core.start()
        load.start()

    def step_a():
        load.wait()
        core.wait()

        def body(i, carry):
            at = pl.ds(aligned(i * block), block)
            acc[at, :] = acc[at, :] + got[at, :]
            return carry

        lax.fori_loop(0, UNIT // block, body, 0, unroll=True)
        to_a.start()

    def step_b():
        to_a.wait()

        def body(i, carry):
            at = pl.ds(aligned(i * block), block)
            acc[at, mine_cols] = acc[at, mine_cols] + got_a[at, :]
            return carry

        lax.fori_loop(0, UNIT // block, body, 0, unroll=True)
        to_b.start()

    def step_z():
        to_b.wait()

        def body(i, carry):
            at = pl.ds(aligned(mine_b + i * block), block)
            acc[at, mine_cols] = acc[at, mine_cols] + got_b[pl.ds(aligned(i * block), block), :]
            return carry

        lax.fori_loop(0, half_rows // block, body, 0, unroll=True)
        for copy in to_z:
            copy.start()

    def step_own():
        for copy in to_z:
            copy.wait()
        total = acc[pl.ds(aligned(mine_b + z * block), block), mine_cols].astype(f32)
        for k in range(1, lanes):
            total = total + got_z[(z + k) % lanes].astype(f32)
        block_ref[...] = total.astype(bf16)
        if block_out is not None:
            block_out[...] = total.astype(bf16)

    return [start, step_a, step_b, step_z, step_own]


def gather_steps(block_in, sum_out, scratch, x_first, lanes, entire):
    full, block_ref = scratch[:2]
    sems, local_sem = scratch[-3:-1], scratch[-1]
    shard, z, here_a, here_b, sibling, peer_a, peer_b, others = unit_places(x_first, lanes)
    half_rows, block = UNIT // 2, UNIT // (2 * lanes)
    mine_cols = pl.ds(aligned(here_a * HALF, 128), HALF)
    mine_b = aligned(here_b * half_rows)
    mine_z = full.at[pl.ds(aligned(mine_b + z * block), block), mine_cols]
    mine_half = full.at[pl.ds(mine_b, half_rows), mine_cols]
    all_z = [remote_copy(sems, 5 + lanes + k, mine_z, mine_z, peer) for k, peer in enumerate(others)]
    all_b = remote_copy(sems, 3, mine_half, mine_half, peer_b)
    mine_all = full.at[:, mine_cols]
    all_a = remote_copy(sems, 4, mine_all, mine_all, peer_a)
    store = pltpu.make_async_copy(full if entire else mine_all, sum_out, local_sem.at[1])

    def start():
        source = block_ref if block_in is None else block_in
        full[pl.ds(aligned(mine_b + z * block), block), mine_cols] = source[...]
        for copy in all_z:
            copy.start()

    def step_b():
        for copy in all_z:
            copy.wait()
        all_b.start()

    def step_a():
        all_b.wait()
        all_a.start()

    def step_store():
        (all_a if entire else all_b).wait()
        store.start()

    return [start, step_b] + [step_a] * entire + [step_store, store.wait]


def joined_steps(scatter, gather):
    own, begin = scatter[-1], gather[0]

    def both():
        own()
        begin()

    return scatter[:-1] + [both] + gather[1:]


def small_scratch(shape, lanes):
    return [
        pltpu.VMEM((3,) + shape, jnp.float32),
        pltpu.VMEM((3,) + shape, jnp.float32),
        pltpu.VMEM((lanes,) + shape, jnp.float32),
        pltpu.SemaphoreType.DMA((3 + lanes,)),
        pltpu.SemaphoreType.DMA((3 + lanes,)),
    ]


def small_steps(term_ref, sum_ref, scratch, lanes):
    held, got, got_z = scratch[:3]
    sems = scratch[3:]
    rep, shard, x, y, z, sibling, peer_x, peer_y, others = peers_of(lanes)
    core = remote_copy(sems, 0, term_ref.at[1 - shard], got.at[0], sibling)
    to_x = remote_copy(sems, 1, held.at[0], got.at[1], peer_x)
    to_y = remote_copy(sems, 2, held.at[1], got.at[2], peer_y)
    to_z = [remote_copy(sems, 3 + k, held.at[2], got_z.at[z], peer) for k, peer in enumerate(others)]

    def step_x():
        core.wait()
        held[0] = term_ref[shard] + got[0]
        to_x.start()

    def step_y():
        to_x.wait()
        held[1] = held[0] + got[1]
        to_y.start()

    def step_z():
        to_y.wait()
        held[2] = held[1] + got[2]
        got_z[z] = held[2]
        for copy in to_z:
            copy.start()

    def step_end():
        for copy in to_z:
            copy.wait()
        total = got_z[0]
        for k in range(1, lanes):
            total = total + got_z[k]
        sum_ref[...] = total

    return [core.start, step_x, step_y, step_z, step_end]


class Traffic:
    def __init__(self, items, lanes, entire, terms=(), blocks=None, small=None):
        self.items, self.lanes, self.entire, self.terms = items, lanes, entire, list(terms)
        self.blocks, self.small = blocks, small
        self.n_scatter = sum(item[0] == "scatter" for item in items)
        summed = [item for item in items if item[0] != "scatter"]
        self.n_x = len(summed) if entire else sum(item[1] for item in summed)
        self.n_y = len(summed) - self.n_x

    def operands(self):
        return self.terms + [x for x in (self.blocks, self.small) if x is not None]

    def in_specs(self):
        vmem = pl.BlockSpec(memory_space=pltpu.VMEM)
        return [pl.BlockSpec(memory_space=pl.ANY)] * len(self.terms) + [vmem] * (
            (self.blocks is not None) + (self.small is not None)
        )

    def outputs(self):
        vmem, anywhere = pl.BlockSpec(memory_space=pltpu.VMEM), pl.BlockSpec(memory_space=pl.ANY)
        shape, bf16 = jax.ShapeDtypeStruct, jnp.bfloat16
        found = []
        if self.n_scatter:
            found.append((vmem, shape((self.n_scatter, UNIT // (2 * self.lanes), HALF), bf16)))
        for count in (self.n_x, self.n_y):
            if count:
                found.append((anywhere, shape((count, UNIT, D if self.entire else HALF), bf16)))
        if self.small is not None:
            found.append((vmem, shape(self.small.shape[1:], jnp.float32)))
        return found

    def out_specs(self):
        return [spec for spec, _ in self.outputs()]

    def out_shape(self):
        return [shape for _, shape in self.outputs()]

    def scratch(self):
        shapes = []
        for item in self.items:
            shapes += unit_scratch(item[0], self.lanes)
        if self.small is not None:
            shapes += small_scratch(self.small.shape[1:], self.lanes)
        return shapes

    def unpack(self, outs):
        outs = list(outs)
        blocks = outs.pop(0) if self.n_scatter else None
        halves = [outs.pop(0) if count else None for count in (self.n_x, self.n_y)]
        return blocks, halves, outs.pop(0) if self.small is not None else None

    def steps(self, ins, outs, scratch):
        ins, scratch = list(ins), list(scratch)
        terms = [ins.pop(0) for _ in self.terms]
        blocks = ins.pop(0) if self.blocks is not None else None
        small = ins.pop(0) if self.small is not None else None
        block_out, halves, small_out = self.unpack(outs)
        found = []
        n_block, n_in, n_half = 0, 0, [0, 0]
        for mode, x_first, which, row in self.items:
            count = len(unit_scratch(mode, self.lanes))
            mine, scratch = scratch[:count], scratch[count:]
            scatter, gather = [], []
            if mode != "gather":
                target = block_out.at[n_block] if mode == "scatter" else None
                scatter = scatter_steps(terms[which], row, mine, x_first, self.lanes, target)
                n_block += mode == "scatter"
            if mode != "scatter":
                source = None
                if mode == "gather":
                    source = blocks.at[n_in]
                    n_in += 1
                kind = 0 if self.entire or x_first else 1
                gather = gather_steps(
                    source, halves[kind].at[n_half[kind]], mine, x_first, self.lanes, self.entire
                )
                n_half[kind] += 1
            found.append(joined_steps(scatter, gather) if mode == "both" else scatter + gather)
        if small is not None:
            found.append(small_steps(small, small_out, scratch, self.lanes))
        return found


def traffic_kernel(traffic, order, *refs):
    n_in, n_out = len(traffic.in_specs()), len(traffic.out_specs())
    steps = traffic.steps(refs[:n_in], refs[n_in : n_in + n_out], refs[n_in + n_out :])
    enter_barrier(traffic.lanes)
    for which, step in order:
        steps[which][step]()


def run_traffic(traffic, order, collective_id):
    return pl.pallas_call(
        partial(traffic_kernel, traffic, order),
        in_specs=traffic.in_specs(),
        out_specs=traffic.out_specs(),
        out_shape=traffic.out_shape(),
        scratch_shapes=traffic.scratch(),
        compiler_params=pltpu.CompilerParams(
            collective_id=collective_id, has_side_effects=True, vmem_limit_bytes=58 << 20
        ),
    )(*traffic.operands())


def gather_kernel(wide_ref, narrow_ref, wide_out, narrow_out, held, send_sem, recv_sem, local_sem):
    step = pl.program_id(0)
    rep, shard = lax.axis_index("rep"), lax.axis_index("shard")
    sibling = (rep, 1 - shard)

    @pl.when(step == 0)
    def _():
        barrier = pltpu.get_barrier_semaphore()
        pl.semaphore_signal(barrier, inc=1, device_id=sibling, device_id_type=MESH_ID)
        pl.semaphore_wait(barrier, 1)

    def copies(unit, target):
        local = pltpu.make_async_copy(held.at[unit], target, local_sem.at[unit])
        return local, remote_copy((send_sem, recv_sem), unit, held.at[unit], target, sibling)

    def wide_copies(unit):
        target = wide_out.at[
            pl.ds(aligned(shard * UNIT), UNIT), pl.ds(aligned(unit * D, 128), D)
        ]
        return copies(unit, target)

    def narrow_copies(unit):
        row = aligned(shard * (FF // 2) + (unit - WIDE_UNITS) * UNIT)
        return copies(unit, narrow_out.at[pl.ds(row, UNIT)])

    @pl.when(step < WIDE_UNITS)
    def _():
        held[step] = wide_ref[...].astype(jnp.bfloat16)
        for copy in wide_copies(step):
            copy.start()

    @pl.when(step >= WIDE_UNITS)
    def _():
        held[step] = narrow_ref[...].astype(jnp.bfloat16)
        for copy in narrow_copies(step):
            copy.start()

    @pl.when(step == ALL_UNITS - 1)
    def _():
        for unit in range(ALL_UNITS):
            for copy in wide_copies(unit) if unit < WIDE_UNITS else narrow_copies(unit):
                copy.wait()


def gather_weights(wide_master, narrow_master):
    bf16 = jnp.bfloat16
    return pl.pallas_call(
        gather_kernel,
        grid=(ALL_UNITS,),
        in_specs=[
            pl.BlockSpec((UNIT, D), lambda i: (0, jnp.minimum(i, WIDE_UNITS - 1))),
            pl.BlockSpec((UNIT, D), lambda i: (jnp.maximum(i - WIDE_UNITS, 0), 0)),
        ],
        out_specs=[pl.BlockSpec(memory_space=pl.ANY)] * 2,
        out_shape=[
            jax.ShapeDtypeStruct((D, wide_master.shape[1]), bf16),
            jax.ShapeDtypeStruct((FF, D), bf16),
        ],
        scratch_shapes=[
            pltpu.VMEM((ALL_UNITS, UNIT, D), bf16),
            pltpu.SemaphoreType.DMA((ALL_UNITS,)),
            pltpu.SemaphoreType.DMA((ALL_UNITS,)),
            pltpu.SemaphoreType.DMA((ALL_UNITS,)),
        ],
        compiler_params=pltpu.CompilerParams(
            collective_id=3, has_side_effects=True, vmem_limit_bytes=40 << 20
        ),
    )(wide_master, narrow_master)


def backward_kernel(causal, traffic, table, factor, *refs):
    refs = list(refs)
    take = lambda count: [refs.pop(0) for _ in range(count)]
    mask_ref, q_ref, k_ref, v_ref, m_ref, x_ref, lse_ref, left_q_ref, up_ref, wq_ref, wk_ref, wv_ref = take(12)
    if not causal:
        left_k_ref, wo_ref, res_ref, mixo_ref, vec_ref = take(5)
    traffic_in = take(len(traffic.in_specs()) if traffic else 0)
    tq_ref, tk_ref, tv_ref, pair_sums_ref, grad_ref = take(5)
    if not causal:
        encg_ref, gmix_ref, to_ref, norm_sums_ref = take(4)
    traffic_out = take(len(traffic.out_specs()) if traffic else 0)
    qm_ref, mm_ref, qt_ref, mt_ref, col_ref, acc_ref, dkt_ref, dvt_ref, total_ref, up_sem = take(10)
    if not causal:
        total_k_ref, low_ref = take(2)
    bf16, f32 = jnp.bfloat16, jnp.float32
    rows, keys = q_ref.shape[0], k_ref.shape[0]
    pair = pl.program_id(0)
    step, tile = (BLK, BLK) if causal else (2 * BLK, 2 * BLK)
    slot = [0]
    if traffic:
        steps = traffic.steps(traffic_in, traffic_out, refs)

        @pl.when(pair == 0)
        def _():
            enter_barrier(traffic.lanes)

    def hook():
        if traffic:
            for at_pair in range(D // 128):
                todo = table.get((at_pair, slot[0]), ())
                if todo:

                    @pl.when(pair == at_pair)
                    def _():
                        for which, index in todo:
                            steps[which][index]()

        slot[0] += 1

    def each(count, size, body):
        def run(r, carry):
            body(pl.ds(pl.multiple_of(r * size, size), size))
            return carry

        lax.fori_loop(0, count // size, run, 0, unroll=True)

    hook()

    @pl.when(pair == 0)
    def _():
        load = pltpu.make_async_copy(up_ref, total_ref, up_sem)
        load.start()
        load.wait()
        if not causal:
            total_k_ref[...] = jnp.zeros_like(total_k_ref)

    masks = head_masks(rows)
    masks_k = head_masks(tile)
    queries, grads = q_ref[...], m_ref[...]
    qt_ref[...] = queries.T
    mt_ref[...] = grads.T
    product = grads.astype(f32) * x_ref[...].astype(f32)
    lse = lse_ref[0].T
    for head in range(2):
        qm_ref[head] = keep(masks[head], queries)
        mm_ref[head] = keep(masks[head], grads)
        centre = jnp.sum(keep(masks[head], product), axis=1, keepdims=True)
        col_ref[head] = jnp.broadcast_to(centre, (rows, 128))
        col_ref[2 + head] = jnp.broadcast_to(lse[:, head : head + 1], (rows, 128))
    if causal:
        below = lax.broadcasted_iota(jnp.int32, (BLK, BLK), 0) >= lax.broadcasted_iota(
            jnp.int32, (BLK, BLK), 1
        )

    def widen(column):
        return jnp.concatenate([column] * (tile // 128), axis=1)

    def level_of(head, j, begin, end):
        level = col_ref[2 + head, begin:end]
        if not causal:
            return level
        pieces = [level[:BLK]] if begin == j * BLK else []
        for i in range(begin // BLK + len(pieces), end // BLK):
            off = jnp.where(mask_ref[0, i, j] > 0, 0.0, -masked_score)
            pieces.append(level[i * BLK - begin : (i + 1) * BLK - begin] + off)
        return jnp.concatenate(pieces, axis=0) if len(pieces) > 1 else pieces[0]

    for j in range(keys // tile):
        key_rows = slice(j * tile, (j + 1) * tile)
        key, value = k_ref[key_rows, :], v_ref[key_rows, :]
        key_masked = [keep(mask, key) for mask in masks_k]
        total_k, total_v = [None, None], [None, None]
        cuts = (j * tile, rows) if causal else tuple(range(0, rows + 1, step))
        for begin, end in zip(cuts[:-1], cuts[1:]):
            here = slice(begin, end)
            hook()
            for head in range(2):
                scores = rows_dot_t(qm_ref[head, here, :], key)
                prob_grad = rows_dot_t(mm_ref[head, here, :], value)
                scores = scores * SCALE2 - widen(level_of(head, j, begin, end))
                if causal:
                    top = jnp.where(below, scores[:BLK], masked_score)
                    scores = top if end == begin + BLK else jnp.concatenate([top, scores[BLK:]], axis=0)
                probs = jnp.exp2(scores)
                score_grad = (probs * (prob_grad - widen(col_ref[head, here]))).astype(bf16)
                probs = probs.astype(bf16)
                part = slice(head * HD, (head + 1) * HD)
                add_v = rows_dot(mt_ref[part, here], probs)
                add_k = rows_dot(qt_ref[part, here], score_grad)
                total_v[head] = add_v if total_v[head] is None else total_v[head] + add_v
                total_k[head] = add_k if total_k[head] is None else total_k[head] + add_k
                add_q = rows_dot(score_grad, key_masked[head])
                if j == 0 and head == 0:
                    acc_ref[here, :] = add_q
                else:
                    acc_ref[here, :] += add_q
        for head in range(2):
            part = slice(head * HD, (head + 1) * HD)
            dkt_ref[part, key_rows] = (total_k[head] * FACTOR).astype(bf16)
            dvt_ref[part, key_rows] = total_v[head].astype(bf16)
    hook()
    grad_q = (acc_ref[...] * FACTOR).astype(bf16)
    grad_qt = grad_q.T
    pair_sums_ref[0:1, :] = row_total(grad_q.astype(f32))
    pair_sums_ref[1:2, :] = jnp.sum(dvt_ref[...].astype(f32), axis=1, keepdims=True).T

    def put(target, transposed):
        target[...] = (transposed * factor).T.astype(bf16)

    grad_k, grad_v = dkt_ref[...].T, dvt_ref[...].T
    if causal:
        joined = jnp.concatenate([grad_qt, dkt_ref[...], dvt_ref[...]], axis=0)
        found = rows_dot(joined, left_q_ref[...])
        put(tq_ref, found[:128])
        put(tk_ref, found[128:256])
        put(tv_ref, found[256:])
        hook()
        weights = jnp.concatenate([wq_ref[...], wk_ref[...], wv_ref[...]], axis=1)
        total_ref[...] += rows_dot_t(jnp.concatenate([grad_q, grad_k, grad_v], axis=1), weights)
        hook()

        @pl.when(pair == D // 128 - 1)
        def _():
            grad_ref[...] = total_ref[...].astype(bf16)
    else:
        put(tq_ref, rows_dot(grad_qt, left_q_ref[...]))
        total_ref[...] += rows_dot_t(grad_q, wq_ref[...])
        hook()
        found = rows_dot(jnp.concatenate([dkt_ref[...], dvt_ref[...]], axis=0), left_k_ref[...])
        put(tk_ref, found[:128])
        put(tv_ref, found[128:])
        hook()
        weights = jnp.concatenate([wk_ref[...], wv_ref[...]], axis=1)
        total_k_ref[...] += rows_dot_t(jnp.concatenate([grad_k, grad_v], axis=1), weights)
        hook()

        @pl.when(pair == D // 128 - 1)
        def _():
            encg_ref[...] = total_k_ref[...].astype(bf16)
            norm_sums_ref[...] = jnp.zeros_like(norm_sums_ref)

            def body(at):
                unit, inverse = unit_rows(res_ref[at, :])
                upstream = total_ref[at, :]
                grad = back_rows(upstream, unit, inverse, vec_ref[11:12, :])
                grad_ref[at, :] = grad
                low = grad.astype(bf16)
                low_ref[at, :] = low
                gmix_ref[at, :] = rows_dot_t(low, wo_ref[...]).astype(bf16)
                norm_sums_ref[0:1, :] += row_total(upstream * unit)
                norm_sums_ref[1:2, :] += row_total(upstream)
                norm_sums_ref[2:3, :] += row_total(low.astype(f32))

            each(rows, ROWS, body)
            to_ref[...] = (column_dot(mixo_ref[...], low_ref[...]) * factor).astype(bf16)

    hook()


def attend_backward(
    queries, keys_in, values_in, block_table, causal, mixed, lse, mixed_grad, left_q, upstream, wide_full,
    factor, extra, traffic, table, collective_id,
):
    rows, keys = queries.shape[0], keys_in.shape[0]
    bf16, f32 = jnp.bfloat16, jnp.float32
    first = 0 if causal else 4

    def columns(count):
        return pl.BlockSpec((count, 128), lambda i: (0, i))

    def whole(shape):
        return pl.BlockSpec(shape, lambda i: (0,) * len(shape), pipeline_mode=pl.Buffered(1))

    def weight(unit):
        return pl.BlockSpec((D, 128), lambda i: (0, unit * (D // 128) + i))

    spec_q, spec_k = columns(rows), columns(keys)
    in_specs = [pl.BlockSpec(memory_space=pltpu.SMEM), spec_q, spec_k, spec_k, spec_q, spec_q]
    in_specs += [pl.BlockSpec((1, 8, rows), lambda i: (i, 0, 0)), whole((rows, D)), pl.BlockSpec(memory_space=pl.ANY)]
    in_specs += [weight(first), weight(first + 1), weight(first + 2)]
    operands = [block_table, queries, keys_in, values_in, mixed_grad, mixed, lse, left_q, upstream]
    operands += [wide_full] * 3
    shape = jax.ShapeDtypeStruct
    out_specs = [columns(D)] * 3 + [columns(8), whole((rows, D))]
    out_shape = [shape((D, D), bf16)] * 3 + [shape((8, D), f32), shape((rows, D), bf16 if causal else f32)]
    scratch = [
        pltpu.VMEM((2, rows, 128), bf16),
        pltpu.VMEM((2, rows, 128), bf16),
        pltpu.VMEM((128, rows), bf16),
        pltpu.VMEM((128, rows), bf16),
        pltpu.VMEM((4, rows, 128), f32),
        pltpu.VMEM((rows, 128), f32),
        pltpu.VMEM((128, keys), bf16),
        pltpu.VMEM((128, keys), bf16),
        pltpu.VMEM((rows, D), f32),
        pltpu.SemaphoreType.DMA,
    ]
    if not causal:
        states, resid, mixed_self, vec_rows = extra
        in_specs += [whole((keys, D)), pl.BlockSpec((D, D), lambda i: (0, 3), pipeline_mode=pl.Buffered(1)), whole((rows, D)), whole((rows, D))]
        in_specs += [whole(vec_rows.shape)]
        operands += [states, wide_full, resid, mixed_self, vec_rows]
        out_specs += [whole((keys, D)), whole((rows, D)), whole((D, D)), whole((8, D))]
        out_shape += [shape((keys, D), bf16), shape((rows, D), bf16), shape((D, D), bf16), shape((8, D), f32)]
        scratch += [pltpu.VMEM((keys, D), f32), pltpu.VMEM((rows, D), bf16)]
    params = dict(vmem_limit_bytes=62 << 20)
    if traffic:
        in_specs += traffic.in_specs()
        operands += traffic.operands()
        out_specs += traffic.out_specs()
        out_shape += traffic.out_shape()
        scratch += traffic.scratch()
        params.update(collective_id=collective_id, has_side_effects=True)
    return pl.pallas_call(
        partial(backward_kernel, causal, traffic, table, factor),
        grid=(D // 128,),
        in_specs=in_specs,
        out_specs=out_specs,
        out_shape=out_shape,
        scratch_shapes=scratch,
        compiler_params=pltpu.CompilerParams(**params),
        cost_estimate=pl.CostEstimate(
            flops=(20 if causal else 40) * rows * keys * D, bytes_accessed=4 * queries.size, transcendentals=0
        ),
    )(*operands)


def adam_update(master, first, second, gradient, decay_on, rate):
    first_new = beta_one * first + (1.0 - beta_one) * gradient
    second_new = beta_two * second + (1.0 - beta_two) * gradient * gradient
    first_hat = first_new / (1.0 - beta_one**STEP)
    second_hat = second_new / (1.0 - beta_two**STEP)
    master_new = master - rate * (first_hat / (jnp.sqrt(second_hat) + eps_adam) + decay_on * master)
    return (master_new, first_new, second_new)


def adam_kernel(spans, aliased, table_ref, *refs):
    step = pl.program_id(0)
    count = 1 + max(span[0] for span in spans)
    sums = refs[:count]
    masters = refs[count : count + 6]
    outs = refs[count + 6 + aliased :]

    def update(sum_ref, master, first, second, grad, new, first_new, second_new, copy):
        def body(r, carry):
            at = pl.ds(pl.multiple_of(r * 32, 32), 32)
            gradient = sum_ref[0, at, :].astype(jnp.float32)
            grad[at, :] = gradient
            value, one, two = adam_update(
                master[at, :], first[at, :], second[at, :], gradient, weight_decay, learn_rate
            )
            new[at, :] = value
            first_new[at, :] = one
            second_new[at, :] = two
            copy[at, :] = value.astype(jnp.bfloat16)
            return carry

        lax.fori_loop(0, UNIT // 32, body, 0, unroll=3)

    for which, begin, end, wide in spans:

        @pl.when((step >= begin) & (step < end))
        def _():
            if wide:
                update(sums[which], *masters[:3], *outs[:5])
            else:
                update(sums[which], *masters[3:], *outs[5:])


def adam_halves(parts, x, y, wide, narrow, before):
    spans, starts, wides, narrow_rows, narrow_cols = [], [], [], [], []
    step = 0
    for which, (array, names, by_x, own) in enumerate(parts):
        starts.append(step)
        here = x if by_x else y
        entire = array.shape[2] == D
        for k, (kind, index) in enumerate([n for n in names for _ in range(1 + entire)]):
            half = k % 2 if entire else here if own else 1 - here
            is_wide = kind == "wide"
            if spans and spans[-1][0] == which and spans[-1][3] == is_wide:
                spans[-1] = (which, spans[-1][1], step + 1, is_wide)
            else:
                spans.append((which, step, step + 1, is_wide))
            wides.append(2 * index + half if is_wide else None)
            narrow_rows.append(None if is_wide else index)
            narrow_cols.append(None if is_wide else half)
            step += 1

    def filled(values):
        last = next((v for v in values if v is not None), 0)
        found = []
        for v in values:
            last = last if v is None else v
            found.append(jnp.asarray(last, jnp.int32))
        return jnp.stack(found)

    table = jnp.stack([filled(wides), filled(narrow_rows), filled(narrow_cols)])
    f32, bf16 = jnp.float32, jnp.bfloat16
    spec_w = pl.BlockSpec((UNIT, HALF), lambda i, t: (0, t[0, i]))
    spec_n = pl.BlockSpec((UNIT, HALF), lambda i, t: (t[1, i], t[2, i]))

    def spec_sum(start, array):
        halves = array.shape[2] // HALF

        def place(i, t):
            at = jnp.clip(i - start, 0, array.shape[0] * halves - 1)
            return (at // halves, 0, at % halves)

        return pl.BlockSpec((1, UNIT, HALF), place)

    def shapes(like):
        return [jax.ShapeDtypeStruct(like.shape, f32)] * 4 + [jax.ShapeDtypeStruct(like.shape, bf16)]

    operands = [part[0] for part in parts] + list(wide) + list(narrow)
    in_specs = [spec_sum(start, part[0]) for start, part in zip(starts, parts)]
    in_specs += [spec_w] * 3 + [spec_n] * 3
    aliases = {}
    if before is not None:
        aliases = {1 + len(operands) + i: i for i in range(10)}
        operands += list(before)
        in_specs += [pl.BlockSpec(memory_space=pl.ANY)] * 10
    return pl.pallas_call(
        partial(adam_kernel, tuple(spans), 0 if before is None else 10),
        grid_spec=pltpu.PrefetchScalarGridSpec(
            num_scalar_prefetch=1,
            grid=(step,),
            in_specs=in_specs,
            out_specs=[spec_w] * 5 + [spec_n] * 5,
        ),
        out_shape=shapes(wide[0]) + shapes(narrow[0]),
        input_output_aliases=aliases,
        compiler_params=pltpu.CompilerParams(vmem_limit_bytes=58 << 20),
        cost_estimate=pl.CostEstimate(
            flops=30 * step * UNIT * HALF, bytes_accessed=32 * step * UNIT * HALF, transcendentals=0
        ),
    )(table, *operands)


def matmul(left, right):
    return jnp.dot(left, right, preferred_element_type=jnp.float32)


def matmul_left(left, right):
    return lax.dot_general(
        left, right, (((0,), (0,)), ((), ())), preferred_element_type=jnp.float32
    )


def matmul_right(left, right):
    return lax.dot_general(
        left, right, (((1,), (1,)), ((), ())), preferred_element_type=jnp.float32
    )


def norm_forward(resid, gain, shift):
    average = jnp.mean(resid, axis=-1, keepdims=True)
    centred = resid - average
    inverse = lax.rsqrt(jnp.mean(centred * centred, axis=-1, keepdims=True) + eps_norm)
    normed = centred * inverse
    return normed * gain + shift


def on_device(
    tokens,
    encoder_states,
    cotangent,
    block_mask,
    wide_master,
    narrow_master,
    vec_master,
    wide_first,
    narrow_first,
    vec_first,
    wide_second,
    narrow_second,
    vec_second,
):
    replicas = lax.axis_size("rep")
    shards = lax.axis_size("shard")
    tokens_all = tokens.shape[0] * replicas * shards
    factor = float(tokens_all) ** (-0.5)
    bf16, f32 = jnp.bfloat16, jnp.float32

    def gathered(part):
        return lax.all_gather(part.astype(bf16), "shard", axis=0, tiled=True)

    if shards == 2:
        wide_full, narrow_full = gather_weights(wide_master, narrow_master)
    else:
        wide_full, narrow_full = gathered(wide_master), gathered(narrow_master)
    vector = gathered(vec_master).astype(f32)
    vec_rows = jnp.pad(vector.T, ((0, 24 - vector.shape[1]), (0, 0)))
    mixed_self, totals_self, queries, keys_self, values_self = attend_forward(
        tokens, tokens, block_mask, wide_full, vec_rows, True
    )
    resid_one = tokens.astype(f32) + matmul(mixed_self, wide_full[:, 3 * D : 4 * D]) + vector[:, 2]
    normed_one = norm_forward(resid_one, vector[:, 11], vector[:, 14])
    normed_low = normed_one.astype(bf16)
    mixed_cross, totals_cross, cross_queries, cross_keys, cross_values = attend_forward(
        normed_low, encoder_states, block_mask, wide_full, vec_rows, False
    )
    output, grad_two, grad_cross_mix, term_in, term_narrow, term_co, sums = center(
        mixed_cross, normed_one, cotangent, wide_full, narrow_full, vec_rows, factor, shards
    )

    def split(term):
        return term.reshape(shards, -1, D)

    lanes = replicas // 4
    carried = shards == 2 and replicas % 4 == 0 and UNIT % (32 * lanes) == 0
    terms = [term_in, split(term_narrow), split(term_co)]
    names = [("wide", 8 + i) for i in range(4)] + [("narrow", i) for i in range(4)] + [("wide", 7)]
    names += [("wide", i) for i in (4, 5, 6, 3, 0, 1, 2)]
    x_first = [i % 2 == 0 for i in range(9)] + [i % 2 == 1 for i in range(4)] + [i % 2 == 1 for i in range(3)]
    spots = [(0, UNIT * i) for i in range(4)] + [(1, UNIT * i) for i in range(4)] + [(2, 0)]
    parts_own, parts_far = [], []

    def item(mode, unit, which=0, row=0):
        return (mode, x_first[unit], which, row)

    def collect(traffic, outs, units):
        blocks, halves, small = traffic.unpack(outs)
        if traffic.entire:
            summed = [names[u] for u, it in zip(units, traffic.items) if it[0] != "scatter"]
            parts_own.append((halves[0], summed, True, True))
            return blocks, small
        for by_x, array in zip((True, False), halves):
            if array is None:
                continue
            mine = [names[u] for u, it in zip(units, traffic.items) if it[0] != "scatter" and it[1] == by_x]
            pairs = [(r, r ^ (1 if by_x else 2)) for r in range(replicas)]
            parts_own.append((array, mine, by_x, True))
            parts_far.append((lax.ppermute(array, "rep", pairs), mine, by_x, False))
        return blocks, small

    traffic = None
    units = list(range(N_BOTH + N_SCATTER))
    if carried:
        items = [item("both" if u < N_BOTH else "scatter", u, *spots[u]) for u in units]
        traffic = Traffic(items, lanes, True, terms)
    found = attend_backward(
        cross_queries, cross_keys, cross_values, block_mask, False, mixed_cross, totals_cross,
        grad_cross_mix, normed_low, grad_two, wide_full, factor,
        (encoder_states, resid_one, mixed_self, vec_rows), traffic, CROSS_TABLE, 1,
    )
    term_cq, term_ck, term_cv, cross_sums, grad_one, enc_grad, grad_self_mix, term_wo, norm_sums = found[:9]
    middle = [split(term) for term in (term_cq, term_ck, term_cv, term_wo)]
    if carried:
        blocks, _ = collect(traffic, found[9:], units)
        units = list(range(N_BOTH, N_BOTH + N_GATHER)) + list(range(9, 9 + N_MIDDLE))
        items = [item("gather", u) for u in units[:N_GATHER]]
        items += [item("scatter", 9 + i, i) for i in range(N_MIDDLE)]
        traffic = Traffic(items, lanes, True, middle[:N_MIDDLE], blocks[:N_GATHER])
    found = attend_backward(
        queries, keys_self, values_self, block_mask, True, mixed_self, totals_self,
        grad_self_mix, tokens, grad_one, wide_full, factor, None, traffic, SELF_TABLE, 2,
    )
    late = [split(term) for term in found[:3]]
    self_sums, in_grad = found[3:5]
    term_vec = jnp.concatenate(
        [
            self_sums[0:2],
            norm_sums[2:3],
            cross_sums[0:2],
            sums[5:11],
            norm_sums[0:1],
            sums[12:14],
            norm_sums[1:2],
            sums[15:],
        ],
        0,
    )
    term_vec = (term_vec * factor).reshape(24, shards, -1).transpose(1, 0, 2)
    wide = (wide_master, wide_first, wide_second)
    narrow = (narrow_master, narrow_first, narrow_second)
    if carried:
        blocks_self, _ = collect(traffic, found[5:], units)
        kept = list(range(N_BOTH + N_GATHER, N_BOTH + N_SCATTER)) + list(range(9, 9 + N_MIDDLE))
        fresh = list(range(N_BOTH + N_SCATTER, 9))
        items = [item("gather", u) for u in kept] + [item("both", u, *spots[u]) for u in fresh]
        others = middle[N_MIDDLE:] + late
        items += [item("both", 9 + N_MIDDLE + i, 3 + i) for i in range(len(others))]
        held = jnp.concatenate([blocks[N_GATHER:], blocks_self], 0)
        traffic = Traffic(items, lanes, False, terms + others, held, term_vec)
        _, vec_sum = collect(
            traffic, run_traffic(traffic, TAIL_ORDER, 0), kept + fresh + list(range(9 + N_MIDDLE, 16))
        )
        rep = lax.axis_index("rep")
        x, y = rep % 2, (rep // 2) % 2
        updated = adam_halves(parts_own, x, y, wide, narrow, None)
        updated = adam_halves(parts_far, x, y, wide, narrow, updated)
    else:
        by_column = late + [middle[3]] + middle[:3] + [terms[2]]
        by_column += [term_in[:, i * (D // shards) : (i + 1) * (D // shards)] for i in range(4)]
        wide_sum = jnp.concatenate([whole_sum(term) for term in by_column], 1).astype(f32)
        narrow_sum = whole_sum(terms[1]).astype(f32)
        vec_sum = lax.psum(lax.psum_scatter(term_vec, "shard", scatter_dimension=0), "rep")
        updated = []
        for gradient, state in ((wide_sum, wide), (narrow_sum, narrow)):
            new, first_new, second_new = adam_update(*state, gradient, weight_decay, learn_rate)
            updated += [gradient, new, first_new, second_new, new.astype(bf16)]
    (
        wide_grad, wide_new, wide_first_new, wide_second_new, wide_copy,
        narrow_grad, narrow_new, narrow_first_new, narrow_second_new, narrow_copy,
    ) = updated
    vec_grad = vec_sum[: vec_master.shape[1]].T
    vec_new, vec_first_new, vec_second_new = adam_update(
        vec_master, vec_first, vec_second, vec_grad, 0.0, vec_rate
    )
    return (
        output,
        in_grad,
        enc_grad,
        wide_grad,
        narrow_grad,
        vec_grad,
        wide_new,
        narrow_new,
        vec_new,
        wide_first_new,
        narrow_first_new,
        vec_first_new,
        wide_second_new,
        narrow_second_new,
        vec_second_new,
        wide_copy,
        narrow_copy,
        vec_new.astype(bf16),
    )


def whole_sum(term):
    return lax.psum(lax.psum_scatter(term, "shard", scatter_dimension=0), "rep")


def solution(mesh):
    in_specs = (
        P(("rep", "shard"), None),
        P(("rep", "shard"), None),
        P(("rep", "shard"), None),
        P(("rep", "shard"), None, None),
        P("shard", None),
        P("shard", None),
        P("shard", None),
        P("shard", None),
        P("shard", None),
        P("shard", None),
        P("shard", None),
        P("shard", None),
        P("shard", None),
    )
    out_specs = (
        P(("rep", "shard"), None),
        P(("rep", "shard"), None),
        P(("rep", "shard"), None),
        P("shard", None),
        P("shard", None),
        P("shard", None),
        P("shard", None),
        P("shard", None),
        P("shard", None),
        P("shard", None),
        P("shard", None),
        P("shard", None),
        P("shard", None),
        P("shard", None),
        P("shard", None),
        P("shard", None),
        P("shard", None),
        P("shard", None),
    )
    return jax.shard_map(
        on_device, mesh=mesh, in_specs=in_specs, out_specs=out_specs, check_vma=False
    )
```

```python
from functools import partial
import math

import jax
import jax.numpy as jnp
from jax import lax
from jax.experimental import pallas as pl
from jax.experimental.pallas import tpu as pltpu
from jax.sharding import PartitionSpec as P

D = 768
H = 12
HD = 64
FF = 3072
LEN = 1024
BLK = 256
STEP = 4


eps_norm = 1e-05
eps_adam = 1e-08
beta_one = 0.5
beta_two = 0.5
learn_rate = 0.03
vec_rate = 0.25
weight_decay = 0.1
masked_score = -1e30
FACTOR = HD ** (-0.5)
SCALE2 = FACTOR / math.log(2.0)
N_BOTH = 2
N_SCATTER = 6
N_GATHER = 2
N_MIDDLE = 2


CROSS_TABLE = {
    (0, 0): ((0, 0), (1, 0), (2, 0), (3, 0)),
    (0, 9): ((0, 1), (1, 1), (2, 1), (3, 1)),
    (2, 0): ((0, 2), (1, 2), (2, 2), (3, 2)),
    (2, 3): ((4, 0), (5, 0), (6, 0), (7, 0)),
    (2, 9): ((0, 3), (1, 3), (2, 3), (3, 3), (4, 1), (5, 1), (6, 1), (7, 1)),
    (4, 0): ((0, 4), (1, 4), (2, 4), (3, 4), (4, 2), (5, 2), (6, 2), (7, 2)),
    (4, 9): ((0, 5), (1, 5), (4, 3), (5, 3), (6, 3), (7, 3)),
    (5, 3): ((0, 6), (1, 6)),
    (5, 9): ((4, 4), (5, 4), (6, 4), (7, 4), (0, 7), (1, 7), (0, 8), (1, 8)),
}


SELF_TABLE = {
    (0, 0): ((0, 0), (1, 0), (2, 0), (3, 0)),
    (0, 5): ((2, 1), (3, 1)),
    (1, 5): ((0, 1), (1, 1)),
    (2, 5): ((0, 2), (1, 2), (2, 2), (3, 2)),
    (4, 5): ((0, 3), (1, 3), (2, 3), (3, 3)),
    (5, 5): ((0, 4), (1, 4), (2, 4), (3, 4)),
}


TAIL_ORDER = (
    (12, 0), (0, 0), (1, 0), (2, 0), (3, 0), (4, 0), (5, 0), (6, 0),
    (7, 0), (6, 1), (12, 1), (7, 1), (6, 2), (7, 2), (8, 0), (9, 0),
    (8, 1), (9, 1), (6, 3), (7, 3), (12, 2), (0, 1), (1, 1), (2, 1),
    (3, 1), (4, 1), (5, 1), (6, 4), (7, 4), (8, 2), (12, 3), (9, 2),
    (10, 0), (11, 0), (0, 2), (1, 2), (2, 2), (3, 2), (4, 2), (5, 2),
    (12, 4), (6, 5), (7, 5), (10, 1), (11, 1), (0, 3), (1, 3), (2, 3),
    (3, 3), (4, 3), (5, 3), (8, 3), (9, 3), (6, 6), (7, 6), (6, 7),
    (7, 7), (8, 4), (9, 4), (10, 2), (11, 2), (10, 3), (11, 3), (8, 5),
    (9, 5), (8, 6), (9, 6), (10, 4), (11, 4), (8, 7), (9, 7), (10, 5),
    (11, 5), (10, 6), (11, 6), (10, 7), (11, 7),
)


def head_masks(rows):
    first = lax.broadcasted_iota(jnp.int32, (rows, 128), 1) < HD
    return (first, jnp.logical_not(first))


def keep(mask, value):
    return jnp.where(mask, value, jnp.zeros((), value.dtype))


def rows_dot(left, right):
    return jnp.dot(left, right, preferred_element_type=jnp.float32)


def rows_dot_t(left, right):
    return lax.dot_general(
        left, right, (((1,), (1,)), ((), ())), preferred_element_type=jnp.float32
    )


def forward_kernel(causal, carry, *refs):
    mask_ref, left_q_ref, left_k_ref, wq_ref, wk_ref, wv_ref, vec_ref = refs[:7]
    masters, refs = refs[7 : 7 + 2 * carry], refs[7 + 2 * carry :]
    o_ref, lse_ref, q_ref, k_ref, v_ref = refs[:5]
    copies, refs = refs[5 : 5 + 2 * carry], refs[5 + 2 * carry :]
    qm_ref, vt_ref, acc_ref, sum_ref, top_ref = refs[:5]
    rows, keys = q_ref.shape[0], k_ref.shape[0]
    tile = BLK
    bias_q, bias_v = (vec_ref[0:1, :], vec_ref[1:2, :]) if causal else (vec_ref[3:4, :], vec_ref[4:5, :])
    weights = jnp.concatenate([wk_ref[...], wv_ref[...]], axis=1)
    for at in range(0, rows, 2 * BLK):
        here = slice(at, at + 2 * BLK)
        q_ref[here, :] = (rows_dot(left_q_ref[here, :], wq_ref[...]) + bias_q).astype(jnp.bfloat16)
    for at in range(0, keys, 2 * BLK):
        here = slice(at, at + 2 * BLK)
        both = rows_dot(left_k_ref[here, :], weights)
        k_ref[here, :] = both[:, :128].astype(jnp.bfloat16)
        v_ref[here, :] = (both[:, 128:] + bias_v).astype(jnp.bfloat16)
    queries = q_ref[...]
    for head, mask in enumerate(head_masks(rows)):
        qm_ref[head] = keep(mask, queries)
    vt_ref[...] = v_ref[...].T
    if causal:
        below = lax.broadcasted_iota(jnp.int32, (BLK, BLK), 0) <= lax.broadcasted_iota(
            jnp.int32, (BLK, BLK), 1
        )

    def start_of(j):
        return j * tile if causal else 0

    def scores_of(j, head):
        begin = start_of(j)
        scores = rows_dot_t(k_ref[j * tile : (j + 1) * tile, :], qm_ref[head, begin:, :]) * SCALE2
        if causal:
            pieces = [jnp.where(below, scores[:, :BLK], masked_score)]
            for i in range(j + 1, rows // BLK):
                off = jnp.where(mask_ref[0, i, j] > 0, 0.0, masked_score)
                pieces.append(scores[:, (i - j) * BLK : (i - j + 1) * BLK] + off)
            scores = jnp.concatenate(pieces, axis=1)
        return scores

    def add_tile(j, head, scores, shift):
        begin = start_of(j)
        if shift is not None:
            scores = scores - shift[:, begin:]
        probs = jnp.exp2(scores)
        total = jnp.sum(probs, axis=0, keepdims=True)
        mixed = rows_dot(
            vt_ref[head * HD : (head + 1) * HD, j * tile : (j + 1) * tile], probs.astype(jnp.bfloat16)
        )
        if j == 0:
            sum_ref[head : head + 1, :] = total
            acc_ref[head] = mixed
        else:
            sum_ref[head : head + 1, begin:] += total
            acc_ref[head, :, begin:] += mixed

    def finish(shifts):
        both = []
        for head in range(2):
            total = sum_ref[head : head + 1, :]
            lse = jnp.log2(total)
            if shifts is not None:
                lse = lse + shifts[head]
            lse_ref[0, head : head + 1, :] = lse
            both.append(acc_ref[head] * (1.0 / total))
        o_ref[...] = jnp.concatenate(both, axis=0).T.astype(jnp.bfloat16)

    def peaks():
        for head in range(2):
            for j in range(keys // tile):
                peak = jnp.max(scores_of(j, head), axis=0, keepdims=True)
                begin = start_of(j)
                if j == 0:
                    top_ref[head : head + 1, :] = peak
                else:
                    top_ref[head : head + 1, begin:] = jnp.maximum(
                        top_ref[head : head + 1, begin:], peak
                    )
        return [top_ref[0:1, :], top_ref[1:2, :]]

    lse_ref[...] = jnp.zeros_like(lse_ref)
    shifts = peaks() if carry else None
    waiting = []

    def next_tile():
        j, head, scores = waiting.pop(0)
        add_tile(j, head, scores, shifts[head] if carry else None)

    for j in range(keys // tile):
        for head in range(2):
            waiting.append((j, head, scores_of(j, head)))
            if len(waiting) > 1:
                next_tile()
    while waiting:
        next_tile()
    finish(shifts)
    if carry:
        gather_rest(pl.program_id(0), *masters, *copies, refs[5:])
        return
    sums = sum_ref[...]
    usable = jnp.min(jnp.where((sums > 1e-25) & (sums < 1e30), 1, 0))

    @pl.when(usable == 0)
    def _():
        tops = peaks()
        for head in range(2):
            for j in range(keys // tile):
                add_tile(j, head, scores_of(j, head), tops[head])
        finish(tops)


def attend_forward(left_q, left_k, block_table, weights, vec_rows, causal, masters):
    rows, keys = left_q.shape[0], left_k.shape[0]
    first = 0 if causal else 1
    carry = masters is not None
    bf16, f32 = jnp.bfloat16, jnp.float32

    def columns(count):
        return pl.BlockSpec((count, 128), lambda i: (0, i))

    def whole(count):
        return pl.BlockSpec((count, D), lambda i: (0, 0), pipeline_mode=pl.Buffered(1))

    def weight(unit):
        return pl.BlockSpec((D, 128), lambda i: (0, unit * (D // 128) + i))

    anywhere = [pl.BlockSpec(memory_space=pl.ANY)] * 2
    params = dict(vmem_limit_bytes=56 << 20)
    if carry:
        params.update(collective_id=4, has_side_effects=True)
    return pl.pallas_call(
        partial(forward_kernel, causal, carry),
        grid=(D // 128,),
        in_specs=[pl.BlockSpec(memory_space=pltpu.SMEM), whole(rows), whole(keys)]
        + [weight(first), weight(first + 1), weight(first + 2), columns(vec_rows.shape[0])] + anywhere * carry,
        out_specs=[columns(rows), pl.BlockSpec((1, 8, rows), lambda i: (i, 0, 0)), columns(rows)]
        + [columns(keys)] * 2 + anywhere * carry,
        out_shape=[
            jax.ShapeDtypeStruct((rows, D), bf16),
            jax.ShapeDtypeStruct((D // 128, 8, rows), f32),
            jax.ShapeDtypeStruct((rows, D), bf16),
            jax.ShapeDtypeStruct((keys, D), bf16),
            jax.ShapeDtypeStruct((keys, D), bf16),
        ]
        + [jax.ShapeDtypeStruct((D, 9 * D), bf16), jax.ShapeDtypeStruct((FF, D), bf16)] * carry,
        scratch_shapes=[
            pltpu.VMEM((2, rows, 128), bf16),
            pltpu.VMEM((128, keys), bf16),
            pltpu.VMEM((2, HD, rows), f32),
            pltpu.VMEM((2, rows), f32),
            pltpu.VMEM((2, rows), f32),
        ]
        + (rest_scratch() if carry else []),
        compiler_params=pltpu.CompilerParams(**params),
        cost_estimate=pl.CostEstimate(
            flops=(8 if causal else 16) * rows * keys * D, bytes_accessed=4 * left_q.size, transcendentals=0
        ),
    )(block_table, left_q, left_k, weights, weights, weights, vec_rows, *(masters or ()))


ROWS = 256
UNROLL = 4


def gelu_pair(x):
    magnitude = jnp.abs(x)
    bell = jnp.exp2((x * x) * (-0.5 / math.log(2.0)))
    t = 1.0 / (1.0 + (0.3275911 * math.sqrt(0.5)) * magnitude)
    poly = t * (0.127414796 + t * (-0.142248368 + t * (0.7107068705 + t * (-0.7265760135 + t * 0.5307027145))))
    tail = poly * bell
    phi_sum = jnp.where(x >= 0.0, 1.0 - tail, tail)
    return x * phi_sum, phi_sum + x * (bell * (1.0 / math.sqrt(2.0 * math.pi)))


def unit_rows(resid):
    average = jnp.mean(resid, axis=-1, keepdims=True)
    centred = resid - average
    inverse = lax.rsqrt(jnp.mean(centred * centred, axis=-1, keepdims=True) + eps_norm)
    return centred * inverse, inverse


def back_rows(upstream, unit, inverse, gain):
    scaled = upstream * gain
    centred = scaled - jnp.mean(scaled, axis=-1, keepdims=True)
    return inverse * (centred - unit * jnp.mean(scaled * unit, axis=-1, keepdims=True))


def column_dot(left, right):
    return lax.dot_general(left, right, (((0,), (0,)), ((), ())), preferred_element_type=jnp.float32)


def row_total(value):
    return jnp.sum(value, axis=0, keepdims=True)


def center_kernel(
    factor, mix_ref, one_ref, cot_ref, co_ref, win_ref, wout_ref, vec_ref,
    out_ref, two_ref, gmix_ref, tw_ref, tn_ref, tc_ref, sums_ref,
    low_ref, unit_ref, inv_ref, res_ref, act_ref, slope_ref, acc_ref, gffn_ref, bh_ref, gcross_ref,
):
    step = pl.program_id(0)
    rows = mix_ref.shape[0]
    blocks = rows // ROWS

    def vec(i):
        return vec_ref[i : i + 1, :]

    def each(body):
        def run(r, carry):
            body(pl.ds(pl.multiple_of(r * ROWS, ROWS), ROWS))
            return carry

        lax.fori_loop(0, blocks, run, 0, unroll=UNROLL)

    @pl.when(step == 0)
    def _():
        sums_ref[...] = jnp.zeros_like(sums_ref)

        def body(at):
            resid = one_ref[at, :] + rows_dot(mix_ref[at, :], co_ref[...]) + vec(5)
            unit, inverse = unit_rows(resid)
            unit_ref[at, :] = unit
            inv_ref[at, :] = jnp.broadcast_to(inverse, (ROWS, 128))
            normed = unit * vec(12) + vec(15)
            res_ref[at, :] = normed + vec(10)
            low_ref[at, :] = normed.astype(jnp.bfloat16)

        each(body)

    @pl.when(step < 4)
    def _():
        bias = vec_ref[pl.ds(6 + step, 1), :]

        def body(at):
            hidden = rows_dot(low_ref[at, :], win_ref[...]) + bias
            value, slope = gelu_pair(hidden)
            value = value.astype(jnp.bfloat16)
            act_ref[step, at, :] = value
            slope_ref[step, at, :] = slope.astype(jnp.bfloat16)
            res_ref[at, :] += rows_dot(value, wout_ref[...])

        each(body)

    @pl.when(step == 3)
    def _():
        def body(at):
            unit, inverse = unit_rows(res_ref[at, :])
            out_ref[at, :] = (unit * vec(13) + vec(16)).astype(jnp.bfloat16)
            upstream = cot_ref[at, :].astype(jnp.float32)
            grad = back_rows(upstream, unit, inverse, vec(13))
            acc_ref[at, :] = grad
            low = grad.astype(jnp.bfloat16)
            gffn_ref[at, :] = low
            sums_ref[13:14, :] += row_total(upstream * unit)
            sums_ref[16:17, :] += row_total(upstream)
            sums_ref[10:11, :] += row_total(low.astype(jnp.float32))

        each(body)

    @pl.when(step >= 4)
    def _():
        c = step - 4

        def body(at):
            grad = rows_dot_t(gffn_ref[at, :], wout_ref[...]) * slope_ref[c, at, :].astype(jnp.float32)
            low = grad.astype(jnp.bfloat16)
            bh_ref[at, :] = low
            sums_ref[pl.ds(step + 2, 1), :] += row_total(low.astype(jnp.float32))
            acc_ref[at, :] += rows_dot_t(low, win_ref[...])

        each(body)
        tn_ref[...] = (column_dot(act_ref[c], gffn_ref[...]) * factor).astype(jnp.bfloat16)
        rows_each = tw_ref.shape[1]
        for s in range(tw_ref.shape[0]):
            cols = slice(s * rows_each, (s + 1) * rows_each)
            tw_ref[s] = (column_dot(low_ref[:, cols], bh_ref[...]) * factor).astype(jnp.bfloat16)

    @pl.when(step == 7)
    def _():
        def body(at):
            upstream = acc_ref[at, :]
            unit = unit_ref[at, :]
            inverse = inv_ref[at, 0:1]
            grad = back_rows(upstream, unit, inverse, vec(12))
            two_ref[at, :] = grad
            low = grad.astype(jnp.bfloat16)
            gcross_ref[at, :] = low
            gmix_ref[at, :] = rows_dot_t(low, co_ref[...]).astype(jnp.bfloat16)
            sums_ref[12:13, :] += row_total(upstream * unit)
            sums_ref[15:16, :] += row_total(upstream)
            sums_ref[5:6, :] += row_total(low.astype(jnp.float32))

        each(body)
        tc_ref[...] = (column_dot(mix_ref[...], gcross_ref[...]) * factor).astype(jnp.bfloat16)


def center(mixed, one, cotangent, wide_full, narrow_full, vec_rows, factor, shards):
    rows = mixed.shape[0]
    whole = pl.BlockSpec((rows, D), lambda i: (0, 0))
    rows_each = D // shards
    bf16, f32 = jnp.bfloat16, jnp.float32
    return pl.pallas_call(
        partial(center_kernel, factor),
        grid=(8,),
        in_specs=[
            whole,
            whole,
            whole,
            pl.BlockSpec((D, D), lambda i: (0, 4)),
            pl.BlockSpec((D, D), lambda i: (0, 5 + i % 4)),
            pl.BlockSpec((D, D), lambda i: (i % 4, 0)),
            pl.BlockSpec(vec_rows.shape, lambda i: (0, 0)),
        ],
        out_specs=[
            whole,
            whole,
            whole,
            pl.BlockSpec((shards, rows_each, D), lambda i: (0, jnp.maximum(i - 4, 0), 0)),
            pl.BlockSpec((D, D), lambda i: (jnp.maximum(i - 4, 0), 0)),
            pl.BlockSpec((D, D), lambda i: (0, 0)),
            pl.BlockSpec((24, D), lambda i: (0, 0)),
        ],
        out_shape=[
            jax.ShapeDtypeStruct((rows, D), bf16),
            jax.ShapeDtypeStruct((rows, D), f32),
            jax.ShapeDtypeStruct((rows, D), bf16),
            jax.ShapeDtypeStruct((shards, 4 * rows_each, D), bf16),
            jax.ShapeDtypeStruct((FF, D), bf16),
            jax.ShapeDtypeStruct((D, D), bf16),
            jax.ShapeDtypeStruct((24, D), f32),
        ],
        scratch_shapes=[
            pltpu.VMEM((rows, D), bf16),
            pltpu.VMEM((rows, D), f32),
            pltpu.VMEM((rows, 128), f32),
            pltpu.VMEM((rows, D), f32),
            pltpu.VMEM((4, rows, D), bf16),
            pltpu.VMEM((4, rows, D), bf16),
            pltpu.VMEM((rows, D), f32),
            pltpu.VMEM((rows, D), bf16),
            pltpu.VMEM((rows, D), bf16),
            pltpu.VMEM((rows, D), bf16),
        ],
        compiler_params=pltpu.CompilerParams(vmem_limit_bytes=58 << 20),
        cost_estimate=pl.CostEstimate(flops=54 * rows * D * D, bytes_accessed=30 << 20, transcendentals=0),
    )(mixed, one, cotangent, wide_full, wide_full, narrow_full, vec_rows)


MESH_ID = pl.DeviceIdType.MESH
UNIT = 384
HALF = 384


def peers_of(lanes):
    rep, shard = lax.axis_index("rep"), lax.axis_index("shard")
    x, y, z = rep % 2, (rep // 2) % 2, rep // 4
    base = rep - z * 4
    others = [(base + 4 * ((z + k) % lanes), shard) for k in range(1, lanes)]
    first = rep + 1 - 2 * x
    second = rep + 2 - 4 * y
    return rep, shard, x, y, z, (rep, 1 - shard), (first, shard), (second, shard), others


def enter_barrier(lanes):
    _, _, _, _, _, sibling, first, second, others = peers_of(lanes)
    barrier = pltpu.get_barrier_semaphore()
    for peer in [sibling, first, second] + others:
        pl.semaphore_signal(barrier, inc=1, device_id=peer, device_id_type=MESH_ID)
    pl.semaphore_wait(barrier, 2 + lanes)


def aligned(value, by=16):
    return pl.multiple_of(value, by)


def remote_copy(sems, index, source, target, peer):
    return pltpu.make_async_remote_copy(
        src_ref=source,
        dst_ref=target,
        send_sem=sems[0].at[index],
        recv_sem=sems[1].at[index],
        device_id=peer,
        device_id_type=MESH_ID,
    )


def unit_scratch(mode, lanes):
    bf16 = jnp.bfloat16
    block = UNIT // (2 * lanes)
    shapes = [pltpu.VMEM((UNIT, D), bf16), pltpu.VMEM((block, HALF), bf16)]
    if mode != "gather":
        shapes += [
            pltpu.VMEM((UNIT, D), bf16),
            pltpu.VMEM((UNIT // 2, D), bf16),
            pltpu.VMEM((UNIT // 2, HALF), bf16),
            pltpu.VMEM((lanes, block, HALF), bf16),
        ]
    return shapes + [
        pltpu.SemaphoreType.DMA((5 + 2 * lanes,)),
        pltpu.SemaphoreType.DMA((5 + 2 * lanes,)),
        pltpu.SemaphoreType.DMA((3,)),
    ]


def unit_places(x_first, lanes):
    rep, shard, x, y, z, sibling, peer_x, peer_y, others = peers_of(lanes)
    here_a, here_b = (x, y) if x_first else (y, x)
    peer_a, peer_b = (peer_x, peer_y) if x_first else (peer_y, peer_x)
    return shard, z, here_a, here_b, sibling, peer_a, peer_b, others


def scatter_steps(term, row, scratch, x_first, lanes, block_out):
    got, block_ref, acc, got_a, got_b, got_z = scratch[:6]
    sems, local_sem = scratch[-3:-1], scratch[-1]
    shard, z, here_a, here_b, sibling, peer_a, peer_b, others = unit_places(x_first, lanes)
    half_rows, block = UNIT // 2, UNIT // (2 * lanes)
    mine_a = aligned(here_a * half_rows)
    mine_cols = pl.ds(aligned(here_b * HALF, 128), HALF)
    their_cols = pl.ds(aligned((1 - here_b) * HALF, 128), HALF)
    core = remote_copy(sems, 0, term.at[1 - shard, pl.ds(row, UNIT)], got, sibling)
    load = pltpu.make_async_copy(term.at[shard, pl.ds(row, UNIT)], acc, local_sem.at[0])
    to_a = remote_copy(sems, 1, acc.at[pl.ds(aligned((1 - here_a) * half_rows), half_rows)], got_a, peer_a)
    to_b = remote_copy(sems, 2, acc.at[pl.ds(mine_a, half_rows), their_cols], got_b, peer_b)
    to_z = [
        remote_copy(
            sems, 5 + k, acc.at[pl.ds(aligned(mine_a + ((z + k + 1) % lanes) * block), block), mine_cols],
            got_z.at[z], peer,
        )
        for k, peer in enumerate(others)
    ]
    f32, bf16 = jnp.float32, jnp.bfloat16

    def start():
        core.start()
        load.start()

    def step_a():
        load.wait()
        core.wait()

        def body(i, carry):
            at = pl.ds(aligned(i * block), block)
            acc[at, :] = acc[at, :] + got[at, :]
            return carry

        lax.fori_loop(0, UNIT // block, body, 0, unroll=True)
        to_a.start()

    def step_b():
        to_a.wait()

        def body(i, carry):
            at = pl.ds(aligned(mine_a + i * block), block)
            acc[at, :] = acc[at, :] + got_a[pl.ds(aligned(i * block), block), :]
            return carry

        lax.fori_loop(0, half_rows // block, body, 0, unroll=True)
        to_b.start()

    def step_z():
        to_b.wait()

        def body(i, carry):
            at = pl.ds(aligned(mine_a + i * block), block)
            acc[at, mine_cols] = acc[at, mine_cols] + got_b[pl.ds(aligned(i * block), block), :]
            return carry

        lax.fori_loop(0, half_rows // block, body, 0, unroll=True)
        for copy in to_z:
            copy.start()

    def step_own():
        for copy in to_z:
            copy.wait()
        total = acc[pl.ds(aligned(mine_a + z * block), block), mine_cols].astype(f32)
        for k in range(1, lanes):
            total = total + got_z[(z + k) % lanes].astype(f32)
        block_ref[...] = total.astype(bf16)
        if block_out is not None:
            block_out[...] = total.astype(bf16)

    return [start, step_a, step_b, step_z, step_own]


def gather_steps(block_in, sum_out, scratch, x_first, lanes, entire):
    full, block_ref = scratch[:2]
    sems, local_sem = scratch[-3:-1], scratch[-1]
    shard, z, here_a, here_b, sibling, peer_a, peer_b, others = unit_places(x_first, lanes)
    half_rows, block = UNIT // 2, UNIT // (2 * lanes)
    mine_a = aligned(here_a * half_rows)
    mine_cols = pl.ds(aligned(here_b * HALF, 128), HALF)
    mine_z = full.at[pl.ds(aligned(mine_a + z * block), block), mine_cols]
    mine_half = full.at[pl.ds(mine_a, half_rows), mine_cols]
    all_z = [remote_copy(sems, 5 + lanes + k, mine_z, mine_z, peer) for k, peer in enumerate(others)]
    all_b = remote_copy(sems, 3, mine_half, mine_half, peer_b)
    mine_all = full.at[pl.ds(mine_a, half_rows)]
    all_a = remote_copy(sems, 4, mine_all, mine_all, peer_a)
    store = pltpu.make_async_copy(full if entire else mine_all, sum_out, local_sem.at[1])

    def start():
        source = block_ref if block_in is None else block_in
        full[pl.ds(aligned(mine_a + z * block), block), mine_cols] = source[...]
        for copy in all_z:
            copy.start()

    def step_b():
        for copy in all_z:
            copy.wait()
        all_b.start()

    def step_a():
        all_b.wait()
        all_a.start()

    def step_store():
        (all_a if entire else all_b).wait()
        store.start()

    return [start, step_b] + [step_a] * entire + [step_store, store.wait]


def joined_steps(scatter, gather):
    own, begin = scatter[-1], gather[0]

    def both():
        own()
        begin()

    return scatter[:-1] + [both] + gather[1:]


def small_scratch(shape, lanes):
    return [
        pltpu.VMEM((3,) + shape, jnp.float32),
        pltpu.VMEM((3,) + shape, jnp.float32),
        pltpu.VMEM((lanes,) + shape, jnp.float32),
        pltpu.SemaphoreType.DMA((3 + lanes,)),
        pltpu.SemaphoreType.DMA((3 + lanes,)),
    ]


def small_steps(term_ref, sum_ref, scratch, lanes):
    held, got, got_z = scratch[:3]
    sems = scratch[3:]
    rep, shard, x, y, z, sibling, peer_x, peer_y, others = peers_of(lanes)
    core = remote_copy(sems, 0, term_ref.at[1 - shard], got.at[0], sibling)
    to_x = remote_copy(sems, 1, held.at[0], got.at[1], peer_x)
    to_y = remote_copy(sems, 2, held.at[1], got.at[2], peer_y)
    to_z = [remote_copy(sems, 3 + k, held.at[2], got_z.at[z], peer) for k, peer in enumerate(others)]

    def step_x():
        core.wait()
        held[0] = term_ref[shard] + got[0]
        to_x.start()

    def step_y():
        to_x.wait()
        held[1] = held[0] + got[1]
        to_y.start()

    def step_z():
        to_y.wait()
        held[2] = held[1] + got[2]
        got_z[z] = held[2]
        for copy in to_z:
            copy.start()

    def step_end():
        for copy in to_z:
            copy.wait()
        total = got_z[0]
        for k in range(1, lanes):
            total = total + got_z[k]
        sum_ref[...] = total

    return [core.start, step_x, step_y, step_z, step_end]


class Traffic:
    def __init__(self, items, lanes, entire, terms=(), blocks=None, small=None):
        self.items, self.lanes, self.entire, self.terms = items, lanes, entire, list(terms)
        self.blocks, self.small = blocks, small
        self.n_scatter = sum(item[0] == "scatter" for item in items)
        summed = [item for item in items if item[0] != "scatter"]
        self.n_x = len(summed) if entire else sum(item[1] for item in summed)
        self.n_y = len(summed) - self.n_x

    def operands(self):
        return self.terms + [x for x in (self.blocks, self.small) if x is not None]

    def in_specs(self):
        vmem = pl.BlockSpec(memory_space=pltpu.VMEM)
        return [pl.BlockSpec(memory_space=pl.ANY)] * len(self.terms) + [vmem] * (
            (self.blocks is not None) + (self.small is not None)
        )

    def outputs(self):
        vmem, anywhere = pl.BlockSpec(memory_space=pltpu.VMEM), pl.BlockSpec(memory_space=pl.ANY)
        shape, bf16 = jax.ShapeDtypeStruct, jnp.bfloat16
        found = []
        if self.n_scatter:
            found.append((vmem, shape((self.n_scatter, UNIT // (2 * self.lanes), HALF), bf16)))
        for count in (self.n_x, self.n_y):
            if count:
                found.append((anywhere, shape((count, UNIT if self.entire else UNIT // 2, D), bf16)))
        if self.small is not None:
            found.append((vmem, shape(self.small.shape[1:], jnp.float32)))
        return found

    def out_specs(self):
        return [spec for spec, _ in self.outputs()]

    def out_shape(self):
        return [shape for _, shape in self.outputs()]

    def scratch(self):
        shapes = []
        for item in self.items:
            shapes += unit_scratch(item[0], self.lanes)
        if self.small is not None:
            shapes += small_scratch(self.small.shape[1:], self.lanes)
        return shapes

    def unpack(self, outs):
        outs = list(outs)
        blocks = outs.pop(0) if self.n_scatter else None
        halves = [outs.pop(0) if count else None for count in (self.n_x, self.n_y)]
        return blocks, halves, outs.pop(0) if self.small is not None else None

    def steps(self, ins, outs, scratch):
        ins, scratch = list(ins), list(scratch)
        terms = [ins.pop(0) for _ in self.terms]
        blocks = ins.pop(0) if self.blocks is not None else None
        small = ins.pop(0) if self.small is not None else None
        block_out, halves, small_out = self.unpack(outs)
        found = []
        n_block, n_in, n_half = 0, 0, [0, 0]
        for mode, x_first, which, row in self.items:
            count = len(unit_scratch(mode, self.lanes))
            mine, scratch = scratch[:count], scratch[count:]
            scatter, gather = [], []
            if mode != "gather":
                target = block_out.at[n_block] if mode == "scatter" else None
                scatter = scatter_steps(terms[which], row, mine, x_first, self.lanes, target)
                n_block += mode == "scatter"
            if mode != "scatter":
                source = None
                if mode == "gather":
                    source = blocks.at[n_in]
                    n_in += 1
                kind = 0 if self.entire or x_first else 1
                gather = gather_steps(
                    source, halves[kind].at[n_half[kind]], mine, x_first, self.lanes, self.entire
                )
                n_half[kind] += 1
            found.append(joined_steps(scatter, gather) if mode == "both" else scatter + gather)
        if small is not None:
            found.append(small_steps(small, small_out, scratch, self.lanes))
        return found


def traffic_kernel(traffic, order, *refs):
    n_in, n_out = len(traffic.in_specs()), len(traffic.out_specs())
    steps = traffic.steps(refs[:n_in], refs[n_in : n_in + n_out], refs[n_in + n_out :])
    enter_barrier(traffic.lanes)
    for which, step in order:
        steps[which][step]()


def run_traffic(traffic, order, collective_id):
    return pl.pallas_call(
        partial(traffic_kernel, traffic, order),
        in_specs=traffic.in_specs(),
        out_specs=traffic.out_specs(),
        out_shape=traffic.out_shape(),
        scratch_shapes=traffic.scratch(),
        compiler_params=pltpu.CompilerParams(
            collective_id=collective_id, has_side_effects=True, vmem_limit_bytes=58 << 20
        ),
    )(*traffic.operands())


REST = tuple(("wide", i) for i in range(3, 12)) + tuple(("narrow", i) for i in range(4))


def meet_sibling():
    rep, shard = lax.axis_index("rep"), lax.axis_index("shard")
    barrier = pltpu.get_barrier_semaphore()
    pl.semaphore_signal(barrier, inc=1, device_id=(rep, 1 - shard), device_id_type=MESH_ID)
    pl.semaphore_wait(barrier, 1)


def share(index, source, target, sems):
    rep, shard = lax.axis_index("rep"), lax.axis_index("shard")
    local = pltpu.make_async_copy(source, target, sems[2].at[index])
    return local, remote_copy(sems[:2], index, source, target, (rep, 1 - shard))


def first_kernel(wide_ref, vec_ref, wide_out, vec_out, held, held_vec, *sems):
    step = pl.program_id(0)
    shard = lax.axis_index("shard")
    rows = pl.ds(aligned(shard * UNIT), UNIT)

    def wide_copies(unit):
        return share(unit, held.at[unit], wide_out.at[rows, pl.ds(aligned(unit * D, 128), D)], sems)

    def vec_copies():
        return share(3, held_vec, vec_out.at[rows], sems)

    @pl.when(step == 0)
    def _():
        meet_sibling()
        held_vec[...] = vec_ref[...].astype(jnp.bfloat16)
        for copy in vec_copies():
            copy.start()

    held[step] = wide_ref[...].astype(jnp.bfloat16)
    for copy in wide_copies(step):
        copy.start()

    @pl.when(step == 2)
    def _():
        for copies in [wide_copies(unit) for unit in range(3)] + [vec_copies()]:
            for copy in copies:
                copy.wait()


def gather_first(wide_master, vec_master):
    bf16 = jnp.bfloat16
    return pl.pallas_call(
        first_kernel,
        grid=(3,),
        in_specs=[
            pl.BlockSpec((UNIT, D), lambda i: (0, i)),
            pl.BlockSpec(vec_master.shape, lambda i: (0, 0)),
        ],
        out_specs=[pl.BlockSpec(memory_space=pl.ANY)] * 2,
        out_shape=[
            jax.ShapeDtypeStruct((D, 3 * D), bf16),
            jax.ShapeDtypeStruct((D, vec_master.shape[1]), bf16),
        ],
        scratch_shapes=[pltpu.VMEM((3, UNIT, D), bf16), pltpu.VMEM(vec_master.shape, bf16)]
        + [pltpu.SemaphoreType.DMA((4,))] * 3,
        compiler_params=pltpu.CompilerParams(
            collective_id=3, has_side_effects=True, vmem_limit_bytes=40 << 20
        ),
    )(wide_master, vec_master)


def rest_scratch():
    count = len(REST)
    return [
        pltpu.VMEM((count, UNIT, D), jnp.float32),
        pltpu.VMEM((count, UNIT, D), jnp.bfloat16),
        pltpu.SemaphoreType.DMA((count,)),
    ] + [pltpu.SemaphoreType.DMA((count,))] * 3


def gather_rest(pair, wide_ref, narrow_ref, wide_out, narrow_out, scratch):
    raw, held, load_sem = scratch[:3]
    sems = scratch[3:]
    shard = lax.axis_index("shard")
    loads, copies = [], []
    for k, (kind, index) in enumerate(REST):
        if kind == "wide":
            source = wide_ref.at[:, pl.ds(index * D, D)]
            target = wide_out.at[pl.ds(aligned(shard * UNIT), UNIT), pl.ds((index - 3) * D, D)]
        else:
            source = narrow_ref.at[pl.ds(index * UNIT, UNIT)]
            target = narrow_out.at[pl.ds(aligned(shard * (FF // 2) + index * UNIT), UNIT)]
        loads.append(pltpu.make_async_copy(source, raw.at[k], load_sem.at[k]))
        copies.append(share(k, held.at[k], target, sems))

    @pl.when(pair == 0)
    def _():
        meet_sibling()
        for load in loads:
            load.start()

    for turn in range(1, 5):

        @pl.when(pair == turn)
        def _():
            for k in range(4 * turn - 4, min(4 * turn, len(REST))):
                loads[k].wait()
                held[k] = raw[k].astype(jnp.bfloat16)
                for copy in copies[k]:
                    copy.start()

    @pl.when(pair == D // 128 - 1)
    def _():
        for pairs in copies:
            for copy in pairs:
                copy.wait()


def backward_kernel(causal, traffic, table, factor, *refs):
    refs = list(refs)
    take = lambda count: [refs.pop(0) for _ in range(count)]
    mask_ref, q_ref, k_ref, v_ref, m_ref, x_ref, lse_ref, left_q_ref, up_ref, wq_ref, wk_ref, wv_ref = take(12)
    if not causal:
        left_k_ref, wo_ref, res_ref, mixo_ref, vec_ref = take(5)
    traffic_in = take(len(traffic.in_specs()) if traffic else 0)
    tq_ref, tk_ref, tv_ref, pair_sums_ref, grad_ref = take(5)
    if not causal:
        encg_ref, gmix_ref, to_ref, norm_sums_ref = take(4)
    traffic_out = take(len(traffic.out_specs()) if traffic else 0)
    qm_ref, mm_ref, qt_ref, mt_ref, col_ref, acc_ref, dkt_ref, dvt_ref, total_ref, up_sem = take(10)
    if not causal:
        total_k_ref, low_ref = take(2)
    bf16, f32 = jnp.bfloat16, jnp.float32
    rows, keys = q_ref.shape[0], k_ref.shape[0]
    pair = pl.program_id(0)
    step, tile = (BLK, BLK) if causal else (2 * BLK, 2 * BLK)
    slot = [0]
    if traffic:
        steps = traffic.steps(traffic_in, traffic_out, refs)

        @pl.when(pair == 0)
        def _():
            enter_barrier(traffic.lanes)

    def hook():
        if traffic:
            for at_pair in range(D // 128):
                todo = table.get((at_pair, slot[0]), ())
                if todo:

                    @pl.when(pair == at_pair)
                    def _():
                        for which, index in todo:
                            steps[which][index]()

        slot[0] += 1

    def each(count, size, body):
        def run(r, carry):
            body(pl.ds(pl.multiple_of(r * size, size), size))
            return carry

        lax.fori_loop(0, count // size, run, 0, unroll=True)

    hook()

    @pl.when(pair == 0)
    def _():
        load = pltpu.make_async_copy(up_ref, total_ref, up_sem)
        load.start()
        load.wait()
        if not causal:
            total_k_ref[...] = jnp.zeros_like(total_k_ref)

    masks = head_masks(rows)
    masks_k = head_masks(tile)
    queries, grads = q_ref[...], m_ref[...]
    qt_ref[...] = queries.T
    mt_ref[...] = grads.T
    product = grads.astype(f32) * x_ref[...].astype(f32)
    lse = lse_ref[0].T
    for head in range(2):
        qm_ref[head] = keep(masks[head], queries)
        mm_ref[head] = keep(masks[head], grads)
        centre = jnp.sum(keep(masks[head], product), axis=1, keepdims=True)
        col_ref[head] = jnp.broadcast_to(centre, (rows, 128))
        col_ref[2 + head] = jnp.broadcast_to(lse[:, head : head + 1], (rows, 128))
    if causal:
        below = lax.broadcasted_iota(jnp.int32, (BLK, BLK), 0) >= lax.broadcasted_iota(
            jnp.int32, (BLK, BLK), 1
        )

    def widen(column):
        return jnp.concatenate([column] * (tile // 128), axis=1)

    def level_of(head, j, begin, end):
        level = col_ref[2 + head, begin:end]
        if not causal:
            return level
        pieces = [level[:BLK]] if begin == j * BLK else []
        for i in range(begin // BLK + len(pieces), end // BLK):
            off = jnp.where(mask_ref[0, i, j] > 0, 0.0, -masked_score)
            pieces.append(level[i * BLK - begin : (i + 1) * BLK - begin] + off)
        return jnp.concatenate(pieces, axis=0) if len(pieces) > 1 else pieces[0]

    for j in range(keys // tile):
        key_rows = slice(j * tile, (j + 1) * tile)
        key, value = k_ref[key_rows, :], v_ref[key_rows, :]
        key_masked = [keep(mask, key) for mask in masks_k]
        total_k, total_v = [None, None], [None, None]
        cuts = (j * tile, rows) if causal else tuple(range(0, rows + 1, step))
        for begin, end in zip(cuts[:-1], cuts[1:]):
            here = slice(begin, end)
            hook()
            for head in range(2):
                scores = rows_dot_t(qm_ref[head, here, :], key)
                prob_grad = rows_dot_t(mm_ref[head, here, :], value)
                scores = scores * SCALE2 - widen(level_of(head, j, begin, end))
                if causal:
                    top = jnp.where(below, scores[:BLK], masked_score)
                    scores = top if end == begin + BLK else jnp.concatenate([top, scores[BLK:]], axis=0)
                probs = jnp.exp2(scores)
                score_grad = (probs * (prob_grad - widen(col_ref[head, here]))).astype(bf16)
                probs = probs.astype(bf16)
                part = slice(head * HD, (head + 1) * HD)
                add_v = rows_dot(mt_ref[part, here], probs)
                add_k = rows_dot(qt_ref[part, here], score_grad)
                total_v[head] = add_v if total_v[head] is None else total_v[head] + add_v
                total_k[head] = add_k if total_k[head] is None else total_k[head] + add_k
                add_q = rows_dot(score_grad, key_masked[head])
                if j == 0 and head == 0:
                    acc_ref[here, :] = add_q
                else:
                    acc_ref[here, :] += add_q
        for head in range(2):
            part = slice(head * HD, (head + 1) * HD)
            dkt_ref[part, key_rows] = (total_k[head] * FACTOR).astype(bf16)
            dvt_ref[part, key_rows] = total_v[head].astype(bf16)
    hook()
    grad_q = (acc_ref[...] * FACTOR).astype(bf16)
    grad_qt = grad_q.T
    pair_sums_ref[0:1, :] = row_total(grad_q.astype(f32))
    pair_sums_ref[1:2, :] = jnp.sum(dvt_ref[...].astype(f32), axis=1, keepdims=True).T

    def put(target, transposed):
        target[...] = (transposed * factor).T.astype(bf16)

    grad_k, grad_v = dkt_ref[...].T, dvt_ref[...].T
    if causal:
        joined = jnp.concatenate([grad_qt, dkt_ref[...], dvt_ref[...]], axis=0)
        found = rows_dot(joined, left_q_ref[...])
        put(tq_ref, found[:128])
        put(tk_ref, found[128:256])
        put(tv_ref, found[256:])
        hook()
        weights = jnp.concatenate([wq_ref[...], wk_ref[...], wv_ref[...]], axis=1)
        total_ref[...] += rows_dot_t(jnp.concatenate([grad_q, grad_k, grad_v], axis=1), weights)
        hook()

        @pl.when(pair == D // 128 - 1)
        def _():
            grad_ref[...] = total_ref[...].astype(bf16)
    else:
        put(tq_ref, rows_dot(grad_qt, left_q_ref[...]))
        total_ref[...] += rows_dot_t(grad_q, wq_ref[...])
        hook()
        found = rows_dot(jnp.concatenate([dkt_ref[...], dvt_ref[...]], axis=0), left_k_ref[...])
        put(tk_ref, found[:128])
        put(tv_ref, found[128:])
        hook()
        weights = jnp.concatenate([wk_ref[...], wv_ref[...]], axis=1)
        total_k_ref[...] += rows_dot_t(jnp.concatenate([grad_k, grad_v], axis=1), weights)
        hook()

        @pl.when(pair == D // 128 - 1)
        def _():
            encg_ref[...] = total_k_ref[...].astype(bf16)
            norm_sums_ref[...] = jnp.zeros_like(norm_sums_ref)

            def body(at):
                unit, inverse = unit_rows(res_ref[at, :])
                upstream = total_ref[at, :]
                grad = back_rows(upstream, unit, inverse, vec_ref[11:12, :])
                grad_ref[at, :] = grad
                low = grad.astype(bf16)
                low_ref[at, :] = low
                gmix_ref[at, :] = rows_dot_t(low, wo_ref[...]).astype(bf16)
                norm_sums_ref[0:1, :] += row_total(upstream * unit)
                norm_sums_ref[1:2, :] += row_total(upstream)
                norm_sums_ref[2:3, :] += row_total(low.astype(f32))

            each(rows, ROWS, body)
            to_ref[...] = (column_dot(mixo_ref[...], low_ref[...]) * factor).astype(bf16)

    hook()


def attend_backward(
    queries, keys_in, values_in, block_table, causal, mixed, lse, mixed_grad, left_q, upstream, wide_full,
    factor, extra, traffic, table, collective_id,
):
    rows, keys = queries.shape[0], keys_in.shape[0]
    bf16, f32 = jnp.bfloat16, jnp.float32
    first = 0 if causal else 1

    def columns(count):
        return pl.BlockSpec((count, 128), lambda i: (0, i))

    def whole(shape):
        return pl.BlockSpec(shape, lambda i: (0,) * len(shape), pipeline_mode=pl.Buffered(1))

    def weight(unit):
        return pl.BlockSpec((D, 128), lambda i: (0, unit * (D // 128) + i))

    spec_q, spec_k = columns(rows), columns(keys)
    in_specs = [pl.BlockSpec(memory_space=pltpu.SMEM), spec_q, spec_k, spec_k, spec_q, spec_q]
    in_specs += [pl.BlockSpec((1, 8, rows), lambda i: (i, 0, 0)), whole((rows, D)), pl.BlockSpec(memory_space=pl.ANY)]
    in_specs += [weight(first), weight(first + 1), weight(first + 2)]
    operands = [block_table, queries, keys_in, values_in, mixed_grad, mixed, lse, left_q, upstream]
    operands += [wide_full] * 3
    shape = jax.ShapeDtypeStruct
    out_specs = [columns(D)] * 3 + [columns(8), whole((rows, D))]
    out_shape = [shape((D, D), bf16)] * 3 + [shape((8, D), f32), shape((rows, D), bf16 if causal else f32)]
    scratch = [
        pltpu.VMEM((2, rows, 128), bf16),
        pltpu.VMEM((2, rows, 128), bf16),
        pltpu.VMEM((128, rows), bf16),
        pltpu.VMEM((128, rows), bf16),
        pltpu.VMEM((4, rows, 128), f32),
        pltpu.VMEM((rows, 128), f32),
        pltpu.VMEM((128, keys), bf16),
        pltpu.VMEM((128, keys), bf16),
        pltpu.VMEM((rows, D), f32),
        pltpu.SemaphoreType.DMA,
    ]
    if not causal:
        states, resid, mixed_self, vec_rows = extra
        in_specs += [whole((keys, D)), pl.BlockSpec((D, D), lambda i: (0, 0), pipeline_mode=pl.Buffered(1)), whole((rows, D)), whole((rows, D))]
        in_specs += [whole(vec_rows.shape)]
        operands += [states, wide_full, resid, mixed_self, vec_rows]
        out_specs += [whole((keys, D)), whole((rows, D)), whole((D, D)), whole((8, D))]
        out_shape += [shape((keys, D), bf16), shape((rows, D), bf16), shape((D, D), bf16), shape((8, D), f32)]
        scratch += [pltpu.VMEM((keys, D), f32), pltpu.VMEM((rows, D), bf16)]
    params = dict(vmem_limit_bytes=62 << 20)
    if traffic:
        in_specs += traffic.in_specs()
        operands += traffic.operands()
        out_specs += traffic.out_specs()
        out_shape += traffic.out_shape()
        scratch += traffic.scratch()
        params.update(collective_id=collective_id, has_side_effects=True)
    return pl.pallas_call(
        partial(backward_kernel, causal, traffic, table, factor),
        grid=(D // 128,),
        in_specs=in_specs,
        out_specs=out_specs,
        out_shape=out_shape,
        scratch_shapes=scratch,
        compiler_params=pltpu.CompilerParams(**params),
        cost_estimate=pl.CostEstimate(
            flops=(20 if causal else 40) * rows * keys * D, bytes_accessed=4 * queries.size, transcendentals=0
        ),
    )(*operands)


def adam_update(master, first, second, gradient, decay_on, rate):
    first_new = beta_one * first + (1.0 - beta_one) * gradient
    second_new = beta_two * second + (1.0 - beta_two) * gradient * gradient
    first_hat = first_new / (1.0 - beta_one**STEP)
    second_hat = second_new / (1.0 - beta_two**STEP)
    master_new = master - rate * (first_hat / (jnp.sqrt(second_hat) + eps_adam) + decay_on * master)
    return (master_new, first_new, second_new)


def adam_kernel(spans, aliased, table_ref, *refs):
    step = pl.program_id(0)
    count = 1 + max(span[0] for span in spans)
    sums = refs[:count]
    masters = refs[count : count + 6]
    outs = refs[count + 6 + aliased :]

    def update(sum_ref, master, first, second, grad, new, first_new, second_new, copy):
        def body(r, carry):
            at = pl.ds(pl.multiple_of(r * 32, 32), 32)
            gradient = sum_ref[0, at, :].astype(jnp.float32)
            grad[at, :] = gradient
            value, one, two = adam_update(
                master[at, :], first[at, :], second[at, :], gradient, weight_decay, learn_rate
            )
            new[at, :] = value
            first_new[at, :] = one
            second_new[at, :] = two
            copy[at, :] = value.astype(jnp.bfloat16)
            return carry

        lax.fori_loop(0, UNIT // 64, body, 0, unroll=3)

    for which, begin, end, wide in spans:

        @pl.when((step >= begin) & (step < end))
        def _():
            if wide:
                update(sums[which], *masters[:3], *outs[:5])
            else:
                update(sums[which], *masters[3:], *outs[5:])


def adam_halves(parts, x, y, wide, narrow, before):
    spans, starts, wides, wide_halves, narrow_rows = [], [], [], [], []
    step = 0
    for which, (array, names, by_x, own) in enumerate(parts):
        starts.append(step)
        here = x if by_x else y
        entire = array.shape[1] == UNIT
        for k, (kind, index) in enumerate([n for n in names for _ in range(1 + entire)]):
            half = k % 2 if entire else here if own else 1 - here
            is_wide = kind == "wide"
            if spans and spans[-1][0] == which and spans[-1][3] == is_wide:
                spans[-1] = (which, spans[-1][1], step + 1, is_wide)
            else:
                spans.append((which, step, step + 1, is_wide))
            wides.append(index if is_wide else None)
            wide_halves.append(half if is_wide else None)
            narrow_rows.append(None if is_wide else 2 * index + half)
            step += 1

    def filled(values):
        last = next((v for v in values if v is not None), 0)
        found = []
        for v in values:
            last = last if v is None else v
            found.append(jnp.asarray(last, jnp.int32))
        return jnp.stack(found)

    table = jnp.stack([filled(wides), filled(wide_halves), filled(narrow_rows)])
    f32, bf16 = jnp.float32, jnp.bfloat16
    spec_w = pl.BlockSpec((UNIT // 2, D), lambda i, t: (t[1, i], t[0, i]))
    spec_n = pl.BlockSpec((UNIT // 2, D), lambda i, t: (t[2, i], 0))

    def spec_sum(start, array):
        halves = 2 * array.shape[1] // UNIT

        def place(i, t):
            at = jnp.clip(i - start, 0, array.shape[0] * halves - 1)
            return (at // halves, at % halves, 0)

        return pl.BlockSpec((1, UNIT // 2, D), place)

    def shapes(like):
        return [jax.ShapeDtypeStruct(like.shape, f32)] * 4 + [jax.ShapeDtypeStruct(like.shape, bf16)]

    operands = [part[0] for part in parts] + list(wide) + list(narrow)
    in_specs = [spec_sum(start, part[0]) for start, part in zip(starts, parts)]
    in_specs += [spec_w] * 3 + [spec_n] * 3
    aliases = {}
    if before is not None:
        aliases = {1 + len(operands) + i: i for i in range(10)}
        operands += list(before)
        in_specs += [pl.BlockSpec(memory_space=pl.ANY)] * 10
    return pl.pallas_call(
        partial(adam_kernel, tuple(spans), 0 if before is None else 10),
        grid_spec=pltpu.PrefetchScalarGridSpec(
            num_scalar_prefetch=1,
            grid=(step,),
            in_specs=in_specs,
            out_specs=[spec_w] * 5 + [spec_n] * 5,
        ),
        out_shape=shapes(wide[0]) + shapes(narrow[0]),
        input_output_aliases=aliases,
        compiler_params=pltpu.CompilerParams(vmem_limit_bytes=58 << 20),
        cost_estimate=pl.CostEstimate(
            flops=30 * step * UNIT * HALF, bytes_accessed=32 * step * UNIT * HALF, transcendentals=0
        ),
    )(table, *operands)


def matmul(left, right):
    return jnp.dot(left, right, preferred_element_type=jnp.float32)


def matmul_left(left, right):
    return lax.dot_general(
        left, right, (((0,), (0,)), ((), ())), preferred_element_type=jnp.float32
    )


def matmul_right(left, right):
    return lax.dot_general(
        left, right, (((1,), (1,)), ((), ())), preferred_element_type=jnp.float32
    )


def norm_forward(resid, gain, shift):
    average = jnp.mean(resid, axis=-1, keepdims=True)
    centred = resid - average
    inverse = lax.rsqrt(jnp.mean(centred * centred, axis=-1, keepdims=True) + eps_norm)
    normed = centred * inverse
    return normed * gain + shift


def on_device(
    tokens,
    encoder_states,
    cotangent,
    block_mask,
    wide_master,
    narrow_master,
    vec_master,
    wide_first,
    narrow_first,
    vec_first,
    wide_second,
    narrow_second,
    vec_second,
):
    replicas = lax.axis_size("rep")
    shards = lax.axis_size("shard")
    tokens_all = tokens.shape[0] * replicas * shards
    factor = float(tokens_all) ** (-0.5)
    bf16, f32 = jnp.bfloat16, jnp.float32

    def gathered(part):
        return lax.all_gather(part.astype(bf16), "shard", axis=0, tiled=True)

    masters = None
    if shards == 2:
        masters = (wide_master, narrow_master)
        wide_early, vec_full = gather_first(wide_master, vec_master)
    else:
        wide_early, vec_full = gathered(wide_master[:, : 3 * D]), gathered(vec_master)
        wide_late, narrow_full = gathered(wide_master[:, 3 * D :]), gathered(narrow_master)
    vector = vec_full.astype(f32)
    vec_rows = jnp.pad(vector.T, ((0, 24 - vector.shape[1]), (0, 0)))
    found = attend_forward(tokens, tokens, block_mask, wide_early, vec_rows, True, masters)
    mixed_self, totals_self, queries, keys_self, values_self = found[:5]
    if masters is not None:
        wide_late, narrow_full = found[5:]
    resid_one = tokens.astype(f32) + matmul(mixed_self, wide_late[:, :D]) + vector[:, 2]
    normed_one = norm_forward(resid_one, vector[:, 11], vector[:, 14])
    normed_low = normed_one.astype(bf16)
    mixed_cross, totals_cross, cross_queries, cross_keys, cross_values = attend_forward(
        normed_low, encoder_states, block_mask, wide_late, vec_rows, False, None
    )
    output, grad_two, grad_cross_mix, term_in, term_narrow, term_co, sums = center(
        mixed_cross, normed_one, cotangent, wide_late, narrow_full, vec_rows, factor, shards
    )

    def split(term):
        return term.reshape(shards, -1, D)

    lanes = replicas // 4
    carried = shards == 2 and replicas % 4 == 0 and UNIT % (32 * lanes) == 0
    terms = [term_in, split(term_narrow), split(term_co)]
    names = [("wide", 8 + i) for i in range(4)] + [("narrow", i) for i in range(4)] + [("wide", 7)]
    names += [("wide", i) for i in (4, 5, 6, 3, 0, 1, 2)]
    x_first = [i % 2 == 0 for i in range(9)] + [i % 2 == 1 for i in range(4)] + [i % 2 == 1 for i in range(3)]
    spots = [(0, UNIT * i) for i in range(4)] + [(1, UNIT * i) for i in range(4)] + [(2, 0)]
    parts_own, parts_far = [], []

    def item(mode, unit, which=0, row=0):
        return (mode, x_first[unit], which, row)

    def collect(traffic, outs, units):
        blocks, halves, small = traffic.unpack(outs)
        if traffic.entire:
            summed = [names[u] for u, it in zip(units, traffic.items) if it[0] != "scatter"]
            parts_own.append((halves[0], summed, True, True))
            return blocks, small
        for by_x, array in zip((True, False), halves):
            if array is None:
                continue
            mine = [names[u] for u, it in zip(units, traffic.items) if it[0] != "scatter" and it[1] == by_x]
            pairs = [(r, r ^ (1 if by_x else 2)) for r in range(replicas)]
            parts_own.append((array, mine, by_x, True))
            parts_far.append((lax.ppermute(array, "rep", pairs), mine, by_x, False))
        return blocks, small

    traffic = None
    units = list(range(N_BOTH + N_SCATTER))
    if carried:
        items = [item("both" if u < N_BOTH else "scatter", u, *spots[u]) for u in units]
        traffic = Traffic(items, lanes, True, terms)
    found = attend_backward(
        cross_queries, cross_keys, cross_values, block_mask, False, mixed_cross, totals_cross,
        grad_cross_mix, normed_low, grad_two, wide_late, factor,
        (encoder_states, resid_one, mixed_self, vec_rows), traffic, CROSS_TABLE, 1,
    )
    term_cq, term_ck, term_cv, cross_sums, grad_one, enc_grad, grad_self_mix, term_wo, norm_sums = found[:9]
    middle = [split(term) for term in (term_cq, term_ck, term_cv, term_wo)]
    if carried:
        blocks, _ = collect(traffic, found[9:], units)
        units = list(range(N_BOTH, N_BOTH + N_GATHER)) + list(range(9, 9 + N_MIDDLE))
        items = [item("gather", u) for u in units[:N_GATHER]]
        items += [item("scatter", 9 + i, i) for i in range(N_MIDDLE)]
        traffic = Traffic(items, lanes, True, middle[:N_MIDDLE], blocks[:N_GATHER])
    found = attend_backward(
        queries, keys_self, values_self, block_mask, True, mixed_self, totals_self,
        grad_self_mix, tokens, grad_one, wide_early, factor, None, traffic, SELF_TABLE, 2,
    )
    late = [split(term) for term in found[:3]]
    self_sums, in_grad = found[3:5]
    term_vec = jnp.concatenate(
        [
            self_sums[0:2],
            norm_sums[2:3],
            cross_sums[0:2],
            sums[5:11],
            norm_sums[0:1],
            sums[12:14],
            norm_sums[1:2],
            sums[15:],
        ],
        0,
    )
    term_vec = (term_vec * factor).reshape(24, shards, -1).transpose(1, 0, 2)
    wide = (wide_master, wide_first, wide_second)
    narrow = (narrow_master, narrow_first, narrow_second)
    if carried:
        blocks_self, _ = collect(traffic, found[5:], units)
        kept = list(range(N_BOTH + N_GATHER, N_BOTH + N_SCATTER)) + list(range(9, 9 + N_MIDDLE))
        fresh = list(range(N_BOTH + N_SCATTER, 9))
        items = [item("gather", u) for u in kept] + [item("both", u, *spots[u]) for u in fresh]
        others = middle[N_MIDDLE:] + late
        items += [item("both", 9 + N_MIDDLE + i, 3 + i) for i in range(len(others))]
        held = jnp.concatenate([blocks[N_GATHER:], blocks_self], 0)
        traffic = Traffic(items, lanes, False, terms + others, held, term_vec)
        _, vec_sum = collect(
            traffic, run_traffic(traffic, TAIL_ORDER, 0), kept + fresh + list(range(9 + N_MIDDLE, 16))
        )
        rep = lax.axis_index("rep")
        x, y = rep % 2, (rep // 2) % 2
        updated = adam_halves(parts_own, x, y, wide, narrow, None)
        updated = adam_halves(parts_far, x, y, wide, narrow, updated)
    else:
        by_column = late + [middle[3]] + middle[:3] + [terms[2]]
        by_column += [term_in[:, i * (D // shards) : (i + 1) * (D // shards)] for i in range(4)]
        wide_sum = jnp.concatenate([whole_sum(term) for term in by_column], 1).astype(f32)
        narrow_sum = whole_sum(terms[1]).astype(f32)
        vec_sum = lax.psum(lax.psum_scatter(term_vec, "shard", scatter_dimension=0), "rep")
        updated = []
        for gradient, state in ((wide_sum, wide), (narrow_sum, narrow)):
            new, first_new, second_new = adam_update(*state, gradient, weight_decay, learn_rate)
            updated += [gradient, new, first_new, second_new, new.astype(bf16)]
    (
        wide_grad, wide_new, wide_first_new, wide_second_new, wide_copy,
        narrow_grad, narrow_new, narrow_first_new, narrow_second_new, narrow_copy,
    ) = updated
    vec_grad = vec_sum[: vec_master.shape[1]].T
    vec_new, vec_first_new, vec_second_new = adam_update(
        vec_master, vec_first, vec_second, vec_grad, 0.0, vec_rate
    )
    return (
        output,
        in_grad,
        enc_grad,
        wide_grad,
        narrow_grad,
        vec_grad,
        wide_new,
        narrow_new,
        vec_new,
        wide_first_new,
        narrow_first_new,
        vec_first_new,
        wide_second_new,
        narrow_second_new,
        vec_second_new,
        wide_copy,
        narrow_copy,
        vec_new.astype(bf16),
    )


def whole_sum(term):
    return lax.psum(lax.psum_scatter(term, "shard", scatter_dimension=0), "rep")


def solution(mesh):
    in_specs = (
        P(("rep", "shard"), None),
        P(("rep", "shard"), None),
        P(("rep", "shard"), None),
        P(("rep", "shard"), None, None),
        P("shard", None),
        P("shard", None),
        P("shard", None),
        P("shard", None),
        P("shard", None),
        P("shard", None),
        P("shard", None),
        P("shard", None),
        P("shard", None),
    )
    out_specs = (
        P(("rep", "shard"), None),
        P(("rep", "shard"), None),
        P(("rep", "shard"), None),
        P("shard", None),
        P("shard", None),
        P("shard", None),
        P("shard", None),
        P("shard", None),
        P("shard", None),
        P("shard", None),
        P("shard", None),
        P("shard", None),
        P("shard", None),
        P("shard", None),
        P("shard", None),
        P("shard", None),
        P("shard", None),
        P("shard", None),
    )
    return jax.shard_map(
        on_device, mesh=mesh, in_specs=in_specs, out_specs=out_specs, check_vma=False
    )
```

```python
from functools import partial
import math

import jax
import jax.numpy as jnp
from jax import lax
from jax.experimental import pallas as pl
from jax.experimental.pallas import tpu as pltpu
from jax.sharding import PartitionSpec as P

D = 768
H = 12
HD = 64
FF = 3072
LEN = 1024
BLK = 256
STEP = 4


eps_norm = 1e-05
eps_adam = 1e-08
beta_one = 0.5
beta_two = 0.5
learn_rate = 0.03
vec_rate = 0.25
weight_decay = 0.1
masked_score = -1e30
FACTOR = HD ** (-0.5)
SCALE2 = FACTOR / math.log(2.0)
N_BOTH = 3
N_SCATTER = 6
N_GATHER = 2
N_MIDDLE = 2


CROSS_TABLE = {
    (0, 0): ((0, 0), (1, 0), (2, 0), (3, 0)),
    (0, 6): ((0, 1), (1, 1), (2, 1), (3, 1)),
    (1, 6): ((0, 2), (1, 2), (2, 2), (3, 2)),
    (1, 9): ((4, 0), (5, 0), (6, 0), (7, 0)),
    (2, 3): ((0, 3), (1, 3), (2, 3), (3, 3), (4, 1), (5, 1), (6, 1), (7, 1)),
    (3, 3): ((0, 4), (1, 4), (2, 4), (3, 4), (4, 2), (5, 2), (6, 2), (7, 2)),
    (3, 6): ((8, 0),),
    (3, 9): ((8, 1),),
    (4, 0): ((0, 5), (1, 5), (2, 5), (4, 3), (5, 3), (6, 3), (7, 3)),
    (4, 6): ((8, 2),),
    (4, 9): ((0, 6), (1, 6), (2, 6)),
    (5, 0): ((4, 4), (5, 4), (6, 4), (7, 4), (8, 3)),
    (5, 6): ((1, 7), (8, 4)),
    (5, 9): ((0, 7), (1, 8), (2, 7), (0, 8), (2, 8)),
}


SELF_TABLE = {
    (0, 0): ((0, 0), (1, 0), (2, 0), (3, 0)),
    (0, 5): ((2, 1), (3, 1)),
    (1, 5): ((0, 1), (1, 1)),
    (2, 5): ((0, 2), (1, 2), (2, 2), (3, 2)),
    (4, 5): ((0, 3), (1, 3), (2, 3), (3, 3)),
    (5, 5): ((0, 4), (1, 4), (2, 4), (3, 4)),
}


TAIL_ORDER = (
    (11, 0), (0, 0), (1, 0), (2, 0), (3, 0), (4, 0), (5, 0), (6, 0),
    (7, 0), (6, 1), (11, 1), (7, 1), (6, 2), (7, 2), (8, 0), (9, 0),
    (8, 1), (9, 1), (6, 3), (7, 3), (11, 2), (0, 1), (1, 1), (2, 1),
    (3, 1), (4, 1), (5, 1), (6, 4), (7, 4), (8, 2), (11, 3), (9, 2),
    (10, 0), (0, 2), (1, 2), (2, 2), (3, 2), (4, 2), (5, 2), (6, 5),
    (11, 4), (7, 5), (10, 1), (0, 3), (1, 3), (2, 3), (3, 3), (4, 3),
    (5, 3), (8, 3), (9, 3), (6, 6), (6, 7), (7, 6), (7, 7), (8, 4),
    (9, 4), (10, 2), (10, 3), (8, 5), (9, 5), (10, 4), (8, 6), (9, 6),
    (8, 7), (9, 7), (10, 5), (10, 6), (10, 7),
)


def head_masks(rows):
    first = lax.broadcasted_iota(jnp.int32, (rows, 128), 1) < HD
    return (first, jnp.logical_not(first))


def keep(mask, value):
    return jnp.where(mask, value, jnp.zeros((), value.dtype))


def rows_dot(left, right):
    return jnp.dot(left, right, preferred_element_type=jnp.float32)


def rows_dot_t(left, right):
    return lax.dot_general(
        left, right, (((1,), (1,)), ((), ())), preferred_element_type=jnp.float32
    )


def forward_kernel(causal, carry, *refs):
    mask_ref, left_q_ref, left_k_ref, wq_ref, wk_ref, wv_ref, vec_ref = refs[:7]
    masters, refs = refs[7 : 7 + 2 * carry], refs[7 + 2 * carry :]
    o_ref, lse_ref, q_ref, k_ref, v_ref = refs[:5]
    copies, refs = refs[5 : 5 + 2 * carry], refs[5 + 2 * carry :]
    qm_ref, vt_ref, acc_ref, sum_ref, top_ref = refs[:5]
    rows, keys = q_ref.shape[0], k_ref.shape[0]
    tile = BLK
    bias_q, bias_v = (vec_ref[0:1, :], vec_ref[1:2, :]) if causal else (vec_ref[3:4, :], vec_ref[4:5, :])
    weights = jnp.concatenate([wk_ref[...], wv_ref[...]], axis=1)
    for at in range(0, rows, 2 * BLK):
        here = slice(at, at + 2 * BLK)
        q_ref[here, :] = (rows_dot(left_q_ref[here, :], wq_ref[...]) + bias_q).astype(jnp.bfloat16)
    for at in range(0, keys, 2 * BLK):
        here = slice(at, at + 2 * BLK)
        both = rows_dot(left_k_ref[here, :], weights)
        k_ref[here, :] = both[:, :128].astype(jnp.bfloat16)
        v_ref[here, :] = (both[:, 128:] + bias_v).astype(jnp.bfloat16)
    queries = q_ref[...]
    for head, mask in enumerate(head_masks(rows)):
        qm_ref[head] = keep(mask, queries)
    vt_ref[...] = v_ref[...].T
    if causal:
        below = lax.broadcasted_iota(jnp.int32, (BLK, BLK), 0) <= lax.broadcasted_iota(
            jnp.int32, (BLK, BLK), 1
        )

    def start_of(j):
        return j * tile if causal else 0

    def scores_of(j, head):
        begin = start_of(j)
        scores = rows_dot_t(k_ref[j * tile : (j + 1) * tile, :], qm_ref[head, begin:, :]) * SCALE2
        if causal:
            pieces = [jnp.where(below, scores[:, :BLK], masked_score)]
            for i in range(j + 1, rows // BLK):
                off = jnp.where(mask_ref[0, i, j] > 0, 0.0, masked_score)
                pieces.append(scores[:, (i - j) * BLK : (i - j + 1) * BLK] + off)
            scores = jnp.concatenate(pieces, axis=1)
        return scores

    def add_tile(j, head, scores, shift):
        begin = start_of(j)
        if shift is not None:
            scores = scores - shift[:, begin:]
        probs = jnp.exp2(scores)
        total = jnp.sum(probs, axis=0, keepdims=True)
        mixed = rows_dot(
            vt_ref[head * HD : (head + 1) * HD, j * tile : (j + 1) * tile], probs.astype(jnp.bfloat16)
        )
        if j == 0:
            sum_ref[head : head + 1, :] = total
            acc_ref[head] = mixed
        else:
            sum_ref[head : head + 1, begin:] += total
            acc_ref[head, :, begin:] += mixed

    def finish(shifts):
        both = []
        for head in range(2):
            total = sum_ref[head : head + 1, :]
            lse = jnp.log2(total)
            if shifts is not None:
                lse = lse + shifts[head]
            lse_ref[0, head : head + 1, :] = lse
            both.append(acc_ref[head] * (1.0 / total))
        o_ref[...] = jnp.concatenate(both, axis=0).T.astype(jnp.bfloat16)

    def peaks():
        for head in range(2):
            for j in range(keys // tile):
                peak = jnp.max(scores_of(j, head), axis=0, keepdims=True)
                begin = start_of(j)
                if j == 0:
                    top_ref[head : head + 1, :] = peak
                else:
                    top_ref[head : head + 1, begin:] = jnp.maximum(
                        top_ref[head : head + 1, begin:], peak
                    )
        return [top_ref[0:1, :], top_ref[1:2, :]]

    lse_ref[...] = jnp.zeros_like(lse_ref)
    shifts = peaks() if carry else None
    waiting = []

    def next_tile():
        j, head, scores = waiting.pop(0)
        add_tile(j, head, scores, shifts[head] if carry else None)

    for j in range(keys // tile):
        for head in range(2):
            waiting.append((j, head, scores_of(j, head)))
            if len(waiting) > 1:
                next_tile()
    while waiting:
        next_tile()
    finish(shifts)
    if carry:
        gather_rest(pl.program_id(0), *masters, *copies, refs[5:])
        return
    sums = sum_ref[...]
    usable = jnp.min(jnp.where((sums > 1e-25) & (sums < 1e30), 1, 0))

    @pl.when(usable == 0)
    def _():
        tops = peaks()
        for head in range(2):
            for j in range(keys // tile):
                add_tile(j, head, scores_of(j, head), tops[head])
        finish(tops)


def attend_forward(left_q, left_k, block_table, weights, vec_rows, causal, masters):
    rows, keys = left_q.shape[0], left_k.shape[0]
    first = 0 if causal else 1
    carry = masters is not None
    bf16, f32 = jnp.bfloat16, jnp.float32

    def columns(count):
        return pl.BlockSpec((count, 128), lambda i: (0, i))

    def whole(count):
        return pl.BlockSpec((count, D), lambda i: (0, 0), pipeline_mode=pl.Buffered(1))

    def weight(unit):
        return pl.BlockSpec((D, 128), lambda i: (0, unit * (D // 128) + i))

    anywhere = [pl.BlockSpec(memory_space=pl.ANY)] * 2
    params = dict(vmem_limit_bytes=56 << 20)
    if carry:
        params.update(collective_id=4, has_side_effects=True)
    return pl.pallas_call(
        partial(forward_kernel, causal, carry),
        grid=(D // 128,),
        in_specs=[pl.BlockSpec(memory_space=pltpu.SMEM), whole(rows), whole(keys)]
        + [weight(first), weight(first + 1), weight(first + 2), columns(vec_rows.shape[0])] + anywhere * carry,
        out_specs=[columns(rows), pl.BlockSpec((1, 8, rows), lambda i: (i, 0, 0)), columns(rows)]
        + [columns(keys)] * 2 + anywhere * carry,
        out_shape=[
            jax.ShapeDtypeStruct((rows, D), bf16),
            jax.ShapeDtypeStruct((D // 128, 8, rows), f32),
            jax.ShapeDtypeStruct((rows, D), bf16),
            jax.ShapeDtypeStruct((keys, D), bf16),
            jax.ShapeDtypeStruct((keys, D), bf16),
        ]
        + [jax.ShapeDtypeStruct((D, 9 * D), bf16), jax.ShapeDtypeStruct((FF, D), bf16)] * carry,
        scratch_shapes=[
            pltpu.VMEM((2, rows, 128), bf16),
            pltpu.VMEM((128, keys), bf16),
            pltpu.VMEM((2, HD, rows), f32),
            pltpu.VMEM((2, rows), f32),
            pltpu.VMEM((2, rows), f32),
        ]
        + (rest_scratch() if carry else []),
        compiler_params=pltpu.CompilerParams(**params),
        cost_estimate=pl.CostEstimate(
            flops=(8 if causal else 16) * rows * keys * D, bytes_accessed=4 * left_q.size, transcendentals=0
        ),
    )(block_table, left_q, left_k, weights, weights, weights, vec_rows, *(masters or ()))


ROWS = 256
UNROLL = 4


def gelu_pair(x):
    magnitude = jnp.abs(x)
    bell = jnp.exp2((x * x) * (-0.5 / math.log(2.0)))
    t = 1.0 / (1.0 + (0.3275911 * math.sqrt(0.5)) * magnitude)
    poly = t * (0.127414796 + t * (-0.142248368 + t * (0.7107068705 + t * (-0.7265760135 + t * 0.5307027145))))
    tail = poly * bell
    phi_sum = jnp.where(x >= 0.0, 1.0 - tail, tail)
    return x * phi_sum, phi_sum + x * (bell * (1.0 / math.sqrt(2.0 * math.pi)))


def unit_rows(resid):
    average = jnp.mean(resid, axis=-1, keepdims=True)
    centred = resid - average
    inverse = lax.rsqrt(jnp.mean(centred * centred, axis=-1, keepdims=True) + eps_norm)
    return centred * inverse, inverse


def back_rows(upstream, unit, inverse, gain):
    scaled = upstream * gain
    centred = scaled - jnp.mean(scaled, axis=-1, keepdims=True)
    return inverse * (centred - unit * jnp.mean(scaled * unit, axis=-1, keepdims=True))


def column_dot(left, right):
    return lax.dot_general(left, right, (((0,), (0,)), ((), ())), preferred_element_type=jnp.float32)


def row_total(value):
    return jnp.sum(value, axis=0, keepdims=True)


def center_kernel(
    factor, mix_ref, one_ref, cot_ref, co_ref, win_ref, wout_ref, vec_ref,
    out_ref, two_ref, gmix_ref, tw_ref, tn_ref, tc_ref, sums_ref,
    low_ref, unit_ref, inv_ref, res_ref, act_ref, slope_ref, acc_ref, gffn_ref, bh_ref, gcross_ref,
):
    step = pl.program_id(0)
    rows = mix_ref.shape[0]
    blocks = rows // ROWS

    def vec(i):
        return vec_ref[i : i + 1, :]

    def each(body):
        def run(r, carry):
            body(pl.ds(pl.multiple_of(r * ROWS, ROWS), ROWS))
            return carry

        lax.fori_loop(0, blocks, run, 0, unroll=UNROLL)

    @pl.when(step == 0)
    def _():
        sums_ref[...] = jnp.zeros_like(sums_ref)

        def body(at):
            resid = one_ref[at, :] + rows_dot(mix_ref[at, :], co_ref[...]) + vec(5)
            unit, inverse = unit_rows(resid)
            unit_ref[at, :] = unit
            inv_ref[at, :] = jnp.broadcast_to(inverse, (ROWS, 128))
            normed = unit * vec(12) + vec(15)
            res_ref[at, :] = normed + vec(10)
            low_ref[at, :] = normed.astype(jnp.bfloat16)

        each(body)

    @pl.when(step < 4)
    def _():
        bias = vec_ref[pl.ds(6 + step, 1), :]

        def body(at):
            hidden = rows_dot(low_ref[at, :], win_ref[...]) + bias
            value, slope = gelu_pair(hidden)
            value = value.astype(jnp.bfloat16)
            act_ref[step, at, :] = value
            slope_ref[step, at, :] = slope.astype(jnp.bfloat16)
            res_ref[at, :] += rows_dot(value, wout_ref[...])

        each(body)

    @pl.when(step == 3)
    def _():
        def body(at):
            unit, inverse = unit_rows(res_ref[at, :])
            out_ref[at, :] = (unit * vec(13) + vec(16)).astype(jnp.bfloat16)
            upstream = cot_ref[at, :].astype(jnp.float32)
            grad = back_rows(upstream, unit, inverse, vec(13))
            acc_ref[at, :] = grad
            low = grad.astype(jnp.bfloat16)
            gffn_ref[at, :] = low
            sums_ref[13:14, :] += row_total(upstream * unit)
            sums_ref[16:17, :] += row_total(upstream)
            sums_ref[10:11, :] += row_total(low.astype(jnp.float32))

        each(body)

    @pl.when(step >= 4)
    def _():
        c = step - 4

        def body(at):
            grad = rows_dot_t(gffn_ref[at, :], wout_ref[...]) * slope_ref[c, at, :].astype(jnp.float32)
            low = grad.astype(jnp.bfloat16)
            bh_ref[at, :] = low
            sums_ref[pl.ds(step + 2, 1), :] += row_total(low.astype(jnp.float32))
            acc_ref[at, :] += rows_dot_t(low, win_ref[...])

        each(body)
        tn_ref[...] = (column_dot(act_ref[c], gffn_ref[...]) * factor).astype(jnp.bfloat16)
        rows_each = tw_ref.shape[1]
        for s in range(tw_ref.shape[0]):
            cols = slice(s * rows_each, (s + 1) * rows_each)
            tw_ref[s] = (column_dot(low_ref[:, cols], bh_ref[...]) * factor).astype(jnp.bfloat16)

    @pl.when(step == 7)
    def _():
        def body(at):
            upstream = acc_ref[at, :]
            unit = unit_ref[at, :]
            inverse = inv_ref[at, 0:1]
            grad = back_rows(upstream, unit, inverse, vec(12))
            two_ref[at, :] = grad
            low = grad.astype(jnp.bfloat16)
            gcross_ref[at, :] = low
            gmix_ref[at, :] = rows_dot_t(low, co_ref[...]).astype(jnp.bfloat16)
            sums_ref[12:13, :] += row_total(upstream * unit)
            sums_ref[15:16, :] += row_total(upstream)
            sums_ref[5:6, :] += row_total(low.astype(jnp.float32))

        each(body)
        tc_ref[...] = (column_dot(mix_ref[...], gcross_ref[...]) * factor).astype(jnp.bfloat16)


def center(mixed, one, cotangent, wide_full, narrow_full, vec_rows, factor, shards):
    rows = mixed.shape[0]
    whole = pl.BlockSpec((rows, D), lambda i: (0, 0))
    rows_each = D // shards
    bf16, f32 = jnp.bfloat16, jnp.float32
    return pl.pallas_call(
        partial(center_kernel, factor),
        grid=(8,),
        in_specs=[
            whole,
            whole,
            whole,
            pl.BlockSpec((D, D), lambda i: (0, 4)),
            pl.BlockSpec((D, D), lambda i: (0, 5 + i % 4)),
            pl.BlockSpec((D, D), lambda i: (i % 4, 0)),
            pl.BlockSpec(vec_rows.shape, lambda i: (0, 0)),
        ],
        out_specs=[
            whole,
            whole,
            whole,
            pl.BlockSpec((shards, rows_each, D), lambda i: (0, jnp.maximum(i - 4, 0), 0)),
            pl.BlockSpec((D, D), lambda i: (jnp.maximum(i - 4, 0), 0)),
            pl.BlockSpec((D, D), lambda i: (0, 0)),
            pl.BlockSpec((24, D), lambda i: (0, 0)),
        ],
        out_shape=[
            jax.ShapeDtypeStruct((rows, D), bf16),
            jax.ShapeDtypeStruct((rows, D), f32),
            jax.ShapeDtypeStruct((rows, D), bf16),
            jax.ShapeDtypeStruct((shards, 4 * rows_each, D), bf16),
            jax.ShapeDtypeStruct((FF, D), bf16),
            jax.ShapeDtypeStruct((D, D), bf16),
            jax.ShapeDtypeStruct((24, D), f32),
        ],
        scratch_shapes=[
            pltpu.VMEM((rows, D), bf16),
            pltpu.VMEM((rows, D), f32),
            pltpu.VMEM((rows, 128), f32),
            pltpu.VMEM((rows, D), f32),
            pltpu.VMEM((4, rows, D), bf16),
            pltpu.VMEM((4, rows, D), bf16),
            pltpu.VMEM((rows, D), f32),
            pltpu.VMEM((rows, D), bf16),
            pltpu.VMEM((rows, D), bf16),
            pltpu.VMEM((rows, D), bf16),
        ],
        compiler_params=pltpu.CompilerParams(vmem_limit_bytes=58 << 20),
        cost_estimate=pl.CostEstimate(flops=54 * rows * D * D, bytes_accessed=30 << 20, transcendentals=0),
    )(mixed, one, cotangent, wide_full, wide_full, narrow_full, vec_rows)


MESH_ID = pl.DeviceIdType.MESH
UNIT = 384
HALF = 384


def peers_of(lanes):
    rep, shard = lax.axis_index("rep"), lax.axis_index("shard")
    x, y, z = rep % 2, (rep // 2) % 2, rep // 4
    base = rep - z * 4
    others = [(base + 4 * ((z + k) % lanes), shard) for k in range(1, lanes)]
    first = rep + 1 - 2 * x
    second = rep + 2 - 4 * y
    return rep, shard, x, y, z, (rep, 1 - shard), (first, shard), (second, shard), others


def enter_barrier(lanes):
    _, _, _, _, _, sibling, first, second, others = peers_of(lanes)
    barrier = pltpu.get_barrier_semaphore()
    for peer in [sibling, first, second] + others:
        pl.semaphore_signal(barrier, inc=1, device_id=peer, device_id_type=MESH_ID)
    pl.semaphore_wait(barrier, 2 + lanes)


def aligned(value, by=16):
    return pl.multiple_of(value, by)


def remote_copy(sems, index, source, target, peer):
    return pltpu.make_async_remote_copy(
        src_ref=source,
        dst_ref=target,
        send_sem=sems[0].at[index],
        recv_sem=sems[1].at[index],
        device_id=peer,
        device_id_type=MESH_ID,
    )


def unit_scratch(mode, lanes):
    bf16 = jnp.bfloat16
    block = UNIT // (2 * lanes)
    shapes = [pltpu.VMEM((UNIT, D), bf16), pltpu.VMEM((block, HALF), bf16)]
    if mode != "gather":
        shapes += [
            pltpu.VMEM((UNIT, D), bf16),
            pltpu.VMEM((UNIT // 2, D), bf16),
            pltpu.VMEM((UNIT // 2, HALF), bf16),
            pltpu.VMEM((lanes, block, HALF), bf16),
        ]
    return shapes + [
        pltpu.SemaphoreType.DMA((5 + 2 * lanes,)),
        pltpu.SemaphoreType.DMA((5 + 2 * lanes,)),
        pltpu.SemaphoreType.DMA((3,)),
    ]


def unit_places(x_first, lanes):
    rep, shard, x, y, z, sibling, peer_x, peer_y, others = peers_of(lanes)
    here_a, here_b = (x, y) if x_first else (y, x)
    peer_a, peer_b = (peer_x, peer_y) if x_first else (peer_y, peer_x)
    return shard, z, here_a, here_b, sibling, peer_a, peer_b, others


def scatter_steps(term, row, scratch, x_first, lanes, block_out):
    got, block_ref, acc, got_a, got_b, got_z = scratch[:6]
    sems, local_sem = scratch[-3:-1], scratch[-1]
    shard, z, here_a, here_b, sibling, peer_a, peer_b, others = unit_places(x_first, lanes)
    half_rows, block = UNIT // 2, UNIT // (2 * lanes)
    mine_a = aligned(here_a * half_rows)
    mine_cols = pl.ds(aligned(here_b * HALF, 128), HALF)
    their_cols = pl.ds(aligned((1 - here_b) * HALF, 128), HALF)
    core = remote_copy(sems, 0, term.at[1 - shard, pl.ds(row, UNIT)], got, sibling)
    load = pltpu.make_async_copy(term.at[shard, pl.ds(row, UNIT)], acc, local_sem.at[0])
    to_a = remote_copy(sems, 1, acc.at[pl.ds(aligned((1 - here_a) * half_rows), half_rows)], got_a, peer_a)
    to_b = remote_copy(sems, 2, acc.at[pl.ds(mine_a, half_rows), their_cols], got_b, peer_b)
    to_z = [
        remote_copy(
            sems, 5 + k, acc.at[pl.ds(aligned(mine_a + ((z + k + 1) % lanes) * block), block), mine_cols],
            got_z.at[z], peer,
        )
        for k, peer in enumerate(others)
    ]
    f32, bf16 = jnp.float32, jnp.bfloat16

    def start():
        core.start()
        load.start()

    def step_a():
        load.wait()
        core.wait()

        def body(i, carry):
            at = pl.ds(aligned(i * block), block)
            acc[at, :] = acc[at, :] + got[at, :]
            return carry

        lax.fori_loop(0, UNIT // block, body, 0, unroll=True)
        to_a.start()

    def step_b():
        to_a.wait()

        def body(i, carry):
            at = pl.ds(aligned(mine_a + i * block), block)
            acc[at, :] = acc[at, :] + got_a[pl.ds(aligned(i * block), block), :]
            return carry

        lax.fori_loop(0, half_rows // block, body, 0, unroll=True)
        to_b.start()

    def step_z():
        to_b.wait()

        def body(i, carry):
            at = pl.ds(aligned(mine_a + i * block), block)
            acc[at, mine_cols] = acc[at, mine_cols] + got_b[pl.ds(aligned(i * block), block), :]
            return carry

        lax.fori_loop(0, half_rows // block, body, 0, unroll=True)
        for copy in to_z:
            copy.start()

    def step_own():
        for copy in to_z:
            copy.wait()
        total = acc[pl.ds(aligned(mine_a + z * block), block), mine_cols].astype(f32)
        for k in range(1, lanes):
            total = total + got_z[(z + k) % lanes].astype(f32)
        block_ref[...] = total.astype(bf16)
        if block_out is not None:
            block_out[...] = total.astype(bf16)

    return [start, step_a, step_b, step_z, step_own]


def gather_steps(block_in, sum_out, scratch, x_first, lanes, entire):
    full, block_ref = scratch[:2]
    sems, local_sem = scratch[-3:-1], scratch[-1]
    shard, z, here_a, here_b, sibling, peer_a, peer_b, others = unit_places(x_first, lanes)
    half_rows, block = UNIT // 2, UNIT // (2 * lanes)
    mine_a = aligned(here_a * half_rows)
    mine_cols = pl.ds(aligned(here_b * HALF, 128), HALF)
    mine_z = full.at[pl.ds(aligned(mine_a + z * block), block), mine_cols]
    mine_half = full.at[pl.ds(mine_a, half_rows), mine_cols]
    all_z = [remote_copy(sems, 5 + lanes + k, mine_z, mine_z, peer) for k, peer in enumerate(others)]
    all_b = remote_copy(sems, 3, mine_half, mine_half, peer_b)
    mine_all = full.at[pl.ds(mine_a, half_rows)]
    all_a = remote_copy(sems, 4, mine_all, mine_all, peer_a)
    store = pltpu.make_async_copy(full if entire else mine_all, sum_out, local_sem.at[1])

    def start():
        source = block_ref if block_in is None else block_in
        full[pl.ds(aligned(mine_a + z * block), block), mine_cols] = source[...]
        for copy in all_z:
            copy.start()

    def step_b():
        for copy in all_z:
            copy.wait()
        all_b.start()

    def step_a():
        all_b.wait()
        all_a.start()

    def step_store():
        (all_a if entire else all_b).wait()
        store.start()

    return [start, step_b] + [step_a] * entire + [step_store, store.wait]


def joined_steps(scatter, gather):
    own, begin = scatter[-1], gather[0]

    def both():
        own()
        begin()

    return scatter[:-1] + [both] + gather[1:]


def small_scratch(shape, lanes):
    return [
        pltpu.VMEM((3,) + shape, jnp.float32),
        pltpu.VMEM((3,) + shape, jnp.float32),
        pltpu.VMEM((lanes,) + shape, jnp.float32),
        pltpu.SemaphoreType.DMA((3 + lanes,)),
        pltpu.SemaphoreType.DMA((3 + lanes,)),
    ]


def small_steps(term_ref, sum_ref, scratch, lanes):
    held, got, got_z = scratch[:3]
    sems = scratch[3:]
    rep, shard, x, y, z, sibling, peer_x, peer_y, others = peers_of(lanes)
    core = remote_copy(sems, 0, term_ref.at[1 - shard], got.at[0], sibling)
    to_x = remote_copy(sems, 1, held.at[0], got.at[1], peer_x)
    to_y = remote_copy(sems, 2, held.at[1], got.at[2], peer_y)
    to_z = [remote_copy(sems, 3 + k, held.at[2], got_z.at[z], peer) for k, peer in enumerate(others)]

    def step_x():
        core.wait()
        held[0] = term_ref[shard] + got[0]
        to_x.start()

    def step_y():
        to_x.wait()
        held[1] = held[0] + got[1]
        to_y.start()

    def step_z():
        to_y.wait()
        held[2] = held[1] + got[2]
        got_z[z] = held[2]
        for copy in to_z:
            copy.start()

    def step_end():
        for copy in to_z:
            copy.wait()
        total = got_z[0]
        for k in range(1, lanes):
            total = total + got_z[k]
        sum_ref[...] = total

    return [core.start, step_x, step_y, step_z, step_end]


class Traffic:
    def __init__(self, items, lanes, entire, terms=(), blocks=None, small=None):
        self.items, self.lanes, self.entire, self.terms = items, lanes, entire, list(terms)
        self.blocks, self.small = blocks, small
        self.n_scatter = sum(item[0] == "scatter" for item in items)
        summed = [item for item in items if item[0] != "scatter"]
        self.n_x = len(summed) if entire else sum(item[1] for item in summed)
        self.n_y = len(summed) - self.n_x

    def operands(self):
        return self.terms + [x for x in (self.blocks, self.small) if x is not None]

    def in_specs(self):
        vmem = pl.BlockSpec(memory_space=pltpu.VMEM)
        return [pl.BlockSpec(memory_space=pl.ANY)] * len(self.terms) + [vmem] * (
            (self.blocks is not None) + (self.small is not None)
        )

    def outputs(self):
        vmem, anywhere = pl.BlockSpec(memory_space=pltpu.VMEM), pl.BlockSpec(memory_space=pl.ANY)
        shape, bf16 = jax.ShapeDtypeStruct, jnp.bfloat16
        found = []
        if self.n_scatter:
            found.append((vmem, shape((self.n_scatter, UNIT // (2 * self.lanes), HALF), bf16)))
        for count in (self.n_x, self.n_y):
            if count:
                found.append((anywhere, shape((count, UNIT if self.entire else UNIT // 2, D), bf16)))
        if self.small is not None:
            found.append((vmem, shape(self.small.shape[1:], jnp.float32)))
        return found

    def out_specs(self):
        return [spec for spec, _ in self.outputs()]

    def out_shape(self):
        return [shape for _, shape in self.outputs()]

    def scratch(self):
        shapes = []
        for item in self.items:
            shapes += unit_scratch(item[0], self.lanes)
        if self.small is not None:
            shapes += small_scratch(self.small.shape[1:], self.lanes)
        return shapes

    def unpack(self, outs):
        outs = list(outs)
        blocks = outs.pop(0) if self.n_scatter else None
        halves = [outs.pop(0) if count else None for count in (self.n_x, self.n_y)]
        return blocks, halves, outs.pop(0) if self.small is not None else None

    def steps(self, ins, outs, scratch):
        ins, scratch = list(ins), list(scratch)
        terms = [ins.pop(0) for _ in self.terms]
        blocks = ins.pop(0) if self.blocks is not None else None
        small = ins.pop(0) if self.small is not None else None
        block_out, halves, small_out = self.unpack(outs)
        found = []
        n_block, n_in, n_half = 0, 0, [0, 0]
        for mode, x_first, which, row in self.items:
            count = len(unit_scratch(mode, self.lanes))
            mine, scratch = scratch[:count], scratch[count:]
            scatter, gather = [], []
            if mode != "gather":
                target = block_out.at[n_block] if mode == "scatter" else None
                scatter = scatter_steps(terms[which], row, mine, x_first, self.lanes, target)
                n_block += mode == "scatter"
            if mode != "scatter":
                source = None
                if mode == "gather":
                    source = blocks.at[n_in]
                    n_in += 1
                kind = 0 if self.entire or x_first else 1
                gather = gather_steps(
                    source, halves[kind].at[n_half[kind]], mine, x_first, self.lanes, self.entire
                )
                n_half[kind] += 1
            found.append(joined_steps(scatter, gather) if mode == "both" else scatter + gather)
        if small is not None:
            found.append(small_steps(small, small_out, scratch, self.lanes))
        return found


def traffic_kernel(traffic, order, *refs):
    n_in, n_out = len(traffic.in_specs()), len(traffic.out_specs())
    steps = traffic.steps(refs[:n_in], refs[n_in : n_in + n_out], refs[n_in + n_out :])
    enter_barrier(traffic.lanes)
    for which, step in order:
        steps[which][step]()


def run_traffic(traffic, order, collective_id):
    return pl.pallas_call(
        partial(traffic_kernel, traffic, order),
        in_specs=traffic.in_specs(),
        out_specs=traffic.out_specs(),
        out_shape=traffic.out_shape(),
        scratch_shapes=traffic.scratch(),
        compiler_params=pltpu.CompilerParams(
            collective_id=collective_id, has_side_effects=True, vmem_limit_bytes=58 << 20
        ),
    )(*traffic.operands())


REST = tuple(("wide", i) for i in range(3, 12)) + tuple(("narrow", i) for i in range(4))


def meet_sibling():
    rep, shard = lax.axis_index("rep"), lax.axis_index("shard")
    barrier = pltpu.get_barrier_semaphore()
    pl.semaphore_signal(barrier, inc=1, device_id=(rep, 1 - shard), device_id_type=MESH_ID)
    pl.semaphore_wait(barrier, 1)


def share(index, source, target, sems):
    rep, shard = lax.axis_index("rep"), lax.axis_index("shard")
    local = pltpu.make_async_copy(source, target, sems[2].at[index])
    return local, remote_copy(sems[:2], index, source, target, (rep, 1 - shard))


def first_kernel(wide_ref, vec_ref, wide_out, vec_out, held, held_vec, *sems):
    step = pl.program_id(0)
    shard = lax.axis_index("shard")
    rows = pl.ds(aligned(shard * UNIT), UNIT)

    def wide_copies(unit):
        return share(unit, held.at[unit], wide_out.at[rows, pl.ds(aligned(unit * D, 128), D)], sems)

    def vec_copies():
        return share(3, held_vec, vec_out.at[rows], sems)

    @pl.when(step == 0)
    def _():
        meet_sibling()
        held_vec[...] = vec_ref[...].astype(jnp.bfloat16)
        for copy in vec_copies():
            copy.start()

    held[step] = wide_ref[...].astype(jnp.bfloat16)
    for copy in wide_copies(step):
        copy.start()

    @pl.when(step == 2)
    def _():
        for copies in [wide_copies(unit) for unit in range(3)] + [vec_copies()]:
            for copy in copies:
                copy.wait()


def gather_first(wide_master, vec_master):
    bf16 = jnp.bfloat16
    return pl.pallas_call(
        first_kernel,
        grid=(3,),
        in_specs=[
            pl.BlockSpec((UNIT, D), lambda i: (0, i)),
            pl.BlockSpec(vec_master.shape, lambda i: (0, 0)),
        ],
        out_specs=[pl.BlockSpec(memory_space=pl.ANY)] * 2,
        out_shape=[
            jax.ShapeDtypeStruct((D, 3 * D), bf16),
            jax.ShapeDtypeStruct((D, vec_master.shape[1]), bf16),
        ],
        scratch_shapes=[pltpu.VMEM((3, UNIT, D), bf16), pltpu.VMEM(vec_master.shape, bf16)]
        + [pltpu.SemaphoreType.DMA((4,))] * 3,
        compiler_params=pltpu.CompilerParams(
            collective_id=3, has_side_effects=True, vmem_limit_bytes=40 << 20
        ),
    )(wide_master, vec_master)


def rest_scratch():
    count = len(REST)
    return [
        pltpu.VMEM((count, UNIT, D), jnp.float32),
        pltpu.VMEM((count, UNIT, D), jnp.bfloat16),
        pltpu.SemaphoreType.DMA((count,)),
    ] + [pltpu.SemaphoreType.DMA((count,))] * 3


def gather_rest(pair, wide_ref, narrow_ref, wide_out, narrow_out, scratch):
    raw, held, load_sem = scratch[:3]
    sems = scratch[3:]
    shard = lax.axis_index("shard")
    loads, copies = [], []
    for k, (kind, index) in enumerate(REST):
        if kind == "wide":
            source = wide_ref.at[:, pl.ds(index * D, D)]
            target = wide_out.at[pl.ds(aligned(shard * UNIT), UNIT), pl.ds((index - 3) * D, D)]
        else:
            source = narrow_ref.at[pl.ds(index * UNIT, UNIT)]
            target = narrow_out.at[pl.ds(aligned(shard * (FF // 2) + index * UNIT), UNIT)]
        loads.append(pltpu.make_async_copy(source, raw.at[k], load_sem.at[k]))
        copies.append(share(k, held.at[k], target, sems))

    @pl.when(pair == 0)
    def _():
        meet_sibling()
        for load in loads:
            load.start()

    for turn in range(1, 5):

        @pl.when(pair == turn)
        def _():
            for k in range(4 * turn - 4, min(4 * turn, len(REST))):
                loads[k].wait()
                held[k] = raw[k].astype(jnp.bfloat16)
                for copy in copies[k]:
                    copy.start()

    @pl.when(pair == D // 128 - 1)
    def _():
        for pairs in copies:
            for copy in pairs:
                copy.wait()


def backward_kernel(causal, traffic, table, factor, *refs):
    refs = list(refs)
    take = lambda count: [refs.pop(0) for _ in range(count)]
    mask_ref, q_ref, k_ref, v_ref, m_ref, x_ref, lse_ref, left_q_ref, up_ref, wq_ref, wk_ref, wv_ref = take(12)
    if not causal:
        left_k_ref, wo_ref, res_ref, mixo_ref, vec_ref = take(5)
    traffic_in = take(len(traffic.in_specs()) if traffic else 0)
    tq_ref, tk_ref, tv_ref, pair_sums_ref, grad_ref = take(5)
    if not causal:
        encg_ref, gmix_ref, to_ref, norm_sums_ref = take(4)
    traffic_out = take(len(traffic.out_specs()) if traffic else 0)
    qm_ref, mm_ref, qt_ref, mt_ref, col_ref, acc_ref, dkt_ref, dvt_ref, total_ref, up_sem = take(10)
    if not causal:
        total_k_ref, low_ref = take(2)
    bf16, f32 = jnp.bfloat16, jnp.float32
    rows, keys = q_ref.shape[0], k_ref.shape[0]
    pair = pl.program_id(0)
    step, tile = (BLK, BLK) if causal else (2 * BLK, 2 * BLK)
    slot = [0]
    if traffic:
        steps = traffic.steps(traffic_in, traffic_out, refs)

        @pl.when(pair == 0)
        def _():
            enter_barrier(traffic.lanes)

    def hook():
        if traffic:
            for at_pair in range(D // 128):
                todo = table.get((at_pair, slot[0]), ())
                if todo:

                    @pl.when(pair == at_pair)
                    def _():
                        for which, index in todo:
                            steps[which][index]()

        slot[0] += 1

    def each(count, size, body):
        def run(r, carry):
            body(pl.ds(pl.multiple_of(r * size, size), size))
            return carry

        lax.fori_loop(0, count // size, run, 0, unroll=True)

    hook()

    @pl.when(pair == 0)
    def _():
        load = pltpu.make_async_copy(up_ref, total_ref, up_sem)
        load.start()
        load.wait()
        if not causal:
            total_k_ref[...] = jnp.zeros_like(total_k_ref)

    masks = head_masks(rows)
    masks_k = head_masks(tile)
    queries, grads = q_ref[...], m_ref[...]
    qt_ref[...] = queries.T
    mt_ref[...] = grads.T
    product = grads.astype(f32) * x_ref[...].astype(f32)
    lse = lse_ref[0].T
    for head in range(2):
        qm_ref[head] = keep(masks[head], queries)
        mm_ref[head] = keep(masks[head], grads)
        centre = jnp.sum(keep(masks[head], product), axis=1, keepdims=True)
        col_ref[head] = jnp.broadcast_to(centre, (rows, 128))
        col_ref[2 + head] = jnp.broadcast_to(lse[:, head : head + 1], (rows, 128))
    if causal:
        below = lax.broadcasted_iota(jnp.int32, (BLK, BLK), 0) >= lax.broadcasted_iota(
            jnp.int32, (BLK, BLK), 1
        )

    def widen(column):
        return jnp.concatenate([column] * (tile // 128), axis=1)

    def level_of(head, j, begin, end):
        level = col_ref[2 + head, begin:end]
        if not causal:
            return level
        pieces = [level[:BLK]] if begin == j * BLK else []
        for i in range(begin // BLK + len(pieces), end // BLK):
            off = jnp.where(mask_ref[0, i, j] > 0, 0.0, -masked_score)
            pieces.append(level[i * BLK - begin : (i + 1) * BLK - begin] + off)
        return jnp.concatenate(pieces, axis=0) if len(pieces) > 1 else pieces[0]

    for j in range(keys // tile):
        key_rows = slice(j * tile, (j + 1) * tile)
        key, value = k_ref[key_rows, :], v_ref[key_rows, :]
        key_masked = [keep(mask, key) for mask in masks_k]
        total_k, total_v = [None, None], [None, None]
        cuts = (j * tile, rows) if causal else tuple(range(0, rows + 1, step))
        for begin, end in zip(cuts[:-1], cuts[1:]):
            here = slice(begin, end)
            hook()
            for head in range(2):
                scores = rows_dot_t(qm_ref[head, here, :], key)
                prob_grad = rows_dot_t(mm_ref[head, here, :], value)
                scores = scores * SCALE2 - widen(level_of(head, j, begin, end))
                if causal:
                    top = jnp.where(below, scores[:BLK], masked_score)
                    scores = top if end == begin + BLK else jnp.concatenate([top, scores[BLK:]], axis=0)
                probs = jnp.exp2(scores)
                score_grad = (probs * (prob_grad - widen(col_ref[head, here]))).astype(bf16)
                probs = probs.astype(bf16)
                part = slice(head * HD, (head + 1) * HD)
                add_v = rows_dot(mt_ref[part, here], probs)
                add_k = rows_dot(qt_ref[part, here], score_grad)
                total_v[head] = add_v if total_v[head] is None else total_v[head] + add_v
                total_k[head] = add_k if total_k[head] is None else total_k[head] + add_k
                add_q = rows_dot(score_grad, key_masked[head])
                if j == 0 and head == 0:
                    acc_ref[here, :] = add_q
                else:
                    acc_ref[here, :] += add_q
        for head in range(2):
            part = slice(head * HD, (head + 1) * HD)
            dkt_ref[part, key_rows] = (total_k[head] * FACTOR).astype(bf16)
            dvt_ref[part, key_rows] = total_v[head].astype(bf16)
    hook()
    grad_q = (acc_ref[...] * FACTOR).astype(bf16)
    grad_qt = grad_q.T
    pair_sums_ref[0:1, :] = row_total(grad_q.astype(f32))
    pair_sums_ref[1:2, :] = jnp.sum(dvt_ref[...].astype(f32), axis=1, keepdims=True).T

    def put(target, transposed):
        target[...] = (transposed * factor).T.astype(bf16)

    grad_k, grad_v = dkt_ref[...].T, dvt_ref[...].T
    if causal:
        joined = jnp.concatenate([grad_qt, dkt_ref[...], dvt_ref[...]], axis=0)
        found = rows_dot(joined, left_q_ref[...])
        put(tq_ref, found[:128])
        put(tk_ref, found[128:256])
        put(tv_ref, found[256:])
        hook()
        weights = jnp.concatenate([wq_ref[...], wk_ref[...], wv_ref[...]], axis=1)
        total_ref[...] += rows_dot_t(jnp.concatenate([grad_q, grad_k, grad_v], axis=1), weights)
        hook()

        @pl.when(pair == D // 128 - 1)
        def _():
            grad_ref[...] = total_ref[...].astype(bf16)
    else:
        put(tq_ref, rows_dot(grad_qt, left_q_ref[...]))
        total_ref[...] += rows_dot_t(grad_q, wq_ref[...])
        hook()
        found = rows_dot(jnp.concatenate([dkt_ref[...], dvt_ref[...]], axis=0), left_k_ref[...])
        put(tk_ref, found[:128])
        put(tv_ref, found[128:])
        hook()
        weights = jnp.concatenate([wk_ref[...], wv_ref[...]], axis=1)
        total_k_ref[...] += rows_dot_t(jnp.concatenate([grad_k, grad_v], axis=1), weights)
        hook()

        @pl.when(pair == D // 128 - 1)
        def _():
            encg_ref[...] = total_k_ref[...].astype(bf16)
            norm_sums_ref[...] = jnp.zeros_like(norm_sums_ref)

            def body(at):
                unit, inverse = unit_rows(res_ref[at, :])
                upstream = total_ref[at, :]
                grad = back_rows(upstream, unit, inverse, vec_ref[11:12, :])
                grad_ref[at, :] = grad
                low = grad.astype(bf16)
                low_ref[at, :] = low
                gmix_ref[at, :] = rows_dot_t(low, wo_ref[...]).astype(bf16)
                norm_sums_ref[0:1, :] += row_total(upstream * unit)
                norm_sums_ref[1:2, :] += row_total(upstream)
                norm_sums_ref[2:3, :] += row_total(low.astype(f32))

            each(rows, ROWS, body)
            to_ref[...] = (column_dot(mixo_ref[...], low_ref[...]) * factor).astype(bf16)

    hook()


def attend_backward(
    queries, keys_in, values_in, block_table, causal, mixed, lse, mixed_grad, left_q, upstream, wide_full,
    factor, extra, traffic, table, collective_id,
):
    rows, keys = queries.shape[0], keys_in.shape[0]
    bf16, f32 = jnp.bfloat16, jnp.float32
    first = 0 if causal else 1

    def columns(count):
        return pl.BlockSpec((count, 128), lambda i: (0, i))

    def whole(shape):
        return pl.BlockSpec(shape, lambda i: (0,) * len(shape), pipeline_mode=pl.Buffered(1))

    def weight(unit):
        return pl.BlockSpec((D, 128), lambda i: (0, unit * (D // 128) + i))

    spec_q, spec_k = columns(rows), columns(keys)
    in_specs = [pl.BlockSpec(memory_space=pltpu.SMEM), spec_q, spec_k, spec_k, spec_q, spec_q]
    in_specs += [pl.BlockSpec((1, 8, rows), lambda i: (i, 0, 0)), whole((rows, D)), pl.BlockSpec(memory_space=pl.ANY)]
    in_specs += [weight(first), weight(first + 1), weight(first + 2)]
    operands = [block_table, queries, keys_in, values_in, mixed_grad, mixed, lse, left_q, upstream]
    operands += [wide_full] * 3
    shape = jax.ShapeDtypeStruct
    out_specs = [columns(D)] * 3 + [columns(8), whole((rows, D))]
    out_shape = [shape((D, D), bf16)] * 3 + [shape((8, D), f32), shape((rows, D), bf16 if causal else f32)]
    scratch = [
        pltpu.VMEM((2, rows, 128), bf16),
        pltpu.VMEM((2, rows, 128), bf16),
        pltpu.VMEM((128, rows), bf16),
        pltpu.VMEM((128, rows), bf16),
        pltpu.VMEM((4, rows, 128), f32),
        pltpu.VMEM((rows, 128), f32),
        pltpu.VMEM((128, keys), bf16),
        pltpu.VMEM((128, keys), bf16),
        pltpu.VMEM((rows, D), f32),
        pltpu.SemaphoreType.DMA,
    ]
    if not causal:
        states, resid, mixed_self, vec_rows = extra
        in_specs += [whole((keys, D)), pl.BlockSpec((D, D), lambda i: (0, 0), pipeline_mode=pl.Buffered(1)), whole((rows, D)), whole((rows, D))]
        in_specs += [whole(vec_rows.shape)]
        operands += [states, wide_full, resid, mixed_self, vec_rows]
        out_specs += [whole((keys, D)), whole((rows, D)), whole((D, D)), whole((8, D))]
        out_shape += [shape((keys, D), bf16), shape((rows, D), bf16), shape((D, D), bf16), shape((8, D), f32)]
        scratch += [pltpu.VMEM((keys, D), f32), pltpu.VMEM((rows, D), bf16)]
    params = dict(vmem_limit_bytes=62 << 20)
    if traffic:
        in_specs += traffic.in_specs()
        operands += traffic.operands()
        out_specs += traffic.out_specs()
        out_shape += traffic.out_shape()
        scratch += traffic.scratch()
        params.update(collective_id=collective_id, has_side_effects=True)
    return pl.pallas_call(
        partial(backward_kernel, causal, traffic, table, factor),
        grid=(D // 128,),
        in_specs=in_specs,
        out_specs=out_specs,
        out_shape=out_shape,
        scratch_shapes=scratch,
        compiler_params=pltpu.CompilerParams(**params),
        cost_estimate=pl.CostEstimate(
            flops=(20 if causal else 40) * rows * keys * D, bytes_accessed=4 * queries.size, transcendentals=0
        ),
    )(*operands)


def adam_update(master, first, second, gradient, decay_on, rate):
    first_new = beta_one * first + (1.0 - beta_one) * gradient
    second_new = beta_two * second + (1.0 - beta_two) * gradient * gradient
    first_hat = first_new / (1.0 - beta_one**STEP)
    second_hat = second_new / (1.0 - beta_two**STEP)
    master_new = master - rate * (first_hat / (jnp.sqrt(second_hat) + eps_adam) + decay_on * master)
    return (master_new, first_new, second_new)


def adam_kernel(spans, aliased, table_ref, *refs):
    step = pl.program_id(0)
    count = 1 + max(span[0] for span in spans)
    sums = refs[:count]
    masters = refs[count : count + 6]
    outs = refs[count + 6 + aliased :]

    def update(sum_ref, master, first, second, grad, new, first_new, second_new, copy):
        def body(r, carry):
            at = pl.ds(pl.multiple_of(r * 32, 32), 32)
            gradient = sum_ref[0, at, :].astype(jnp.float32)
            grad[at, :] = gradient
            value, one, two = adam_update(
                master[at, :], first[at, :], second[at, :], gradient, weight_decay, learn_rate
            )
            new[at, :] = value
            first_new[at, :] = one
            second_new[at, :] = two
            copy[at, :] = value.astype(jnp.bfloat16)
            return carry

        lax.fori_loop(0, UNIT // 64, body, 0, unroll=3)

    for which, begin, end, wide in spans:

        @pl.when((step >= begin) & (step < end))
        def _():
            if wide:
                update(sums[which], *masters[:3], *outs[:5])
            else:
                update(sums[which], *masters[3:], *outs[5:])


def adam_halves(parts, x, y, wide, narrow, before):
    spans, starts, wides, wide_halves, narrow_rows = [], [], [], [], []
    step = 0
    for which, (array, names, by_x, own) in enumerate(parts):
        starts.append(step)
        here = x if by_x else y
        entire = array.shape[1] == UNIT
        for k, (kind, index) in enumerate([n for n in names for _ in range(1 + entire)]):
            half = k % 2 if entire else here if own else 1 - here
            is_wide = kind == "wide"
            if spans and spans[-1][0] == which and spans[-1][3] == is_wide:
                spans[-1] = (which, spans[-1][1], step + 1, is_wide)
            else:
                spans.append((which, step, step + 1, is_wide))
            wides.append(index if is_wide else None)
            wide_halves.append(half if is_wide else None)
            narrow_rows.append(None if is_wide else 2 * index + half)
            step += 1

    def filled(values):
        last = next((v for v in values if v is not None), 0)
        found = []
        for v in values:
            last = last if v is None else v
            found.append(jnp.asarray(last, jnp.int32))
        return jnp.stack(found)

    table = jnp.stack([filled(wides), filled(wide_halves), filled(narrow_rows)])
    f32, bf16 = jnp.float32, jnp.bfloat16
    spec_w = pl.BlockSpec((UNIT // 2, D), lambda i, t: (t[1, i], t[0, i]))
    spec_n = pl.BlockSpec((UNIT // 2, D), lambda i, t: (t[2, i], 0))

    def spec_sum(start, array):
        halves = 2 * array.shape[1] // UNIT

        def place(i, t):
            at = jnp.clip(i - start, 0, array.shape[0] * halves - 1)
            return (at // halves, at % halves, 0)

        return pl.BlockSpec((1, UNIT // 2, D), place)

    def shapes(like):
        return [jax.ShapeDtypeStruct(like.shape, f32)] * 4 + [jax.ShapeDtypeStruct(like.shape, bf16)]

    operands = [part[0] for part in parts] + list(wide) + list(narrow)
    in_specs = [spec_sum(start, part[0]) for start, part in zip(starts, parts)]
    in_specs += [spec_w] * 3 + [spec_n] * 3
    aliases = {}
    if before is not None:
        aliases = {1 + len(operands) + i: i for i in range(10)}
        operands += list(before)
        in_specs += [pl.BlockSpec(memory_space=pl.ANY)] * 10
    return pl.pallas_call(
        partial(adam_kernel, tuple(spans), 0 if before is None else 10),
        grid_spec=pltpu.PrefetchScalarGridSpec(
            num_scalar_prefetch=1,
            grid=(step,),
            in_specs=in_specs,
            out_specs=[spec_w] * 5 + [spec_n] * 5,
        ),
        out_shape=shapes(wide[0]) + shapes(narrow[0]),
        input_output_aliases=aliases,
        compiler_params=pltpu.CompilerParams(vmem_limit_bytes=58 << 20),
        cost_estimate=pl.CostEstimate(
            flops=30 * step * UNIT * HALF, bytes_accessed=32 * step * UNIT * HALF, transcendentals=0
        ),
    )(table, *operands)


def matmul(left, right):
    return jnp.dot(left, right, preferred_element_type=jnp.float32)


def matmul_left(left, right):
    return lax.dot_general(
        left, right, (((0,), (0,)), ((), ())), preferred_element_type=jnp.float32
    )


def matmul_right(left, right):
    return lax.dot_general(
        left, right, (((1,), (1,)), ((), ())), preferred_element_type=jnp.float32
    )


def norm_forward(resid, gain, shift):
    average = jnp.mean(resid, axis=-1, keepdims=True)
    centred = resid - average
    inverse = lax.rsqrt(jnp.mean(centred * centred, axis=-1, keepdims=True) + eps_norm)
    normed = centred * inverse
    return normed * gain + shift


def on_device(
    tokens,
    encoder_states,
    cotangent,
    block_mask,
    wide_master,
    narrow_master,
    vec_master,
    wide_first,
    narrow_first,
    vec_first,
    wide_second,
    narrow_second,
    vec_second,
):
    replicas = lax.axis_size("rep")
    shards = lax.axis_size("shard")
    tokens_all = tokens.shape[0] * replicas * shards
    factor = float(tokens_all) ** (-0.5)
    bf16, f32 = jnp.bfloat16, jnp.float32

    def gathered(part):
        return lax.all_gather(part.astype(bf16), "shard", axis=0, tiled=True)

    masters = None
    if shards == 2:
        masters = (wide_master, narrow_master)
        wide_early, vec_full = gather_first(wide_master, vec_master)
    else:
        wide_early, vec_full = gathered(wide_master[:, : 3 * D]), gathered(vec_master)
        wide_late, narrow_full = gathered(wide_master[:, 3 * D :]), gathered(narrow_master)
    vector = vec_full.astype(f32)
    vec_rows = jnp.pad(vector.T, ((0, 24 - vector.shape[1]), (0, 0)))
    found = attend_forward(tokens, tokens, block_mask, wide_early, vec_rows, True, masters)
    mixed_self, totals_self, queries, keys_self, values_self = found[:5]
    if masters is not None:
        wide_late, narrow_full = found[5:]
    resid_one = tokens.astype(f32) + matmul(mixed_self, wide_late[:, :D]) + vector[:, 2]
    normed_one = norm_forward(resid_one, vector[:, 11], vector[:, 14])
    normed_low = normed_one.astype(bf16)
    mixed_cross, totals_cross, cross_queries, cross_keys, cross_values = attend_forward(
        normed_low, encoder_states, block_mask, wide_late, vec_rows, False, None
    )
    output, grad_two, grad_cross_mix, term_in, term_narrow, term_co, sums = center(
        mixed_cross, normed_one, cotangent, wide_late, narrow_full, vec_rows, factor, shards
    )

    def split(term):
        return term.reshape(shards, -1, D)

    lanes = replicas // 4
    carried = shards == 2 and replicas % 4 == 0 and UNIT % (32 * lanes) == 0
    terms = [term_in, split(term_narrow), split(term_co)]
    names = [("wide", 8 + i) for i in range(4)] + [("narrow", i) for i in range(4)] + [("wide", 7)]
    names += [("wide", i) for i in (4, 5, 6, 3, 0, 1, 2)]
    x_first = [i % 2 == 0 for i in range(9)] + [i % 2 == 1 for i in range(4)] + [i % 2 == 1 for i in range(3)]
    spots = [(0, UNIT * i) for i in range(4)] + [(1, UNIT * i) for i in range(4)] + [(2, 0)]
    parts_own, parts_far = [], []

    def item(mode, unit, which=0, row=0):
        return (mode, x_first[unit], which, row)

    def collect(traffic, outs, units):
        blocks, halves, small = traffic.unpack(outs)
        if traffic.entire:
            summed = [names[u] for u, it in zip(units, traffic.items) if it[0] != "scatter"]
            parts_own.append((halves[0], summed, True, True))
            return blocks, small
        for by_x, array in zip((True, False), halves):
            if array is None:
                continue
            mine = [names[u] for u, it in zip(units, traffic.items) if it[0] != "scatter" and it[1] == by_x]
            pairs = [(r, r ^ (1 if by_x else 2)) for r in range(replicas)]
            parts_own.append((array, mine, by_x, True))
            parts_far.append((lax.ppermute(array, "rep", pairs), mine, by_x, False))
        return blocks, small

    traffic = None
    units = list(range(N_BOTH + N_SCATTER))
    if carried:
        items = [item("both" if u < N_BOTH else "scatter", u, *spots[u]) for u in units]
        traffic = Traffic(items, lanes, True, terms)
    found = attend_backward(
        cross_queries, cross_keys, cross_values, block_mask, False, mixed_cross, totals_cross,
        grad_cross_mix, normed_low, grad_two, wide_late, factor,
        (encoder_states, resid_one, mixed_self, vec_rows), traffic, CROSS_TABLE, 1,
    )
    term_cq, term_ck, term_cv, cross_sums, grad_one, enc_grad, grad_self_mix, term_wo, norm_sums = found[:9]
    middle = [split(term) for term in (term_cq, term_ck, term_cv, term_wo)]
    if carried:
        blocks, _ = collect(traffic, found[9:], units)
        units = list(range(N_BOTH, N_BOTH + N_GATHER)) + list(range(9, 9 + N_MIDDLE))
        items = [item("gather", u) for u in units[:N_GATHER]]
        items += [item("scatter", 9 + i, i) for i in range(N_MIDDLE)]
        traffic = Traffic(items, lanes, True, middle[:N_MIDDLE], blocks[:N_GATHER])
    found = attend_backward(
        queries, keys_self, values_self, block_mask, True, mixed_self, totals_self,
        grad_self_mix, tokens, grad_one, wide_early, factor, None, traffic, SELF_TABLE, 2,
    )
    late = [split(term) for term in found[:3]]
    self_sums, in_grad = found[3:5]
    term_vec = jnp.concatenate(
        [
            self_sums[0:2],
            norm_sums[2:3],
            cross_sums[0:2],
            sums[5:11],
            norm_sums[0:1],
            sums[12:14],
            norm_sums[1:2],
            sums[15:],
        ],
        0,
    )
    term_vec = (term_vec * factor).reshape(24, shards, -1).transpose(1, 0, 2)
    wide = (wide_master, wide_first, wide_second)
    narrow = (narrow_master, narrow_first, narrow_second)
    if carried:
        blocks_self, _ = collect(traffic, found[5:], units)
        kept = list(range(N_BOTH + N_GATHER, N_BOTH + N_SCATTER)) + list(range(9, 9 + N_MIDDLE))
        fresh = list(range(N_BOTH + N_SCATTER, 9))
        items = [item("gather", u) for u in kept] + [item("both", u, *spots[u]) for u in fresh]
        others = middle[N_MIDDLE:] + late
        items += [item("both", 9 + N_MIDDLE + i, 3 + i) for i in range(len(others))]
        held = jnp.concatenate([blocks[N_GATHER:], blocks_self], 0)
        traffic = Traffic(items, lanes, False, terms + others, held, term_vec)
        _, vec_sum = collect(
            traffic, run_traffic(traffic, TAIL_ORDER, 0), kept + fresh + list(range(9 + N_MIDDLE, 16))
        )
        rep = lax.axis_index("rep")
        x, y = rep % 2, (rep // 2) % 2
        updated = adam_halves(parts_own, x, y, wide, narrow, None)
        updated = adam_halves(parts_far, x, y, wide, narrow, updated)
    else:
        by_column = late + [middle[3]] + middle[:3] + [terms[2]]
        by_column += [term_in[:, i * (D // shards) : (i + 1) * (D // shards)] for i in range(4)]
        wide_sum = jnp.concatenate([whole_sum(term) for term in by_column], 1).astype(f32)
        narrow_sum = whole_sum(terms[1]).astype(f32)
        vec_sum = lax.psum(lax.psum_scatter(term_vec, "shard", scatter_dimension=0), "rep")
        updated = []
        for gradient, state in ((wide_sum, wide), (narrow_sum, narrow)):
            new, first_new, second_new = adam_update(*state, gradient, weight_decay, learn_rate)
            updated += [gradient, new, first_new, second_new, new.astype(bf16)]
    (
        wide_grad, wide_new, wide_first_new, wide_second_new, wide_copy,
        narrow_grad, narrow_new, narrow_first_new, narrow_second_new, narrow_copy,
    ) = updated
    vec_grad = vec_sum[: vec_master.shape[1]].T
    vec_new, vec_first_new, vec_second_new = adam_update(
        vec_master, vec_first, vec_second, vec_grad, 0.0, vec_rate
    )
    return (
        output,
        in_grad,
        enc_grad,
        wide_grad,
        narrow_grad,
        vec_grad,
        wide_new,
        narrow_new,
        vec_new,
        wide_first_new,
        narrow_first_new,
        vec_first_new,
        wide_second_new,
        narrow_second_new,
        vec_second_new,
        wide_copy,
        narrow_copy,
        vec_new.astype(bf16),
    )


def whole_sum(term):
    return lax.psum(lax.psum_scatter(term, "shard", scatter_dimension=0), "rep")


def solution(mesh):
    in_specs = (
        P(("rep", "shard"), None),
        P(("rep", "shard"), None),
        P(("rep", "shard"), None),
        P(("rep", "shard"), None, None),
        P("shard", None),
        P("shard", None),
        P("shard", None),
        P("shard", None),
        P("shard", None),
        P("shard", None),
        P("shard", None),
        P("shard", None),
        P("shard", None),
    )
    out_specs = (
        P(("rep", "shard"), None),
        P(("rep", "shard"), None),
        P(("rep", "shard"), None),
        P("shard", None),
        P("shard", None),
        P("shard", None),
        P("shard", None),
        P("shard", None),
        P("shard", None),
        P("shard", None),
        P("shard", None),
        P("shard", None),
        P("shard", None),
        P("shard", None),
        P("shard", None),
        P("shard", None),
        P("shard", None),
        P("shard", None),
    )
    return jax.shard_map(
        on_device, mesh=mesh, in_specs=in_specs, out_specs=out_specs, check_vma=False
    )
```
